32 devices in a mesh: replica: 16 (over z, y, core), shard: 2 (over x).
Axes of the slice: x: 2, y: 2, z: 4, core: 2. Of those that a mesh axis runs over, the one named last changes fastest.
Arguments:
- tokens: bfloat16 [16384, 1024], P(('replica', 'shard')), may hold values from -6 to 6
- positions: int32 [16384], P(('replica', 'shard')), may hold values from 0 to 1534, as said below
- cotangent: bfloat16 [16384, 1024], P(('replica', 'shard')), may hold values from -6 to 6
- norm1_gain: bfloat16 [1024], P('shard'), may hold values from 0.099609375 to 1.8984375
- w_query: bfloat16 [1024, 2048], P('shard'), may hold values from -0.1875 to 0.1875
- w_key: bfloat16 [1024, 1024], P('shard'), may hold values from -0.1875 to 0.1875
- w_value: bfloat16 [1024, 1024], P('shard'), may hold values from -0.1875 to 0.1875
- w_out: bfloat16 [2048, 1024], P('shard'), may hold values from -1 to 1
- query_gain: bfloat16 [128], P('shard'), may hold values from 0.099609375 to 1.8984375
- key_gain: bfloat16 [128], P('shard'), may hold values from 0.099609375 to 1.8984375
- norm2_gain: bfloat16 [1024], P('shard'), may hold values from 0.099609375 to 1.8984375
- w_gate: bfloat16 [1024, 3072], P('shard'), may hold values from -0.1875 to 0.1875
- w_up: bfloat16 [1024, 3072], P('shard'), may hold values from -0.1875 to 0.1875
- w_down: bfloat16 [3072, 1024], P('shard'), may hold values from -0.109375 to 0.109375
Outputs:
- result: bfloat16 [16384, 1024], P(('replica', 'shard'))
- grad_input: float32 [16384, 1024], P(('replica', 'shard'))
- grad_norm1_gain: float32 [1024], P('shard')
- grad_w_query: float32 [1024, 2048], P('shard')
- grad_w_key: float32 [1024, 1024], P('shard')
- grad_w_value: float32 [1024, 1024], P('shard')
- grad_w_out: float32 [2048, 1024], P('shard')
- grad_query_gain: float32 [128], P('shard')
- grad_key_gain: float32 [128], P('shard')
- grad_norm2_gain: float32 [1024], P('shard')
- grad_w_gate: float32 [1024, 3072], P('shard')
- grad_w_up: float32 [1024, 3072], P('shard')
- grad_w_down: float32 [3072, 1024], P('shard')
The draws below stay inside these ranges and needn't reach their ends.
Inputs may be any that keep to these rules, and one draw needn't show every extreme that they name: Within each sequence of 1024 tokens positions start at 0 and rise by 1 or 2 from each token to the next, by 2 exactly (1023) // 2 times.
All inputs are finite; a program needn't handle non-finite values.
Results may differ from the reference program's by a relative error of at most 0.023.
Values may be sent and summed in bfloat16 or wider, within the bound.
No kernel may reach another device: no remote copies, remote signals or barrier semaphores. Data moves between devices by JAX's collectives and lax.ppermute only.
A program may use at most 448 MiB of HBM per device.

```python
import math
import jax
import jax.numpy as jnp
from jax import lax

D = 1024
FF = 3072
Q_HEADS = 16
KV_HEADS = 8
HEAD_DIM = 128
LENGTH = 1024
TOKENS = 16384


def draw_positions(key, part):
    key = jax.random.fold_in(key, 11)
    seq_count = TOKENS // LENGTH
    keys = jax.random.split(key, seq_count)
    orders = jax.vmap(lambda one_key: jax.random.permutation(one_key, LENGTH - 1))(keys)
    strides = 1 + (orders < (LENGTH - 1) // 2).astype(jnp.int32)
    places = jnp.concatenate([jnp.zeros((seq_count, 1), jnp.int32), jnp.cumsum(strides, axis=1).astype(jnp.int32)], axis=1)
    return places.reshape(TOKENS).astype(jnp.int32)


def level_of(key, extent, shards, least, top_value):
    level, own = 1.0, jax.random.fold_in(key, 6)
    for axis_at, parts in shards:
        draws = jnp.exp(jax.random.uniform(jax.random.fold_in(own, axis_at), (parts,), jnp.float32, least / len(shards), top_value / len(shards)))
        level = level * jnp.repeat(draws, extent[axis_at] // parts).reshape([-1 if axis == axis_at else 1 for axis in range(len(extent))])
    return level


def bell_draw(key, extent, scale, most, cuts=(), held_as=jnp.bfloat16):
    entries = scale * jax.random.normal(key, extent, jnp.float32)
    if cuts:
        entries = entries * level_of(key, extent, cuts, -0.22, 0.18)
    return jnp.clip(entries, -most, most).astype(held_as)


def setup_inputs(seed: int = 0) -> dict:
    key_list = jax.random.split(jax.random.key(seed), 15)
    tokens = bell_draw(key_list[0], (TOKENS, D), 1.0, 6.0, ((0, 32),))
    positions = draw_positions(jax.random.fold_in(key_list[14], 71), 0)
    cotangent = bell_draw(key_list[2], (TOKENS, D), 1.0, 6.0, ((0, 32),))
    norm1_gain = jnp.clip(1.0 + 0.18 * jax.random.normal(key_list[3], (D,), jnp.float32), 0.099609375, 1.8984375).astype(jnp.bfloat16)
    w_query = bell_draw(key_list[4], (D, Q_HEADS * HEAD_DIM), D ** -0.5, 0.1875, ((0, 2),))
    w_key = bell_draw(key_list[5], (D, KV_HEADS * HEAD_DIM), D ** -0.5, 0.1875, ((0, 2),))
    w_value = bell_draw(key_list[6], (D, KV_HEADS * HEAD_DIM), D ** -0.5, 0.1875, ((0, 2),))
    w_out = bell_draw(key_list[7], (Q_HEADS * HEAD_DIM, D), (Q_HEADS * HEAD_DIM * 16 // LENGTH) ** -0.5, 1.0, ((0, 2),))
    query_gain = jnp.clip(1.0 + 0.18 * jax.random.normal(key_list[8], (HEAD_DIM,), jnp.float32), 0.099609375, 1.8984375).astype(jnp.bfloat16)
    key_gain = jnp.clip(1.0 + 0.18 * jax.random.normal(key_list[9], (HEAD_DIM,), jnp.float32), 0.099609375, 1.8984375).astype(jnp.bfloat16)
    norm2_gain = jnp.clip(1.0 + 0.18 * jax.random.normal(key_list[10], (D,), jnp.float32), 0.099609375, 1.8984375).astype(jnp.bfloat16)
    w_gate = bell_draw(key_list[11], (D, FF), D ** -0.5, 0.1875, ((0, 2),))
    w_up = bell_draw(key_list[12], (D, FF), D ** -0.5, 0.1875, ((0, 2),))
    w_down = bell_draw(key_list[13], (FF, D), FF ** -0.5, 0.109375, ((0, 2),))
    return dict(tokens=tokens, positions=positions, cotangent=cotangent, norm1_gain=norm1_gain, w_query=w_query, w_key=w_key, w_value=w_value, w_out=w_out, query_gain=query_gain, key_gain=key_gain, norm2_gain=norm2_gain, w_gate=w_gate, w_up=w_up, w_down=w_down)


EPS = 1e-06
THETA = 1000000.0
NEG = -1e+30
HIGH = lax.Precision.HIGHEST

@jax.custom_vjp
def low(v):
    return lax.optimization_barrier(v.astype(jnp.bfloat16)).astype(jnp.float32)

@jax.custom_vjp
def low_back(v):
    return v

def low_keep(v):
    return (low(v), None)

def low_pass(kept, grad):
    return (grad,)

def back_keep(v):
    return (v, None)

def back_low(kept, grad):
    return (low(grad),)
low.defvjp(low_keep, low_pass)
low_back.defvjp(back_keep, back_low)

def rms_scale(values):
    return lax.rsqrt(lax.optimization_barrier(jnp.mean(values * values, axis=-1, keepdims=True)) + EPS)

def rotation_tables(places, width):
    half_width = width // 2
    freqs = THETA ** (-jnp.arange(half_width, dtype=jnp.float32) * 2.0 / width)
    angles = places.astype(jnp.float32)[:, None, None] * freqs
    return (jnp.cos(angles), jnp.sin(angles))

def rotate(values, cosine, sine_table):
    half_width = values.shape[-1] // 2
    first_half, second_half = (values[..., :half_width], values[..., half_width:])
    return jnp.concatenate([first_half * cosine - second_half * sine_table, second_half * cosine + first_half * sine_table], axis=-1)

def layer(x_float, gain_one, w_query, w_key, w_value, w_out, query_gain, key_gain, gain_two, w_gate, w_up, w_down, cosine, sine_table):
    span = x_float.shape[0]
    group = Q_HEADS // KV_HEADS
    inv_scale = 1.0 / math.sqrt(HEAD_DIM)
    h_one = low(x_float * rms_scale(x_float) * gain_one)
    q_proj = low_back(jnp.dot(h_one, w_query, precision=HIGH)).reshape(span, Q_HEADS, HEAD_DIM)
    k_proj = low_back(jnp.dot(h_one, w_key, precision=HIGH)).reshape(span, KV_HEADS, HEAD_DIM)
    v_proj = low(low_back(jnp.dot(h_one, w_value, precision=HIGH))).reshape(span, KV_HEADS, HEAD_DIM)
    q_use = low(rotate(q_proj * rms_scale(q_proj) * query_gain, cosine, sine_table) * inv_scale)
    q_use = q_use.reshape(span, KV_HEADS, group, HEAD_DIM)
    k_use = low(rotate(k_proj * rms_scale(k_proj) * key_gain, cosine, sine_table))
    scores = low_back(jnp.einsum('sngd,tnd->ngst', q_use, k_use, precision=HIGH))
    place = jnp.arange(span)
    allowed = place[None, :] <= place[:, None]
    masked = jnp.where(allowed, scores, NEG)
    peak = lax.optimization_barrier(jnp.max(masked, axis=-1, keepdims=True))
    expo = jnp.exp(masked - peak)
    probs = low(expo / lax.optimization_barrier(jnp.sum(expo, axis=-1, keepdims=True)))
    attended = jnp.einsum('ngst,tnd->sngd', probs, v_proj, precision=HIGH).reshape(span, Q_HEADS * HEAD_DIM)
    out_low = low(low_back(attended))
    resid_one = x_float + low_back(jnp.dot(out_low, w_out, precision=HIGH))
    h_two = low(resid_one * rms_scale(resid_one) * gain_two)
    gate = low_back(jnp.dot(h_two, w_gate, precision=HIGH))
    up_val = low_back(jnp.dot(h_two, w_up, precision=HIGH))
    hidden = low(jax.nn.silu(gate) * up_val)
    return resid_one + low_back(jnp.dot(hidden, w_down, precision=HIGH))

def reference(tokens, positions, cotangent, norm1_gain, w_query, w_key, w_value, w_out, query_gain, key_gain, norm2_gain, w_gate, w_up, w_down):
    params = tuple((item.astype(jnp.float32) for item in (norm1_gain, w_query, w_key, w_value, w_out, query_gain, key_gain, norm2_gain, w_gate, w_up, w_down)))
    seq_count = tokens.shape[0] // LENGTH
    token_seqs = tokens.astype(jnp.float32).reshape(seq_count, LENGTH, D)
    place_seqs = positions.reshape(seq_count, LENGTH)
    cot_seqs = cotangent.astype(jnp.float32).reshape(seq_count, LENGTH, D)

    def one_sequence(totals, inputs):
        x_seq, place_seq, cot_seq = inputs
        cosine, sine_table = rotation_tables(place_seq, HEAD_DIM)

        def forward(x_float, *weights):
            return layer(x_float, *weights, cosine, sine_table)
        output, pullback = jax.vjp(forward, x_seq, *params)
        grads = pullback(cot_seq)
        totals = jax.tree.map(lambda left, right: left + right, totals, tuple(grads[1:]))
        return (totals, (output.astype(jnp.bfloat16), grads[0]))
    start = tuple((jnp.zeros_like(item) for item in params))
    totals, (outputs, input_grads) = lax.scan(one_sequence, start, (token_seqs, place_seqs, cot_seqs))
    return (outputs.reshape(tokens.shape[0], D), input_grads.reshape(tokens.shape[0], D), totals[0], totals[1], totals[2], totals[3], totals[4], totals[5], totals[6], totals[7], totals[8], totals[9], totals[10])
```

```python
from functools import partial
import math

import jax
import jax.numpy as jnp
from jax import lax
from jax.experimental import pallas as pl
from jax.experimental.pallas import tpu as pltpu
from jax.sharding import Mesh, PartitionSpec as P

EPS = 1e-06
THETA = 1000000.0
NEG = -1e30
QUERY_BLOCK = 256
VMEM_BYTES = 56 * 1024 * 1024


def rms_scale(values):
    return lax.rsqrt(jnp.mean(values * values, axis=-1, keepdims=True) + EPS)


def norm_back(values, gain, incoming):
    scale = rms_scale(values)
    normed = values * scale
    scaled_in = incoming * gain
    return (
        scale * (scaled_in - normed * jnp.mean(scaled_in * normed, axis=-1, keepdims=True)),
        incoming * normed,
    )


def rotation_tables(places, width):
    half_width = width // 2
    freqs = THETA ** (-jnp.arange(half_width, dtype=jnp.float32) * 2.0 / width)
    angles = places.astype(jnp.float32)[:, None, None] * freqs
    return (jnp.cos(angles), jnp.sin(angles))


def rotate(values, cosine, sine_table):
    half_width = values.shape[-1] // 2
    first_half, second_half = (values[..., :half_width], values[..., half_width:])
    return jnp.concatenate(
        [
            first_half * cosine - second_half * sine_table,
            second_half * cosine + first_half * sine_table,
        ],
        axis=-1,
    )


def unrotate(grads, cosine, sine_table):
    half_width = grads.shape[-1] // 2
    first_half, second_half = (grads[..., :half_width], grads[..., half_width:])
    return jnp.concatenate(
        [
            first_half * cosine + second_half * sine_table,
            second_half * cosine - first_half * sine_table,
        ],
        axis=-1,
    )


def inner_rows(left, right):
    return lax.dot_general(
        left, right, (((0,), (0,)), ((), ())), preferred_element_type=jnp.float32
    )


def times_t(left, right):
    return lax.dot_general(
        left, right, (((1,), (1,)), ((), ())), preferred_element_type=jnp.float32
    )


def local(
    tokens,
    positions,
    cotangent,
    norm1_gain,
    w_query,
    w_key,
    w_value,
    w_out,
    query_gain,
    key_gain,
    norm2_gain,
    w_gate,
    w_up,
    w_down,
):
    row_count = tokens.shape[0]
    blocks = lax.axis_size("shard")
    own_index = lax.axis_index("shard")
    head_dim = query_gain.shape[0] * blocks
    attn_set = (
        lax.all_gather(norm1_gain, "shard", axis=0, tiled=True),
        lax.all_gather(w_query, "shard", axis=0, tiled=True),
        lax.all_gather(w_key, "shard", axis=0, tiled=True),
        lax.all_gather(w_value, "shard", axis=0, tiled=True),
        lax.all_gather(w_out, "shard", axis=0, tiled=True),
        lax.all_gather(query_gain, "shard", axis=0, tiled=True),
        lax.all_gather(key_gain, "shard", axis=0, tiled=True),
    )
    gain_one = attn_set[0].astype(jnp.float32)
    q_gain = attn_set[5].astype(jnp.float32)
    k_gain = attn_set[6].astype(jnp.float32)
    q_heads = attn_set[1].shape[1] // head_dim
    kv_heads = attn_set[2].shape[1] // head_dim
    group = q_heads // kv_heads
    inv_scale = 1.0 / math.sqrt(head_dim)
    cosine, sine_table = rotation_tables(positions, head_dim)
    x_float = tokens.astype(jnp.float32)
    h_one = (x_float * rms_scale(x_float) * gain_one).astype(jnp.bfloat16)
    q_proj = jnp.dot(h_one, attn_set[1], preferred_element_type=jnp.float32).reshape(
        row_count, q_heads, head_dim
    )
    k_proj = jnp.dot(h_one, attn_set[2], preferred_element_type=jnp.float32).reshape(
        row_count, kv_heads, head_dim
    )
    v_low = jnp.dot(h_one, attn_set[3], preferred_element_type=jnp.float32).astype(jnp.bfloat16)
    q_low = (rotate(q_proj * rms_scale(q_proj) * q_gain, cosine, sine_table) * inv_scale).astype(
        jnp.bfloat16
    )
    q_low = q_low.reshape(row_count, kv_heads, group, head_dim)
    k_low = rotate(k_proj * rms_scale(k_proj) * k_gain, cosine, sine_table).astype(jnp.bfloat16)
    k_low = k_low.reshape(row_count, kv_heads * head_dim)
    key_full, value_full = (
        lax.all_gather(k_low, "shard", axis=0, tiled=True),
        lax.all_gather(v_low, "shard", axis=0, tiled=True),
    )
    query_place = own_index * row_count + jnp.arange(row_count)

    def block_of(full, kblock):
        return full[kblock * row_count : (kblock + 1) * row_count].reshape(
            row_count, kv_heads, head_dim
        )

    def block_scores(keys_all, kblock):
        raw = jnp.einsum(
            "sngd,tnd->ngst", q_low, block_of(keys_all, kblock), preferred_element_type=jnp.float32
        )
        key_place = kblock * row_count + jnp.arange(row_count)
        return jnp.where(key_place[None, :] <= query_place[:, None], raw, NEG)

    empty_scores = jnp.full((kv_heads, group, row_count, row_count), NEG, jnp.float32)
    zero_scores = jnp.zeros((kv_heads, group, row_count, row_count), jnp.float32)
    zero_out = jnp.zeros((row_count, kv_heads, group, head_dim), jnp.float32)
    zero_keys = jnp.zeros((row_count, kv_heads, head_dim), jnp.float32)
    score_list = [
        lax.cond(kblock <= own_index, partial(block_scores, key_full, kblock), lambda: empty_scores)
        for kblock in range(blocks)
    ]
    score_all = jnp.concatenate(score_list, axis=-1)
    peak = jnp.max(score_all, axis=-1, keepdims=True)
    log_total = peak + jnp.log(jnp.sum(jnp.exp(score_all - peak), axis=-1, keepdims=True))
    probs_low = jnp.exp(score_all - log_total).astype(jnp.bfloat16)

    def block_output(kblock):
        part_probs = probs_low[..., kblock * row_count : (kblock + 1) * row_count]
        return jnp.einsum(
            "ngst,tnd->sngd",
            part_probs,
            block_of(value_full, kblock),
            preferred_element_type=jnp.float32,
        )

    attended = zero_out
    for kblock in range(blocks):
        attended = attended + lax.cond(
            kblock <= own_index, partial(block_output, kblock), lambda: zero_out
        )
    out_low = attended.reshape(row_count, q_heads * head_dim).astype(jnp.bfloat16)
    resid_one = x_float + jnp.dot(out_low, attn_set[4], preferred_element_type=jnp.float32)
    mlp_set = (
        lax.all_gather(norm2_gain, "shard", axis=0, tiled=True),
        lax.all_gather(w_gate, "shard", axis=0, tiled=True),
        lax.all_gather(w_up, "shard", axis=0, tiled=True),
        lax.all_gather(w_down, "shard", axis=0, tiled=True),
    )
    gain_two = mlp_set[0].astype(jnp.float32)
    h_two = (resid_one * rms_scale(resid_one) * gain_two).astype(jnp.bfloat16)
    gate = jnp.dot(h_two, mlp_set[1], preferred_element_type=jnp.float32)
    up_val = jnp.dot(h_two, mlp_set[2], preferred_element_type=jnp.float32)
    sigmoid_gate = jax.nn.sigmoid(gate)
    hidden_low = (gate * sigmoid_gate * up_val).astype(jnp.bfloat16)
    result = (
        resid_one + jnp.dot(hidden_low, mlp_set[3], preferred_element_type=jnp.float32)
    ).astype(jnp.bfloat16)
    mlp_back = (
        lax.all_gather(norm2_gain, "shard", axis=0, tiled=True),
        lax.all_gather(w_gate, "shard", axis=0, tiled=True),
        lax.all_gather(w_up, "shard", axis=0, tiled=True),
        lax.all_gather(w_down, "shard", axis=0, tiled=True),
    )
    grad_hidden = times_t(cotangent, mlp_back[3])
    grad_gate_low = (
        grad_hidden * up_val * sigmoid_gate * (1.0 + gate * (1.0 - sigmoid_gate))
    ).astype(jnp.bfloat16)
    grad_up_low = (grad_hidden * gate * sigmoid_gate).astype(jnp.bfloat16)
    grad_h_two = times_t(grad_gate_low, mlp_back[1]) + times_t(grad_up_low, mlp_back[2])
    resid_part, gain_two_terms = norm_back(resid_one, gain_two, grad_h_two)
    grad_resid = cotangent.astype(jnp.float32) + resid_part
    grad_down = inner_rows(hidden_low, cotangent)
    grad_gate_w = inner_rows(h_two, grad_gate_low)
    grad_up_w = inner_rows(h_two, grad_up_low)
    mlp_shares = (
        lax.psum_scatter(
            jnp.sum(gain_two_terms, axis=0).astype(jnp.bfloat16),
            "shard",
            scatter_dimension=0,
            tiled=True,
        ).astype(jnp.float32),
        lax.psum_scatter(
            grad_gate_w.astype(jnp.bfloat16), "shard", scatter_dimension=0, tiled=True
        ).astype(jnp.float32),
        lax.psum_scatter(
            grad_up_w.astype(jnp.bfloat16), "shard", scatter_dimension=0, tiled=True
        ).astype(jnp.float32),
        lax.psum_scatter(
            grad_down.astype(jnp.bfloat16), "shard", scatter_dimension=0, tiled=True
        ).astype(jnp.float32),
    )
    attn_back = (
        lax.all_gather(norm1_gain, "shard", axis=0, tiled=True),
        lax.all_gather(w_query, "shard", axis=0, tiled=True),
        lax.all_gather(w_key, "shard", axis=0, tiled=True),
        lax.all_gather(w_value, "shard", axis=0, tiled=True),
        lax.all_gather(w_out, "shard", axis=0, tiled=True),
        lax.all_gather(query_gain, "shard", axis=0, tiled=True),
        lax.all_gather(key_gain, "shard", axis=0, tiled=True),
    )
    resid_low = grad_resid.astype(jnp.bfloat16)
    grad_att_low = (
        times_t(resid_low, attn_back[4])
        .astype(jnp.bfloat16)
        .reshape(row_count, kv_heads, group, head_dim)
    )
    key_back, value_back = (key_full, value_full)

    def first_pass(kblock):
        part_probs = jnp.exp(block_scores(key_back, kblock) - log_total)
        part_dprobs = jnp.einsum(
            "sngd,tnd->ngst",
            grad_att_low,
            block_of(value_back, kblock),
            preferred_element_type=jnp.float32,
        )
        return (part_probs, part_dprobs)

    pass_list = [
        lax.cond(
            kblock <= own_index, partial(first_pass, kblock), lambda: (zero_scores, zero_scores)
        )
        for kblock in range(blocks)
    ]
    delta_sum = jnp.zeros((kv_heads, group, row_count, 1), jnp.float32)
    for part_probs, part_dprobs in pass_list:
        delta_sum = delta_sum + jnp.sum(part_probs * part_dprobs, axis=-1, keepdims=True)

    def second_pass(kblock):
        part_probs, part_dprobs = pass_list[kblock]
        dscore_low = (part_probs * (part_dprobs - delta_sum)).astype(jnp.bfloat16)
        query_term = jnp.einsum(
            "ngst,tnd->sngd",
            dscore_low,
            block_of(key_back, kblock),
            preferred_element_type=jnp.float32,
        )
        key_term = jnp.einsum(
            "ngst,sngd->tnd", dscore_low, q_low, preferred_element_type=jnp.float32
        )
        value_term = jnp.einsum(
            "ngst,sngd->tnd",
            part_probs.astype(jnp.bfloat16),
            grad_att_low,
            preferred_element_type=jnp.float32,
        )
        return (query_term, key_term, value_term)

    grad_query = zero_out
    key_terms = []
    value_terms = []
    for kblock in range(blocks):
        query_term, key_term, value_term = lax.cond(
            kblock <= own_index,
            partial(second_pass, kblock),
            lambda: (zero_out, zero_keys, zero_keys),
        )
        grad_query = grad_query + query_term
        key_terms.append(key_term.reshape(row_count, kv_heads * head_dim))
        value_terms.append(value_term.reshape(row_count, kv_heads * head_dim))
    grad_key_local, grad_value_local = (
        lax.psum_scatter(
            jnp.concatenate(key_terms, axis=0).astype(jnp.bfloat16),
            "shard",
            scatter_dimension=0,
            tiled=True,
        ).astype(jnp.float32),
        lax.psum_scatter(
            jnp.concatenate(value_terms, axis=0).astype(jnp.bfloat16),
            "shard",
            scatter_dimension=0,
            tiled=True,
        ).astype(jnp.float32),
    )
    grad_value_low = grad_value_local.astype(jnp.bfloat16)
    key_rot = unrotate(grad_key_local.reshape(row_count, kv_heads, head_dim), cosine, sine_table)
    key_proj_grad, key_gain_terms = norm_back(k_proj, k_gain, key_rot)
    grad_key_low = key_proj_grad.reshape(row_count, kv_heads * head_dim).astype(jnp.bfloat16)
    query_rot = unrotate(
        grad_query.reshape(row_count, q_heads, head_dim) * inv_scale, cosine, sine_table
    )
    query_proj_grad, query_gain_terms = norm_back(q_proj, q_gain, query_rot)
    grad_query_low = query_proj_grad.reshape(row_count, q_heads * head_dim).astype(jnp.bfloat16)
    grad_h_one = (
        times_t(grad_query_low, attn_back[1])
        + times_t(grad_key_low, attn_back[2])
        + times_t(grad_value_low, attn_back[3])
    )
    input_part, gain_one_terms = norm_back(x_float, gain_one, grad_h_one)
    grad_input = grad_resid + input_part
    gain_one_sum = jnp.sum(gain_one_terms, axis=0)
    query_gain_sum = jnp.sum(query_gain_terms, axis=(0, 1))
    key_gain_sum = jnp.sum(key_gain_terms, axis=(0, 1))
    grad_out_w = inner_rows(out_low, resid_low)
    grad_query_w = inner_rows(h_one, grad_query_low)
    grad_key_w = inner_rows(h_one, grad_key_low)
    grad_value_w = inner_rows(h_one, grad_value_low)
    attn_shares = (
        lax.psum_scatter(
            gain_one_sum.astype(jnp.bfloat16), "shard", scatter_dimension=0, tiled=True
        ).astype(jnp.float32),
        lax.psum_scatter(
            grad_query_w.astype(jnp.bfloat16), "shard", scatter_dimension=0, tiled=True
        ).astype(jnp.float32),
        lax.psum_scatter(
            grad_key_w.astype(jnp.bfloat16), "shard", scatter_dimension=0, tiled=True
        ).astype(jnp.float32),
        lax.psum_scatter(
            grad_value_w.astype(jnp.bfloat16), "shard", scatter_dimension=0, tiled=True
        ).astype(jnp.float32),
        lax.psum_scatter(
            grad_out_w.astype(jnp.bfloat16), "shard", scatter_dimension=0, tiled=True
        ).astype(jnp.float32),
        lax.psum_scatter(
            query_gain_sum.astype(jnp.bfloat16), "shard", scatter_dimension=0, tiled=True
        ).astype(jnp.float32),
        lax.psum_scatter(
            key_gain_sum.astype(jnp.bfloat16), "shard", scatter_dimension=0, tiled=True
        ).astype(jnp.float32),
    )
    totals = (
        lax.psum(attn_shares[0].astype(jnp.bfloat16), "replica").astype(jnp.float32),
        lax.psum(attn_shares[1].astype(jnp.bfloat16), "replica").astype(jnp.float32),
        lax.psum(attn_shares[2].astype(jnp.bfloat16), "replica").astype(jnp.float32),
        lax.psum(attn_shares[3].astype(jnp.bfloat16), "replica").astype(jnp.float32),
        lax.psum(attn_shares[4].astype(jnp.bfloat16), "replica").astype(jnp.float32),
        lax.psum(attn_shares[5].astype(jnp.bfloat16), "replica").astype(jnp.float32),
        lax.psum(attn_shares[6].astype(jnp.bfloat16), "replica").astype(jnp.float32),
        lax.psum(mlp_shares[0].astype(jnp.bfloat16), "replica").astype(jnp.float32),
        lax.psum(mlp_shares[1].astype(jnp.bfloat16), "replica").astype(jnp.float32),
        lax.psum(mlp_shares[2].astype(jnp.bfloat16), "replica").astype(jnp.float32),
        lax.psum(mlp_shares[3].astype(jnp.bfloat16), "replica").astype(jnp.float32),
    )
    return (
        result,
        grad_input,
        totals[0],
        totals[1],
        totals[2],
        totals[3],
        totals[4],
        totals[5],
        totals[6],
        totals[7],
        totals[8],
        totals[9],
        totals[10],
    )


def head_norm(values, gain):
    scale = lax.rsqrt(jnp.mean(values * values, axis=-1, keepdims=True) + EPS)
    return values * scale * gain


def attend_kernel(
    qp_ref, kp_ref, v_ref, cos_ref, sin_ref, qg_ref, kg_ref, o_ref, q_ref, k_ref, lse_ref
):
    span, head_dim = kp_ref.shape
    group = qp_ref.shape[1] // head_dim
    block = min(QUERY_BLOCK, span)
    cosine, sine = cos_ref[...], sin_ref[...]
    keyed = head_norm(kp_ref[...], kg_ref[...])
    key_low = (keyed * cosine + pltpu.roll(keyed, head_dim // 2, 1) * sine).astype(jnp.bfloat16)
    k_ref[...] = key_low
    value_t = v_ref[...].T
    ahead = lax.broadcasted_iota(jnp.int32, (block, block), 0) > lax.broadcasted_iota(
        jnp.int32, (block, block), 1
    )
    for head in range(group):
        lanes = slice(head * head_dim, (head + 1) * head_dim)
        asked = head_norm(qp_ref[:, lanes], qg_ref[...])
        asked = asked * cosine + pltpu.roll(asked, head_dim // 2, 1) * sine
        query_low = (asked * (1.0 / math.sqrt(head_dim))).astype(jnp.bfloat16)
        q_ref[:, lanes] = query_low
        for start in range(0, span, block):
            stop = start + block
            scores = times_t(key_low[:stop], query_low[start:stop])
            last = jnp.where(ahead, NEG, scores[start:])
            scores = last if start == 0 else jnp.concatenate([scores[:start], last], axis=0)
            peak = jnp.max(scores, axis=0, keepdims=True)
            powers = jnp.exp(scores - peak)
            total = jnp.sum(powers, axis=0, keepdims=True)
            lse_ref[0, head : head + 1, start:stop] = peak + jnp.log(total)
            probs = (powers * (1.0 / total)).astype(jnp.bfloat16)
            out_t = jnp.dot(value_t[:, :stop], probs, preferred_element_type=jnp.float32)
            o_ref[start:stop, lanes] = out_t.T.astype(jnp.bfloat16)


def attend_back_kernel(
    q_ref,
    k_ref,
    v_ref,
    do_ref,
    lse_ref,
    qp_ref,
    kp_ref,
    cos_ref,
    sin_ref,
    qg_ref,
    kg_ref,
    dq_ref,
    dk_ref,
    dv_ref,
    gain_ref,
    key_acc,
    value_acc,
):
    span, head_dim = kp_ref.shape
    group = qp_ref.shape[1] // head_dim
    block = min(QUERY_BLOCK, span)
    inv_scale = 1.0 / math.sqrt(head_dim)
    key_low, value_low = k_ref[...], v_ref[...]
    key_t = key_low.T
    ahead = lax.broadcasted_iota(jnp.int32, (block, block), 0) > lax.broadcasted_iota(
        jnp.int32, (block, block), 1
    )

    def proj_back(grads, proj, cosine, sine, gain):
        turned = grads * cosine - pltpu.roll(grads, head_dim // 2, 1) * sine
        scale = lax.rsqrt(jnp.mean(proj * proj, axis=-1, keepdims=True) + EPS)
        normed = proj * scale
        scaled = turned * gain
        back = scale * (scaled - normed * jnp.mean(scaled * normed, axis=-1, keepdims=True))
        return back, jnp.sum(turned * normed, axis=0, keepdims=True)

    key_acc[...] = jnp.zeros_like(key_acc)
    value_acc[...] = jnp.zeros_like(value_acc)
    query_gain = jnp.zeros((1, head_dim), jnp.float32)
    for head in range(group):
        lanes = slice(head * head_dim, (head + 1) * head_dim)
        for start in range(0, span, block):
            stop = start + block
            rows = slice(start, stop)
            query_low, grad_out = q_ref[rows, lanes], do_ref[rows, lanes]
            scores = times_t(key_low[:stop], query_low)
            last = jnp.where(ahead, NEG, scores[start:])
            scores = last if start == 0 else jnp.concatenate([scores[:start], last], axis=0)
            probs = jnp.exp(scores - lse_ref[0, head : head + 1, rows])
            dprobs = times_t(value_low[:stop], grad_out)
            delta = jnp.sum(probs * dprobs, axis=0, keepdims=True)
            dscore = (probs * (dprobs - delta)).astype(jnp.bfloat16)
            value_acc[:stop, :] += jnp.dot(
                probs.astype(jnp.bfloat16), grad_out, preferred_element_type=jnp.float32
            )
            key_acc[:stop, :] += jnp.dot(dscore, query_low, preferred_element_type=jnp.float32)
            grad_query = jnp.dot(key_t[:, :stop], dscore, preferred_element_type=jnp.float32).T
            back, gain_term = proj_back(
                grad_query * inv_scale,
                qp_ref[rows, lanes],
                cos_ref[rows, :],
                sin_ref[rows, :],
                qg_ref[...],
            )
            dq_ref[rows, lanes] = back.astype(jnp.bfloat16)
            query_gain = query_gain + gain_term
    back, key_gain = proj_back(key_acc[...], kp_ref[...], cos_ref[...], sin_ref[...], kg_ref[...])
    dk_ref[...] = back.astype(jnp.bfloat16)
    dv_ref[...] = value_acc[...].astype(jnp.bfloat16)
    gain_ref[0] = jnp.concatenate(
        [query_gain, key_gain, jnp.zeros((gain_ref.shape[1] - 2, head_dim), jnp.float32)], axis=0
    )


def attend(q_proj, k_proj, value_low, cosine, sine, q_gain, k_gain):
    span, q_width = q_proj.shape
    kv_width = k_proj.shape[1]
    head_dim = q_gain.shape[1]
    heads, group = kv_width // head_dim, q_width // kv_width
    q_spec = pl.BlockSpec((span, group * head_dim), lambda head: (0, head))
    k_spec = pl.BlockSpec((span, head_dim), lambda head: (0, head))
    table = pl.BlockSpec((span, head_dim), lambda head: (0, 0))
    gain = pl.BlockSpec((1, head_dim), lambda head: (0, 0))
    return pl.pallas_call(
        attend_kernel,
        grid=(heads,),
        in_specs=[q_spec, k_spec, k_spec, table, table, gain, gain],
        out_specs=[q_spec, q_spec, k_spec, pl.BlockSpec((1, group, span), lambda h: (h, 0, 0))],
        out_shape=[
            jax.ShapeDtypeStruct((span, q_width), jnp.bfloat16),
            jax.ShapeDtypeStruct((span, q_width), jnp.bfloat16),
            jax.ShapeDtypeStruct((span, kv_width), jnp.bfloat16),
            jax.ShapeDtypeStruct((heads, group, span), jnp.float32),
        ],
        compiler_params=pltpu.CompilerParams(vmem_limit_bytes=VMEM_BYTES),
        cost_estimate=pl.CostEstimate(
            flops=2 * span * span * q_width * 2,
            bytes_accessed=span * (q_width * 8 + kv_width * 8),
            transcendentals=span * span * heads * group // 2,
        ),
        name="attend",
    )(q_proj, k_proj, value_low, cosine, sine, q_gain, k_gain)


def attend_back(
    query_low, key_low, value_low, grad_out, lse, q_proj, k_proj, cosine, sine, q_gain, k_gain
):
    span, q_width = q_proj.shape
    kv_width = k_proj.shape[1]
    head_dim = q_gain.shape[1]
    heads, group = kv_width // head_dim, q_width // kv_width
    q_spec = pl.BlockSpec((span, group * head_dim), lambda head: (0, head))
    k_spec = pl.BlockSpec((span, head_dim), lambda head: (0, head))
    table = pl.BlockSpec((span, head_dim), lambda head: (0, 0))
    gain = pl.BlockSpec((1, head_dim), lambda head: (0, 0))
    return pl.pallas_call(
        attend_back_kernel,
        grid=(heads,),
        in_specs=[
            q_spec,
            k_spec,
            k_spec,
            q_spec,
            pl.BlockSpec((1, group, span), lambda h: (h, 0, 0)),
            q_spec,
            k_spec,
            table,
            table,
            gain,
            gain,
        ],
        out_specs=[q_spec, k_spec, k_spec, pl.BlockSpec((1, 8, head_dim), lambda h: (h, 0, 0))],
        out_shape=[
            jax.ShapeDtypeStruct((span, q_width), jnp.bfloat16),
            jax.ShapeDtypeStruct((span, kv_width), jnp.bfloat16),
            jax.ShapeDtypeStruct((span, kv_width), jnp.bfloat16),
            jax.ShapeDtypeStruct((heads, 8, head_dim), jnp.float32),
        ],
        scratch_shapes=[
            pltpu.VMEM((span, head_dim), jnp.float32),
            pltpu.VMEM((span, head_dim), jnp.float32),
        ],
        compiler_params=pltpu.CompilerParams(vmem_limit_bytes=VMEM_BYTES),
        cost_estimate=pl.CostEstimate(
            flops=5 * span * span * q_width * 2,
            bytes_accessed=span * (q_width * 12 + kv_width * 12),
            transcendentals=span * span * heads * group // 2,
        ),
        name="attend_back",
    )(query_low, key_low, value_low, grad_out, lse, q_proj, k_proj, cosine, sine, q_gain, k_gain)


def swap(values, axis):
    return lax.ppermute(values, axis, [(0, 1), (1, 0)])


def turn(values):
    return lax.ppermute(values, ("c", "x"), [(0, 0), (1, 2), (2, 1), (3, 3)])


def rows_at(values, index, count):
    return lax.dynamic_slice_in_dim(values, index * count, count, axis=0)


def cols_at(values, index, count):
    return lax.dynamic_slice_in_dim(values, index * count, count, axis=1)


def ordered(first, mine, other, axis=0):
    return jnp.where(
        first,
        jnp.concatenate([mine, other], axis=axis),
        jnp.concatenate([other, mine], axis=axis),
    )


def paired(
    tokens,
    positions,
    cotangent,
    norm1_gain,
    w_query,
    w_key,
    w_value,
    w_out,
    query_gain,
    key_gain,
    norm2_gain,
    w_gate,
    w_up,
    w_down,
):
    x, c = lax.axis_index("x"), lax.axis_index("c")
    half, width = tokens.shape
    head_dim = query_gain.shape[0] * 2
    bf16, f32 = jnp.bfloat16, jnp.float32

    def flip(values):
        mid = values.shape[1] // 2
        swapped = jnp.concatenate([values[:, mid:], values[:, :mid]], axis=1)
        return jnp.where(x == 0, values, swapped)

    def both(values):
        return ordered(c == 0, values, swap(values, "c"))

    def fetch(piece):
        count = piece.shape[0] // 2
        y = lax.axis_index("y")
        near = swap(rows_at(piece, y, count), "x")
        return ordered(y == 0, near, swap(near, "y"))

    def column_parts(weight):
        count = weight.shape[1] // 4
        return cols_at(weight, 2 * x + c, count), cols_at(weight, 2 * (1 - x) + c, count)

    def column_weights(weights):
        parts = [column_parts(weight) for weight in weights]
        own = jnp.concatenate([part for pair in parts for part in pair], axis=1)
        sent = jnp.concatenate([part for pair in parts for part in pair[::-1]], axis=1)
        return jnp.concatenate([own, fetch(sent)], axis=0)

    def row_weights(weight):
        own = rows_at(weight, c, weight.shape[0] // 2)
        return jnp.concatenate([own, fetch(own)], axis=0)

    own_tokens = turn(tokens)
    all_tokens = both(own_tokens)
    places = both(turn(positions))
    gains = jnp.concatenate([norm1_gain, norm2_gain, query_gain, key_gain])
    far_gains = swap(gains, "x")
    gains, far_gains = gains.astype(f32), far_gains.astype(f32)
    part = norm1_gain.shape[0]
    q_part = query_gain.shape[0]
    gain_one = jnp.concatenate([gains[:part], far_gains[:part]])
    gain_two = jnp.concatenate([gains[part : 2 * part], far_gains[part : 2 * part]])
    q_gain = ordered(
        x == 0, gains[2 * part : 2 * part + q_part], far_gains[2 * part : 2 * part + q_part]
    )[None]
    k_gain = ordered(x == 0, gains[2 * part + q_part :], far_gains[2 * part + q_part :])[None]

    qkv_w = column_weights([w_query, w_key, w_value])
    out_w = row_weights(w_out)
    own_cot = turn(cotangent)
    all_cot = both(own_cot)
    gu_w = column_weights([w_gate, w_up])
    down_w = row_weights(w_down)

    cosine, sine = rotation_tables(places, head_dim)
    cosine = jnp.concatenate([cosine[:, 0], cosine[:, 0]], axis=-1)
    sine = jnp.concatenate([-sine[:, 0], sine[:, 0]], axis=-1)

    x_all = flip(all_tokens).astype(f32)
    h_one = (x_all * rms_scale(x_all) * gain_one).astype(bf16)
    q_width = w_query.shape[1] // 2
    kv_width = w_key.shape[1] // 2
    qkv = jnp.dot(h_one, qkv_w, preferred_element_type=f32)
    q_proj, k_proj = qkv[:, :q_width], qkv[:, q_width : q_width + kv_width]
    value_low = qkv[:, q_width + kv_width :].astype(bf16)
    out_low, query_low, key_low, lse = attend(
        q_proj, k_proj, value_low, cosine, sine, q_gain, k_gain
    )

    def shared(left, right, product):
        sent = product(rows_at(left, 1 - c, half), right).astype(bf16)
        got = swap(sent, "c")
        return product(rows_at(left, c, half), right) + got.astype(f32)

    def plain(left, right):
        return jnp.dot(left, right, preferred_element_type=f32)

    x_own = own_tokens.astype(f32)
    resid = x_own + shared(out_low, out_w, plain)
    resid_flip = flip(resid)
    h_two = both((resid_flip * rms_scale(resid_flip) * gain_two).astype(bf16))
    units = w_down.shape[0]
    gate_up = jnp.dot(h_two, gu_w, preferred_element_type=f32)
    gate, up_val = gate_up[:, :units], gate_up[:, units:]
    sigmoid_gate = jax.nn.sigmoid(gate)
    hidden_low = (gate * sigmoid_gate * up_val).astype(bf16)
    grad_hidden = times_t(all_cot, down_w)
    grad_gate_low = (
        grad_hidden * up_val * sigmoid_gate * (1.0 + gate * (1.0 - sigmoid_gate))
    ).astype(bf16)
    grad_up_low = (grad_hidden * gate * sigmoid_gate).astype(bf16)
    grad_gu = jnp.concatenate([grad_gate_low, grad_up_low], axis=1)

    def rs(values, axis):
        index, count = lax.axis_index(axis), values.shape[0] // 2
        return rows_at(values, index, count) + swap(rows_at(values, 1 - index, count), axis)

    def ag(values, axis):
        return ordered(lax.axis_index(axis) == 0, values, swap(values, axis))

    def total_of(values):
        values = rs(values, "y")
        values = rs(values, "za")
        values = values + swap(values, "zb")
        values = ag(values, "za")
        return ag(values, "y")

    def grad_rows(left, right):
        rows = left.shape[1] // 2
        sent = inner_rows(left[:, rows:], right).astype(bf16)
        got = swap(sent, "x")
        mine = total_of((inner_rows(left[:, :rows], right) + got.astype(f32)).astype(bf16))
        return ordered(c == 0, mine, swap(mine, "c")).astype(f32)

    def grad_cols(left, right, widths):
        rows = left.shape[1] // 2
        sent = inner_rows(left[:, rows:], right).astype(bf16)
        got = swap(sent, "x")
        kept = inner_rows(left[:, :rows], right)
        pieces, at = [], 0
        for count in widths:
            pieces += [got[:, at + count : at + 2 * count], got[:, at : at + count]]
            at += 2 * count
        mine = total_of((kept + jnp.concatenate(pieces, axis=1).astype(f32)).astype(bf16))
        other = swap(mine, "c")
        results, at = [], 0
        for count in widths:

            def block(values, index):
                return jnp.where(
                    x == index,
                    values[:, at : at + count],
                    values[:, at + count : at + 2 * count],
                )

            results.append(
                jnp.concatenate(
                    [
                        piece
                        for index in range(2)
                        for piece in (
                            jnp.where(c == 0, block(mine, index), block(other, index)),
                            jnp.where(c == 0, block(other, index), block(mine, index)),
                        )
                    ],
                    axis=1,
                ).astype(f32)
            )
            at += 2 * count
        return results

    grad_down = grad_rows(hidden_low, all_cot)
    grad_gate_w, grad_up_w = grad_cols(h_two, grad_gu, [units // 2, units // 2])
    result = turn((resid + shared(hidden_low, down_w, plain)).astype(bf16))

    grad_h_two = shared(grad_gu, gu_w, times_t)
    resid_part, gain_two_terms = norm_back(resid_flip, gain_two, grad_h_two)
    grad_resid = own_cot.astype(f32) + flip(resid_part)
    resid_low = both(grad_resid.astype(bf16))
    grad_out_w = grad_rows(out_low, resid_low)
    grad_att = times_t(resid_low, out_w).astype(bf16)
    grad_query, grad_key, grad_value, head_gains = attend_back(
        query_low,
        key_low,
        value_low,
        grad_att,
        lse,
        q_proj,
        k_proj,
        cosine,
        sine,
        q_gain,
        k_gain,
    )
    grad_qkv = jnp.concatenate([grad_query, grad_key, grad_value], axis=1)
    grad_query_w, grad_key_w, grad_value_w = grad_cols(
        h_one, grad_qkv, [q_width // 2, kv_width // 2, kv_width // 2]
    )
    grad_h_one = shared(grad_qkv, qkv_w, times_t)
    input_part, gain_one_terms = norm_back(flip(x_own), gain_one, grad_h_one)
    grad_input = turn((grad_resid + flip(input_part)).astype(bf16)).astype(f32)

    def natural(values):
        return ordered(x == 0, values[:part], values[part:])

    gain_sums = jnp.concatenate(
        [
            natural(jnp.sum(gain_one_terms, axis=0)),
            natural(jnp.sum(gain_two_terms, axis=0)),
            jnp.sum(head_gains[:, 0], axis=0),
            jnp.sum(head_gains[:, 1], axis=0),
        ]
    )
    gain_sums = lax.psum(gain_sums, ("zb", "za", "y", "c", "x"))

    def own_gain(start, count):
        return lax.dynamic_slice_in_dim(gain_sums, start + x * count, count)

    return (
        result,
        grad_input,
        own_gain(0, part),
        grad_query_w,
        grad_key_w,
        grad_value_w,
        grad_out_w,
        own_gain(4 * part, q_part),
        own_gain(4 * part + 2 * q_part, q_part),
        own_gain(2 * part, part),
        grad_gate_w,
        grad_up_w,
        grad_down,
    )


def solution(mesh):
    if mesh.shape["shard"] == 2 and mesh.shape["replica"] == 16:
        names = ("zb", "za", "y", "c", "x")
        grid = Mesh(mesh.devices.reshape((2,) * len(names)), names)
        body, over, owned = paired, names, "x"
    else:
        grid, body, over, owned = mesh, local, ("replica", "shard"), "shard"
    rows, vector, matrix = P(over, None), P(owned), P(owned, None)
    return jax.shard_map(
        body,
        mesh=grid,
        in_specs=(
            rows,
            P(over),
            rows,
            vector,
            matrix,
            matrix,
            matrix,
            matrix,
            vector,
            vector,
            vector,
            matrix,
            matrix,
            matrix,
        ),
        out_specs=(
            rows,
            rows,
            vector,
            matrix,
            matrix,
            matrix,
            matrix,
            vector,
            vector,
            vector,
            matrix,
            matrix,
            matrix,
        ),
        check_vma=False,
    )
```

```python
import functools
from functools import partial
import math

import jax
import jax.numpy as jnp
from jax import lax
from jax.experimental import pallas as pl
from jax.experimental.pallas import tpu as pltpu
from jax.sharding import Mesh, PartitionSpec as P

EPS = 1e-06
THETA = 1000000.0
NEG = -1e30
QUERY_BLOCK = 256
UNIT_BLOCK = 256
VMEM_BYTES = 56 * 1024 * 1024
GAIN_ROWS = 64
ROW_BLOCK = 256


def rms_scale(values):
    return lax.rsqrt(jnp.mean(values * values, axis=-1, keepdims=True) + EPS)


def norm_back(values, gain, incoming):
    scale = rms_scale(values)
    normed = values * scale
    scaled_in = incoming * gain
    return (
        scale * (scaled_in - normed * jnp.mean(scaled_in * normed, axis=-1, keepdims=True)),
        incoming * normed,
    )


def rotation_tables(places, width):
    half_width = width // 2
    freqs = THETA ** (-jnp.arange(half_width, dtype=jnp.float32) * 2.0 / width)
    angles = places.astype(jnp.float32)[:, None, None] * freqs
    return (jnp.cos(angles), jnp.sin(angles))


def rotate(values, cosine, sine_table):
    half_width = values.shape[-1] // 2
    first_half, second_half = (values[..., :half_width], values[..., half_width:])
    return jnp.concatenate(
        [
            first_half * cosine - second_half * sine_table,
            second_half * cosine + first_half * sine_table,
        ],
        axis=-1,
    )


def unrotate(grads, cosine, sine_table):
    half_width = grads.shape[-1] // 2
    first_half, second_half = (grads[..., :half_width], grads[..., half_width:])
    return jnp.concatenate(
        [
            first_half * cosine + second_half * sine_table,
            second_half * cosine - first_half * sine_table,
        ],
        axis=-1,
    )


def inner_rows(left, right):
    return lax.dot_general(
        left, right, (((0,), (0,)), ((), ())), preferred_element_type=jnp.float32
    )


def times_t(left, right):
    return lax.dot_general(
        left, right, (((1,), (1,)), ((), ())), preferred_element_type=jnp.float32
    )


def local(
    tokens,
    positions,
    cotangent,
    norm1_gain,
    w_query,
    w_key,
    w_value,
    w_out,
    query_gain,
    key_gain,
    norm2_gain,
    w_gate,
    w_up,
    w_down,
):
    row_count = tokens.shape[0]
    blocks = lax.axis_size("shard")
    own_index = lax.axis_index("shard")
    head_dim = query_gain.shape[0] * blocks
    attn_set = (
        lax.all_gather(norm1_gain, "shard", axis=0, tiled=True),
        lax.all_gather(w_query, "shard", axis=0, tiled=True),
        lax.all_gather(w_key, "shard", axis=0, tiled=True),
        lax.all_gather(w_value, "shard", axis=0, tiled=True),
        lax.all_gather(w_out, "shard", axis=0, tiled=True),
        lax.all_gather(query_gain, "shard", axis=0, tiled=True),
        lax.all_gather(key_gain, "shard", axis=0, tiled=True),
    )
    gain_one = attn_set[0].astype(jnp.float32)
    q_gain = attn_set[5].astype(jnp.float32)
    k_gain = attn_set[6].astype(jnp.float32)
    q_heads = attn_set[1].shape[1] // head_dim
    kv_heads = attn_set[2].shape[1] // head_dim
    group = q_heads // kv_heads
    inv_scale = 1.0 / math.sqrt(head_dim)
    cosine, sine_table = rotation_tables(positions, head_dim)
    x_float = tokens.astype(jnp.float32)
    h_one = (x_float * rms_scale(x_float) * gain_one).astype(jnp.bfloat16)
    q_proj = jnp.dot(h_one, attn_set[1], preferred_element_type=jnp.float32).reshape(
        row_count, q_heads, head_dim
    )
    k_proj = jnp.dot(h_one, attn_set[2], preferred_element_type=jnp.float32).reshape(
        row_count, kv_heads, head_dim
    )
    v_low = jnp.dot(h_one, attn_set[3], preferred_element_type=jnp.float32).astype(jnp.bfloat16)
    q_low = (rotate(q_proj * rms_scale(q_proj) * q_gain, cosine, sine_table) * inv_scale).astype(
        jnp.bfloat16
    )
    q_low = q_low.reshape(row_count, kv_heads, group, head_dim)
    k_low = rotate(k_proj * rms_scale(k_proj) * k_gain, cosine, sine_table).astype(jnp.bfloat16)
    k_low = k_low.reshape(row_count, kv_heads * head_dim)
    key_full, value_full = (
        lax.all_gather(k_low, "shard", axis=0, tiled=True),
        lax.all_gather(v_low, "shard", axis=0, tiled=True),
    )
    query_place = own_index * row_count + jnp.arange(row_count)

    def block_of(full, kblock):
        return full[kblock * row_count : (kblock + 1) * row_count].reshape(
            row_count, kv_heads, head_dim
        )

    def block_scores(keys_all, kblock):
        raw = jnp.einsum(
            "sngd,tnd->ngst", q_low, block_of(keys_all, kblock), preferred_element_type=jnp.float32
        )
        key_place = kblock * row_count + jnp.arange(row_count)
        return jnp.where(key_place[None, :] <= query_place[:, None], raw, NEG)

    empty_scores = jnp.full((kv_heads, group, row_count, row_count), NEG, jnp.float32)
    zero_scores = jnp.zeros((kv_heads, group, row_count, row_count), jnp.float32)
    zero_out = jnp.zeros((row_count, kv_heads, group, head_dim), jnp.float32)
    zero_keys = jnp.zeros((row_count, kv_heads, head_dim), jnp.float32)
    score_list = [
        lax.cond(kblock <= own_index, partial(block_scores, key_full, kblock), lambda: empty_scores)
        for kblock in range(blocks)
    ]
    score_all = jnp.concatenate(score_list, axis=-1)
    peak = jnp.max(score_all, axis=-1, keepdims=True)
    log_total = peak + jnp.log(jnp.sum(jnp.exp(score_all - peak), axis=-1, keepdims=True))
    probs_low = jnp.exp(score_all - log_total).astype(jnp.bfloat16)

    def block_output(kblock):
        part_probs = probs_low[..., kblock * row_count : (kblock + 1) * row_count]
        return jnp.einsum(
            "ngst,tnd->sngd",
            part_probs,
            block_of(value_full, kblock),
            preferred_element_type=jnp.float32,
        )

    attended = zero_out
    for kblock in range(blocks):
        attended = attended + lax.cond(
            kblock <= own_index, partial(block_output, kblock), lambda: zero_out
        )
    out_low = attended.reshape(row_count, q_heads * head_dim).astype(jnp.bfloat16)
    resid_one = x_float + jnp.dot(out_low, attn_set[4], preferred_element_type=jnp.float32)
    mlp_set = (
        lax.all_gather(norm2_gain, "shard", axis=0, tiled=True),
        lax.all_gather(w_gate, "shard", axis=0, tiled=True),
        lax.all_gather(w_up, "shard", axis=0, tiled=True),
        lax.all_gather(w_down, "shard", axis=0, tiled=True),
    )
    gain_two = mlp_set[0].astype(jnp.float32)
    h_two = (resid_one * rms_scale(resid_one) * gain_two).astype(jnp.bfloat16)
    gate = jnp.dot(h_two, mlp_set[1], preferred_element_type=jnp.float32)
    up_val = jnp.dot(h_two, mlp_set[2], preferred_element_type=jnp.float32)
    sigmoid_gate = jax.nn.sigmoid(gate)
    hidden_low = (gate * sigmoid_gate * up_val).astype(jnp.bfloat16)
    result = (
        resid_one + jnp.dot(hidden_low, mlp_set[3], preferred_element_type=jnp.float32)
    ).astype(jnp.bfloat16)
    mlp_back = (
        lax.all_gather(norm2_gain, "shard", axis=0, tiled=True),
        lax.all_gather(w_gate, "shard", axis=0, tiled=True),
        lax.all_gather(w_up, "shard", axis=0, tiled=True),
        lax.all_gather(w_down, "shard", axis=0, tiled=True),
    )
    grad_hidden = times_t(cotangent, mlp_back[3])
    grad_gate_low = (
        grad_hidden * up_val * sigmoid_gate * (1.0 + gate * (1.0 - sigmoid_gate))
    ).astype(jnp.bfloat16)
    grad_up_low = (grad_hidden * gate * sigmoid_gate).astype(jnp.bfloat16)
    grad_h_two = times_t(grad_gate_low, mlp_back[1]) + times_t(grad_up_low, mlp_back[2])
    resid_part, gain_two_terms = norm_back(resid_one, gain_two, grad_h_two)
    grad_resid = cotangent.astype(jnp.float32) + resid_part
    grad_down = inner_rows(hidden_low, cotangent)
    grad_gate_w = inner_rows(h_two, grad_gate_low)
    grad_up_w = inner_rows(h_two, grad_up_low)
    mlp_shares = (
        lax.psum_scatter(
            jnp.sum(gain_two_terms, axis=0).astype(jnp.bfloat16),
            "shard",
            scatter_dimension=0,
            tiled=True,
        ).astype(jnp.float32),
        lax.psum_scatter(
            grad_gate_w.astype(jnp.bfloat16), "shard", scatter_dimension=0, tiled=True
        ).astype(jnp.float32),
        lax.psum_scatter(
            grad_up_w.astype(jnp.bfloat16), "shard", scatter_dimension=0, tiled=True
        ).astype(jnp.float32),
        lax.psum_scatter(
            grad_down.astype(jnp.bfloat16), "shard", scatter_dimension=0, tiled=True
        ).astype(jnp.float32),
    )
    attn_back = (
        lax.all_gather(norm1_gain, "shard", axis=0, tiled=True),
        lax.all_gather(w_query, "shard", axis=0, tiled=True),
        lax.all_gather(w_key, "shard", axis=0, tiled=True),
        lax.all_gather(w_value, "shard", axis=0, tiled=True),
        lax.all_gather(w_out, "shard", axis=0, tiled=True),
        lax.all_gather(query_gain, "shard", axis=0, tiled=True),
        lax.all_gather(key_gain, "shard", axis=0, tiled=True),
    )
    resid_low = grad_resid.astype(jnp.bfloat16)
    grad_att_low = (
        times_t(resid_low, attn_back[4])
        .astype(jnp.bfloat16)
        .reshape(row_count, kv_heads, group, head_dim)
    )
    key_back, value_back = (key_full, value_full)

    def first_pass(kblock):
        part_probs = jnp.exp(block_scores(key_back, kblock) - log_total)
        part_dprobs = jnp.einsum(
            "sngd,tnd->ngst",
            grad_att_low,
            block_of(value_back, kblock),
            preferred_element_type=jnp.float32,
        )
        return (part_probs, part_dprobs)

    pass_list = [
        lax.cond(
            kblock <= own_index, partial(first_pass, kblock), lambda: (zero_scores, zero_scores)
        )
        for kblock in range(blocks)
    ]
    delta_sum = jnp.zeros((kv_heads, group, row_count, 1), jnp.float32)
    for part_probs, part_dprobs in pass_list:
        delta_sum = delta_sum + jnp.sum(part_probs * part_dprobs, axis=-1, keepdims=True)

    def second_pass(kblock):
        part_probs, part_dprobs = pass_list[kblock]
        dscore_low = (part_probs * (part_dprobs - delta_sum)).astype(jnp.bfloat16)
        query_term = jnp.einsum(
            "ngst,tnd->sngd",
            dscore_low,
            block_of(key_back, kblock),
            preferred_element_type=jnp.float32,
        )
        key_term = jnp.einsum(
            "ngst,sngd->tnd", dscore_low, q_low, preferred_element_type=jnp.float32
        )
        value_term = jnp.einsum(
            "ngst,sngd->tnd",
            part_probs.astype(jnp.bfloat16),
            grad_att_low,
            preferred_element_type=jnp.float32,
        )
        return (query_term, key_term, value_term)

    grad_query = zero_out
    key_terms = []
    value_terms = []
    for kblock in range(blocks):
        query_term, key_term, value_term = lax.cond(
            kblock <= own_index,
            partial(second_pass, kblock),
            lambda: (zero_out, zero_keys, zero_keys),
        )
        grad_query = grad_query + query_term
        key_terms.append(key_term.reshape(row_count, kv_heads * head_dim))
        value_terms.append(value_term.reshape(row_count, kv_heads * head_dim))
    grad_key_local, grad_value_local = (
        lax.psum_scatter(
            jnp.concatenate(key_terms, axis=0).astype(jnp.bfloat16),
            "shard",
            scatter_dimension=0,
            tiled=True,
        ).astype(jnp.float32),
        lax.psum_scatter(
            jnp.concatenate(value_terms, axis=0).astype(jnp.bfloat16),
            "shard",
            scatter_dimension=0,
            tiled=True,
        ).astype(jnp.float32),
    )
    grad_value_low = grad_value_local.astype(jnp.bfloat16)
    key_rot = unrotate(grad_key_local.reshape(row_count, kv_heads, head_dim), cosine, sine_table)
    key_proj_grad, key_gain_terms = norm_back(k_proj, k_gain, key_rot)
    grad_key_low = key_proj_grad.reshape(row_count, kv_heads * head_dim).astype(jnp.bfloat16)
    query_rot = unrotate(
        grad_query.reshape(row_count, q_heads, head_dim) * inv_scale, cosine, sine_table
    )
    query_proj_grad, query_gain_terms = norm_back(q_proj, q_gain, query_rot)
    grad_query_low = query_proj_grad.reshape(row_count, q_heads * head_dim).astype(jnp.bfloat16)
    grad_h_one = (
        times_t(grad_query_low, attn_back[1])
        + times_t(grad_key_low, attn_back[2])
        + times_t(grad_value_low, attn_back[3])
    )
    input_part, gain_one_terms = norm_back(x_float, gain_one, grad_h_one)
    grad_input = grad_resid + input_part
    gain_one_sum = jnp.sum(gain_one_terms, axis=0)
    query_gain_sum = jnp.sum(query_gain_terms, axis=(0, 1))
    key_gain_sum = jnp.sum(key_gain_terms, axis=(0, 1))
    grad_out_w = inner_rows(out_low, resid_low)
    grad_query_w = inner_rows(h_one, grad_query_low)
    grad_key_w = inner_rows(h_one, grad_key_low)
    grad_value_w = inner_rows(h_one, grad_value_low)
    attn_shares = (
        lax.psum_scatter(
            gain_one_sum.astype(jnp.bfloat16), "shard", scatter_dimension=0, tiled=True
        ).astype(jnp.float32),
        lax.psum_scatter(
            grad_query_w.astype(jnp.bfloat16), "shard", scatter_dimension=0, tiled=True
        ).astype(jnp.float32),
        lax.psum_scatter(
            grad_key_w.astype(jnp.bfloat16), "shard", scatter_dimension=0, tiled=True
        ).astype(jnp.float32),
        lax.psum_scatter(
            grad_value_w.astype(jnp.bfloat16), "shard", scatter_dimension=0, tiled=True
        ).astype(jnp.float32),
        lax.psum_scatter(
            grad_out_w.astype(jnp.bfloat16), "shard", scatter_dimension=0, tiled=True
        ).astype(jnp.float32),
        lax.psum_scatter(
            query_gain_sum.astype(jnp.bfloat16), "shard", scatter_dimension=0, tiled=True
        ).astype(jnp.float32),
        lax.psum_scatter(
            key_gain_sum.astype(jnp.bfloat16), "shard", scatter_dimension=0, tiled=True
        ).astype(jnp.float32),
    )
    totals = (
        lax.psum(attn_shares[0].astype(jnp.bfloat16), "replica").astype(jnp.float32),
        lax.psum(attn_shares[1].astype(jnp.bfloat16), "replica").astype(jnp.float32),
        lax.psum(attn_shares[2].astype(jnp.bfloat16), "replica").astype(jnp.float32),
        lax.psum(attn_shares[3].astype(jnp.bfloat16), "replica").astype(jnp.float32),
        lax.psum(attn_shares[4].astype(jnp.bfloat16), "replica").astype(jnp.float32),
        lax.psum(attn_shares[5].astype(jnp.bfloat16), "replica").astype(jnp.float32),
        lax.psum(attn_shares[6].astype(jnp.bfloat16), "replica").astype(jnp.float32),
        lax.psum(mlp_shares[0].astype(jnp.bfloat16), "replica").astype(jnp.float32),
        lax.psum(mlp_shares[1].astype(jnp.bfloat16), "replica").astype(jnp.float32),
        lax.psum(mlp_shares[2].astype(jnp.bfloat16), "replica").astype(jnp.float32),
        lax.psum(mlp_shares[3].astype(jnp.bfloat16), "replica").astype(jnp.float32),
    )
    return (
        result,
        grad_input,
        totals[0],
        totals[1],
        totals[2],
        totals[3],
        totals[4],
        totals[5],
        totals[6],
        totals[7],
        totals[8],
        totals[9],
        totals[10],
    )
NO_COST = pl.CostEstimate(flops=0, bytes_accessed=0, transcendentals=0)


def head_norm(values, gain):
    scale = lax.rsqrt(jnp.mean(values * values, axis=-1, keepdims=True) + EPS)
    return values * scale * gain


def attend_kernel(
    h_ref, w_ref, cos_ref, sin_ref, qg_ref, kg_ref, o_ref, q_ref, k_ref, lse_ref, qkv_ref
):
    qkv_ref[...] = jnp.dot(h_ref[...], w_ref[...], preferred_element_type=jnp.float32)
    span, head_dim = cos_ref.shape
    group = o_ref.shape[1] // head_dim
    block = min(QUERY_BLOCK, span)
    cosine, sine = cos_ref[...], sin_ref[...]
    key_lanes = slice(group * head_dim, (group + 1) * head_dim)
    keyed = head_norm(qkv_ref[:, key_lanes], kg_ref[...])
    key_low = (keyed * cosine + pltpu.roll(keyed, head_dim // 2, 1) * sine).astype(jnp.bfloat16)
    k_ref[...] = key_low
    value_t = qkv_ref[:, (group + 1) * head_dim :].astype(jnp.bfloat16).T
    ahead = lax.broadcasted_iota(jnp.int32, (block, block), 0) > lax.broadcasted_iota(
        jnp.int32, (block, block), 1
    )
    for head in range(group):
        lanes = slice(head * head_dim, (head + 1) * head_dim)
        asked = head_norm(qkv_ref[:, lanes], qg_ref[...])
        asked = asked * cosine + pltpu.roll(asked, head_dim // 2, 1) * sine
        query_low = (asked * (1.0 / math.sqrt(head_dim))).astype(jnp.bfloat16)
        q_ref[:, lanes] = query_low
        for start in range(0, span, block):
            stop = start + block
            scores = times_t(key_low[:stop], query_low[start:stop])
            last = jnp.where(ahead, NEG, scores[start:])
            scores = last if start == 0 else jnp.concatenate([scores[:start], last], axis=0)
            peak = jnp.max(scores, axis=0, keepdims=True)
            powers = jnp.exp(scores - peak)
            total = jnp.sum(powers, axis=0, keepdims=True)
            lse_ref[0, head : head + 1, start:stop] = peak + jnp.log(total)
            probs = (powers * (1.0 / total)).astype(jnp.bfloat16)
            out_t = jnp.dot(value_t[:, :stop], probs, preferred_element_type=jnp.float32)
            o_ref[start:stop, lanes] = out_t.T.astype(jnp.bfloat16)


def attend_back_kernel(
    q_ref,
    k_ref,
    qkv_ref,
    do_ref,
    lse_ref,
    cos_ref,
    sin_ref,
    qg_ref,
    kg_ref,
    h_ref,
    w_ref,
    *rest,
    first,
):
    dh_in = None if first else rest[0]
    grad_ref, gain_ref, dh_ref, own_ref, key_acc, value_acc, ht_ref = rest[0 if first else 1 :]
    span, head_dim = cos_ref.shape
    group = q_ref.shape[1] // head_dim

    @pl.when(pl.program_id(0) == 0)
    def _():
        ht_ref[...] = h_ref[...].T
        dh_ref[...] = jnp.zeros_like(dh_ref) if first else dh_in[...]

    block = min(QUERY_BLOCK, span)
    inv_scale = 1.0 / math.sqrt(head_dim)
    key_lanes = slice(group * head_dim, (group + 1) * head_dim)
    value_lanes = slice((group + 1) * head_dim, (group + 2) * head_dim)
    key_low, value_low = k_ref[...], qkv_ref[:, value_lanes].astype(jnp.bfloat16)
    key_t = key_low.T
    ahead = lax.broadcasted_iota(jnp.int32, (block, block), 0) > lax.broadcasted_iota(
        jnp.int32, (block, block), 1
    )

    def proj_back(grads, proj, cosine, sine, gain):
        turned = grads * cosine - pltpu.roll(grads, head_dim // 2, 1) * sine
        scale = lax.rsqrt(jnp.mean(proj * proj, axis=-1, keepdims=True) + EPS)
        normed = proj * scale
        scaled = turned * gain
        back = scale * (scaled - normed * jnp.mean(scaled * normed, axis=-1, keepdims=True))
        return back, jnp.sum(turned * normed, axis=0, keepdims=True)

    key_acc[...] = jnp.zeros_like(key_acc)
    value_acc[...] = jnp.zeros_like(value_acc)
    query_gain = jnp.zeros((1, head_dim), jnp.float32)
    for head in range(group):
        lanes = slice(head * head_dim, (head + 1) * head_dim)
        for start in range(0, span, block):
            stop = start + block
            rows = slice(start, stop)
            query_low, grad_out = q_ref[rows, lanes], do_ref[rows, lanes]
            scores = times_t(key_low[:stop], query_low)
            last = jnp.where(ahead, NEG, scores[start:])
            scores = last if start == 0 else jnp.concatenate([scores[:start], last], axis=0)
            probs = jnp.exp(scores - lse_ref[0, head : head + 1, rows])
            dprobs = times_t(value_low[:stop], grad_out)
            delta = jnp.sum(probs * dprobs, axis=0, keepdims=True)
            dscore = (probs * (dprobs - delta)).astype(jnp.bfloat16)
            value_acc[:stop, :] += jnp.dot(
                probs.astype(jnp.bfloat16), grad_out, preferred_element_type=jnp.float32
            )
            key_acc[:stop, :] += jnp.dot(dscore, query_low, preferred_element_type=jnp.float32)
            grad_query = jnp.dot(key_t[:, :stop], dscore, preferred_element_type=jnp.float32).T
            back, gain_term = proj_back(
                grad_query * inv_scale,
                qkv_ref[rows, lanes],
                cos_ref[rows, :],
                sin_ref[rows, :],
                qg_ref[...],
            )
            own_ref[rows, lanes] = back.astype(jnp.bfloat16)
            query_gain = query_gain + gain_term
    back, key_gain = proj_back(
        key_acc[...], qkv_ref[:, key_lanes], cos_ref[...], sin_ref[...], kg_ref[...]
    )
    own_ref[:, key_lanes] = back.astype(jnp.bfloat16)
    own_ref[:, value_lanes] = value_acc[...].astype(jnp.bfloat16)
    gain_ref[0] = jnp.concatenate(
        [query_gain, key_gain, jnp.zeros((gain_ref.shape[1] - 2, head_dim), jnp.float32)], axis=0
    )
    grads = own_ref[...]
    grad_ref[...] = jnp.dot(ht_ref[...], grads, preferred_element_type=jnp.float32).astype(
        jnp.bfloat16
    )
    dh_ref[...] += times_t(grads, w_ref[...])


def attend(h_one, qkv_w, cosine, sine, q_gain, k_gain, group):
    span, head_dim = cosine.shape
    step = (group + 2) * head_dim
    heads = qkv_w.shape[1] // step
    wide = pl.BlockSpec((span, step), lambda head: (0, head))
    q_spec = pl.BlockSpec((span, group * head_dim), lambda head: (0, head))
    k_spec = pl.BlockSpec((span, head_dim), lambda head: (0, head))
    table = pl.BlockSpec((span, head_dim), lambda head: (0, 0))
    gain = pl.BlockSpec((1, head_dim), lambda head: (0, 0))
    return pl.pallas_call(
        attend_kernel,
        grid=(heads,),
        in_specs=[
            pl.BlockSpec(h_one.shape, lambda head: (0, 0)),
            pl.BlockSpec((qkv_w.shape[0], step), lambda head: (0, head)),
            table,
            table,
            gain,
            gain,
        ],
        out_specs=[
            q_spec,
            q_spec,
            k_spec,
            pl.BlockSpec((1, group, span), lambda h: (h, 0, 0)),
            wide,
        ],
        out_shape=[
            jax.ShapeDtypeStruct((span, heads * group * head_dim), jnp.bfloat16),
            jax.ShapeDtypeStruct((span, heads * group * head_dim), jnp.bfloat16),
            jax.ShapeDtypeStruct((span, heads * head_dim), jnp.bfloat16),
            jax.ShapeDtypeStruct((heads, group, span), jnp.float32),
            jax.ShapeDtypeStruct((span, heads * step), jnp.float32),
        ],
        compiler_params=pltpu.CompilerParams(vmem_limit_bytes=VMEM_BYTES),
        cost_estimate=NO_COST,
        name="attend",
    )(h_one, qkv_w, cosine, sine, q_gain, k_gain)


def norm_first_kernel(place_ref, mine_ref, other_ref, gain_ref, h_ref):
    x, c = place_ref[0], place_ref[1]
    half = mine_ref.shape[0]
    for source, index in ((mine_ref, c), (other_ref, 1 - c)):
        values = source[...].astype(jnp.float32)
        values = jnp.where(x == 0, values, pltpu.roll(values, values.shape[1] // 2, 1))
        normed = (values * rms_scale(values) * gain_ref[...]).astype(jnp.bfloat16)
        h_ref[pl.ds(pl.multiple_of(index * half, half), half), :] = normed


def norm_first(place, mine, other, gain):
    half, width = mine.shape
    return pl.pallas_call(
        norm_first_kernel,
        in_specs=[pl.BlockSpec(memory_space=pltpu.SMEM)]
        + [pl.BlockSpec(memory_space=pltpu.VMEM)] * 3,
        out_specs=pl.BlockSpec(memory_space=pltpu.VMEM),
        out_shape=jax.ShapeDtypeStruct((2 * half, width), jnp.bfloat16),
        compiler_params=pltpu.CompilerParams(vmem_limit_bytes=VMEM_BYTES),
        cost_estimate=NO_COST,
        name="norm_first",
    )(place, mine, other, gain)


def out_forward_kernel(place_ref, o_ref, w_ref, sent_ref, kept_ref):
    product = jnp.dot(o_ref[...], w_ref[...], preferred_element_type=jnp.float32)

    @pl.when(pl.program_id(0) == 0)
    def _():
        sent_ref[...] = product.astype(jnp.bfloat16)

    @pl.when(pl.program_id(0) == 1)
    def _():
        kept_ref[...] = product


def out_forward(place, out_low, out_w):
    half, count = out_low.shape[0] // 2, out_low.shape[1]
    width = out_w.shape[1]
    whole = pl.BlockSpec((half, width), lambda i, place: (0, 0))
    return pl.pallas_call(
        out_forward_kernel,
        grid_spec=pltpu.PrefetchScalarGridSpec(
            num_scalar_prefetch=1,
            grid=(2,),
            in_specs=[
                pl.BlockSpec(
                    (half, count), lambda i, place: (i * place[1] + (1 - i) * (1 - place[1]), 0)
                ),
                pl.BlockSpec((count, width), lambda i, place: (0, 0)),
            ],
            out_specs=[whole, whole],
        ),
        out_shape=[
            jax.ShapeDtypeStruct((half, width), jnp.bfloat16),
            jax.ShapeDtypeStruct((half, width), jnp.float32),
        ],
        compiler_params=pltpu.CompilerParams(vmem_limit_bytes=VMEM_BYTES),
        cost_estimate=NO_COST,
        name="out_forward",
    )(place, out_low, out_w)


def norm_second_kernel(place_ref, x_ref, kept_ref, got_ref, gain_ref, resid_ref, h_ref):
    resid = x_ref[...].astype(jnp.float32) + kept_ref[...] + got_ref[...].astype(jnp.float32)
    resid_ref[...] = resid
    values = jnp.where(place_ref[0] == 0, resid, pltpu.roll(resid, resid.shape[1] // 2, 1))
    h_ref[...] = (values * rms_scale(values) * gain_ref[...]).astype(jnp.bfloat16)


def norm_second(place, tokens, kept, got, gain):
    half, width = tokens.shape
    rows = min(ROW_BLOCK, half)
    spec = pl.BlockSpec((rows, width), lambda i, place: (i, 0))
    return pl.pallas_call(
        norm_second_kernel,
        grid_spec=pltpu.PrefetchScalarGridSpec(
            num_scalar_prefetch=1,
            grid=(half // rows,),
            in_specs=[spec, spec, spec, pl.BlockSpec((1, width), lambda i, place: (0, 0))],
            out_specs=[spec, spec],
        ),
        out_shape=[
            jax.ShapeDtypeStruct((half, width), jnp.float32),
            jax.ShapeDtypeStruct((half, width), jnp.bfloat16),
        ],
        compiler_params=pltpu.CompilerParams(vmem_limit_bytes=VMEM_BYTES),
        cost_estimate=NO_COST,
        name="norm_second",
    )(place, tokens, kept, got, gain)


def attend_back(
    query_low, key_low, qkv, grad_out, lse, cosine, sine, q_gain, k_gain, h_one, qkv_w, part, dh=None
):
    span, head_dim = cosine.shape
    width = h_one.shape[1]
    group = query_low.shape[1] // key_low.shape[1]
    heads = key_low.shape[1] // head_dim // 2
    base = part * heads
    step = (group + 2) * head_dim
    once = pl.Buffered(1)
    wide = pl.BlockSpec((span, step), lambda head: (0, base + head))
    q_spec = pl.BlockSpec((span, group * head_dim), lambda head: (0, base + head))
    k_spec = pl.BlockSpec((span, head_dim), lambda head: (0, base + head))
    table = pl.BlockSpec((span, head_dim), lambda head: (0, 0))
    gain = pl.BlockSpec((1, head_dim), lambda head: (0, 0))
    whole = pl.BlockSpec((span, width), lambda head: (0, 0), pipeline_mode=once)
    first = dh is None
    return pl.pallas_call(
        functools.partial(attend_back_kernel, first=first),
        grid=(heads,),
        in_specs=[
            q_spec,
            k_spec,
            wide,
            q_spec,
            pl.BlockSpec((1, group, span), lambda h: (base + h, 0, 0)),
            table,
            table,
            gain,
            gain,
            whole,
            pl.BlockSpec((width, step), lambda head: (0, base + head)),
        ]
        + ([] if first else [whole]),
        out_specs=[
            pl.BlockSpec((width, step), lambda head: (0, head)),
            pl.BlockSpec((1, 8, head_dim), lambda h: (h, 0, 0)),
            pl.BlockSpec((span, width), lambda head: (0, 0)),
        ],
        out_shape=[
            jax.ShapeDtypeStruct((width, heads * step), jnp.bfloat16),
            jax.ShapeDtypeStruct((heads, 8, head_dim), jnp.float32),
            jax.ShapeDtypeStruct((span, width), jnp.float32),
        ],
        scratch_shapes=[
            pltpu.VMEM((span, step), jnp.bfloat16),
            pltpu.VMEM((span, head_dim), jnp.float32),
            pltpu.VMEM((span, head_dim), jnp.float32),
            pltpu.VMEM((width, span), jnp.bfloat16),
        ],
        compiler_params=pltpu.CompilerParams(vmem_limit_bytes=VMEM_BYTES),
        cost_estimate=NO_COST,
        name="attend_back",
    )(
        query_low,
        key_low,
        qkv,
        grad_out,
        lse,
        cosine,
        sine,
        q_gain,
        k_gain,
        h_one,
        qkv_w,
        *([] if first else [dh]),
    )


def norm_back_kernel(place_ref, values_ref, part_ref, got_ref, base_ref, gain_ref, *outs):
    x = place_ref[0]

    def flipped(values):
        return jnp.where(x == 0, values, pltpu.roll(values, values.shape[1] // 2, 1))

    *sums, low_ref, gain_out = outs
    values = flipped(values_ref[...].astype(jnp.float32))
    incoming = part_ref[...] + got_ref[...].astype(jnp.float32)
    back, terms = norm_back(values, gain_ref[...], incoming)
    total = base_ref[...].astype(jnp.float32) + flipped(back)
    if sums:
        sums[0][...] = total
    low_ref[...] = total.astype(jnp.bfloat16)
    summed = jnp.sum(terms, axis=0, keepdims=True)

    @pl.when(pl.program_id(0) == 0)
    def _():
        gain_out[...] = jnp.zeros_like(gain_out)

    gain_out[...] += summed


def norm_gradient(place, values, part, got, base, gain, keep):
    half, width = values.shape
    rows = min(ROW_BLOCK, half)
    steps = half // rows
    spec = pl.BlockSpec((rows, width), lambda i, place: (i, 0))
    line = pl.BlockSpec((1, width), lambda i, place: (0, 0))
    shapes = [jax.ShapeDtypeStruct((half, width), jnp.bfloat16)]
    if keep:
        shapes = [jax.ShapeDtypeStruct((half, width), jnp.float32)] + shapes
    return pl.pallas_call(
        norm_back_kernel,
        grid_spec=pltpu.PrefetchScalarGridSpec(
            num_scalar_prefetch=1,
            grid=(steps,),
            in_specs=[
                spec,
                pl.BlockSpec((rows, width), lambda i, place: (place[1] * steps + i, 0)),
                spec,
                spec,
                line,
            ],
            out_specs=[spec] * len(shapes) + [line],
        ),
        out_shape=shapes + [jax.ShapeDtypeStruct((1, width), jnp.float32)],
        compiler_params=pltpu.CompilerParams(vmem_limit_bytes=VMEM_BYTES),
        cost_estimate=NO_COST,
        name="norm_gradient",
    )(place, values, part, got, base, gain)


def whole_rows(place_ref, mine_ref, other_ref, whole_ref):
    half, c = mine_ref.shape[0], place_ref[1]
    whole_ref[pl.ds(pl.multiple_of(c * half, half), half), :] = mine_ref[...]
    whole_ref[pl.ds(pl.multiple_of((1 - c) * half, half), half), :] = other_ref[...]


def out_back_kernel(place_ref, mine_ref, other_ref, o_ref, w_ref, do_ref, grad_ref, dr_ref):
    @pl.when(pl.program_id(0) == 0)
    def _():
        whole_rows(place_ref, mine_ref, other_ref, dr_ref)

    do_ref[...] = times_t(dr_ref[...], w_ref[...]).astype(jnp.bfloat16)
    grad_ref[...] = inner_rows(o_ref[...], dr_ref[...]).astype(jnp.bfloat16)


def out_back(place, mine, other, out_low, out_w):
    half, width = mine.shape
    count = out_low.shape[1]
    block = count // 4

    def at(i):
        return (i + 2) % 4

    whole = pl.BlockSpec((half, width), lambda i: (0, 0))
    return pl.pallas_call(
        out_back_kernel,
        grid=(4,),
        in_specs=[
            pl.BlockSpec(memory_space=pltpu.SMEM),
            whole,
            whole,
            pl.BlockSpec((2 * half, block), lambda i: (0, at(i))),
            pl.BlockSpec((block, width), lambda i: (at(i), 0)),
        ],
        out_specs=[
            pl.BlockSpec((2 * half, block), lambda i: (0, at(i))),
            pl.BlockSpec((block, width), lambda i: (at(i), 0)),
        ],
        out_shape=[
            jax.ShapeDtypeStruct((2 * half, count), jnp.bfloat16),
            jax.ShapeDtypeStruct((count, width), jnp.bfloat16),
        ],
        scratch_shapes=[pltpu.VMEM((2 * half, width), jnp.bfloat16)],
        compiler_params=pltpu.CompilerParams(vmem_limit_bytes=VMEM_BYTES),
        cost_estimate=NO_COST,
        name="out_back",
    )(place, mine, other, out_low, out_w)


def half_kernel(place_ref, whole_ref, half_ref):
    half_ref[...] = whole_ref[...].astype(half_ref.dtype)


def other_half(place, values):
    half, width = values.shape[0] // 2, values.shape[1]
    rows = min(ROW_BLOCK, half)
    steps = half // rows
    return pl.pallas_call(
        half_kernel,
        grid_spec=pltpu.PrefetchScalarGridSpec(
            num_scalar_prefetch=1,
            grid=(steps,),
            in_specs=[
                pl.BlockSpec((rows, width), lambda i, place: ((1 - place[1]) * steps + i, 0))
            ],
            out_specs=pl.BlockSpec((rows, width), lambda i, place: (i, 0)),
        ),
        out_shape=jax.ShapeDtypeStruct((half, width), jnp.bfloat16),
        compiler_params=pltpu.CompilerParams(vmem_limit_bytes=VMEM_BYTES),
        cost_estimate=NO_COST,
        name="other_half",
    )(place, values)


def mlp_kernel(place_ref, hm_ref, ho_ref, dm_ref, do_ref, gu_ref, down_ref, *rest, block, first):
    res_in, dh_in = (None, None) if first else rest[:2]
    ggu_ref, gdown_ref, res_ref, dh_ref, h_ref, dy_ref, ht_ref = rest[0 if first else 2 :]

    @pl.when(pl.program_id(0) == 0)
    def _():
        whole_rows(place_ref, hm_ref, ho_ref, h_ref)
        whole_rows(place_ref, dm_ref, do_ref, dy_ref)
        ht_ref[...] = h_ref[...].T
        res_ref[...] = jnp.zeros_like(res_ref) if first else res_in[...]
        dh_ref[...] = jnp.zeros_like(dh_ref) if first else dh_in[...]

    weights = gu_ref[...]
    both = jnp.dot(h_ref[...], weights, preferred_element_type=jnp.float32)
    gate, up_val = both[:, :block], both[:, block:]
    sigmoid_gate = jax.nn.sigmoid(gate)
    active = gate * sigmoid_gate
    grad_hidden = times_t(dy_ref[...], down_ref[...])
    hidden = (active * up_val).astype(jnp.bfloat16)
    grad_gate = (
        grad_hidden * up_val * sigmoid_gate * (1.0 + gate * (1.0 - sigmoid_gate))
    ).astype(jnp.bfloat16)
    grads = jnp.concatenate([grad_gate, (grad_hidden * active).astype(jnp.bfloat16)], axis=1)
    res_ref[...] += jnp.dot(hidden, down_ref[...], preferred_element_type=jnp.float32)
    dh_ref[...] += times_t(grads, weights)
    ggu_ref[...] = jnp.dot(ht_ref[...], grads, preferred_element_type=jnp.float32).astype(
        jnp.bfloat16
    )
    gdown_ref[...] = inner_rows(hidden, dy_ref[...]).astype(jnp.bfloat16)


def mlp(place, h_halves, dy_halves, gu_w, down_w, part, sums=None):
    half, width = h_halves[0].shape
    span = 2 * half
    units = down_w.shape[0] // 2
    block = math.gcd(UNIT_BLOCK, units)
    steps = units // block
    base = part * steps
    once = pl.Buffered(1)
    piece = pl.BlockSpec((half, width), lambda j: (0, 0), pipeline_mode=once)
    whole = pl.BlockSpec((span, width), lambda j: (0, 0), pipeline_mode=once)
    total = pl.BlockSpec((span, width), lambda j: (0, 0))
    first = sums is None
    return pl.pallas_call(
        functools.partial(mlp_kernel, block=block, first=first),
        grid=(steps,),
        in_specs=[
            pl.BlockSpec(memory_space=pltpu.SMEM),
            piece,
            piece,
            piece,
            piece,
            pl.BlockSpec((width, 2 * block), lambda j: (0, base + j)),
            pl.BlockSpec((block, width), lambda j: (base + j, 0)),
        ]
        + ([] if first else [whole, whole]),
        out_specs=[
            pl.BlockSpec((width, 2 * block), lambda j: (0, j)),
            pl.BlockSpec((block, width), lambda j: (j, 0)),
            total,
            total,
        ],
        out_shape=[
            jax.ShapeDtypeStruct((width, 2 * units), jnp.bfloat16),
            jax.ShapeDtypeStruct((units, width), jnp.bfloat16),
            jax.ShapeDtypeStruct((span, width), jnp.float32),
            jax.ShapeDtypeStruct((span, width), jnp.float32),
        ],
        scratch_shapes=[
            pltpu.VMEM((span, width), jnp.bfloat16),
            pltpu.VMEM((span, width), jnp.bfloat16),
            pltpu.VMEM((width, span), jnp.bfloat16),
        ],
        compiler_params=pltpu.CompilerParams(vmem_limit_bytes=VMEM_BYTES),
        cost_estimate=NO_COST,
        name="mlp",
    )(place, *h_halves, *dy_halves, gu_w, down_w, *(sums or ()))


def copy_kernel(plan, place_ref, *refs):
    sems = refs[-1]
    copies = [
        pltpu.make_async_copy(source, target, sems.at[index])
        for index, (source, target) in enumerate(plan(place_ref, refs[:-1]))
    ]
    for copy in copies:
        copy.start()
    for copy in copies:
        copy.wait()


def copied(plan, count, place, operands, shapes, name):
    anywhere = pl.BlockSpec(memory_space=pl.ANY)
    return pl.pallas_call(
        functools.partial(copy_kernel, plan),
        in_specs=[pl.BlockSpec(memory_space=pltpu.SMEM)] + [anywhere] * len(operands),
        out_specs=[pl.BlockSpec(memory_space=pltpu.VMEM)] * len(shapes),
        out_shape=[jax.ShapeDtypeStruct(shape, jnp.bfloat16) for shape in shapes],
        scratch_shapes=[pltpu.SemaphoreType.DMA((count,))],
        compiler_params=pltpu.CompilerParams(vmem_limit_bytes=VMEM_BYTES),
        cost_estimate=NO_COST,
        name=name,
    )(place, *operands)


def column_moves(sources, target, groups, first, second, row, rows):
    moves, at = [], 0
    for block in (first, second):
        for group in range(groups):
            for source in sources:
                quarter = source.shape[1] // 4
                count = quarter // groups
                start = pl.multiple_of(block * quarter + group * count, math.gcd(count, quarter))
                moves.append(
                    (
                        source.at[pl.ds(row, rows), pl.ds(start, count)],
                        target.at[pl.ds(0, rows), pl.ds(at, count)],
                    )
                )
                at += count
    return moves


def shared_rows(place_ref, start, rows):
    count = rows // 4
    near_y = start + place_ref[2] * count
    near_z = start + 2 * count + place_ref[3] * count
    return pl.multiple_of(near_y, count), pl.multiple_of(near_z, count), count


def send_columns(place, weights, groups, name):
    def plan(place_ref, refs):
        x, c = place_ref[0], place_ref[1]
        sources, targets = refs[:-2], refs[-2:]
        row_y, row_z, count = shared_rows(place_ref, 0, sources[0].shape[0])
        moves = []
        for row, target in zip((row_y, row_z), targets):
            moves += column_moves(
                sources, target, groups, 2 * (1 - x) + c, 2 * x + c, row, count
            )
        return moves

    shape = (weights[0].shape[0] // 4, sum(w.shape[1] for w in weights) // 2)
    return copied(plan, 4 * groups * len(weights), place, weights, [shape] * 2, name)


def send_rows(place, weight, name):
    def plan(place_ref, refs):
        source, *targets = refs
        half = source.shape[0] // 2
        row_y, row_z, count = shared_rows(place_ref, place_ref[1] * half, half)
        return [
            (source.at[pl.ds(row, count)], target)
            for row, target in zip((row_y, row_z), targets)
        ]

    shape = (weight.shape[0] // 8, weight.shape[1])
    return copied(plan, 2, place, [weight], [shape] * 2, name)


def far_moves(place_ref, parts, target, rows):
    near_y, near_z, far_y, far_z = parts
    row_y, row_z, count = shared_rows(place_ref, rows, rows)
    other_y = pl.multiple_of(rows + (1 - place_ref[2]) * count, count)
    other_z = pl.multiple_of(rows + 2 * count + (1 - place_ref[3]) * count, count)
    return [
        (part, target.at[pl.ds(row, count)])
        for part, row in ((near_y, row_y), (near_z, row_z), (far_y, other_y), (far_z, other_z))
    ]


def join_columns(place, weights, groups, parts):
    def plan(place_ref, refs):
        x, c = place_ref[0], place_ref[1]
        sources, parts, target = refs[:-5], refs[-5:-1], refs[-1]
        rows = sources[0].shape[0]
        moves = column_moves(sources, target, groups, 2 * x + c, 2 * (1 - x) + c, 0, rows)
        return moves + far_moves(place_ref, parts, target, rows)

    shape = (2 * weights[0].shape[0], parts[0].shape[1])
    count = 2 * groups * len(weights) + 4
    return copied(plan, count, place, [*weights, *parts], [shape], "join_columns")[0]


def join_rows(place, weight, parts):
    def plan(place_ref, refs):
        source, *parts, target = refs
        rows = source.shape[0] // 2
        row = pl.multiple_of(place_ref[1] * rows, rows)
        moves = [(source.at[pl.ds(row, rows)], target.at[pl.ds(0, rows)])]
        return moves + far_moves(place_ref, parts, target, rows)

    return copied(plan, 5, place, [weight, *parts], [weight.shape], "join_rows")[0]


def swap(values, axis):
    return lax.ppermute(values, axis, [(0, 1), (1, 0)])


def rows_at(values, index, count):
    return lax.dynamic_slice_in_dim(values, index * count, count, axis=0)


def cols_at(values, index, count):
    return lax.dynamic_slice_in_dim(values, index * count, count, axis=1)


def ordered(first, mine, other, axis=0):
    return jnp.where(
        first,
        jnp.concatenate([mine, other], axis=axis),
        jnp.concatenate([other, mine], axis=axis),
    )


def hold(value, *others):
    return lax.optimization_barrier((value, *others))[0]


def mixed(parts, groups):
    pieces = []
    for group in range(groups):
        for part in parts:
            count = part.shape[1] // groups
            pieces.append(part[:, group * count : (group + 1) * count])
    return jnp.concatenate(pieces, axis=1)


def halves_swapped(values):
    mid = values.shape[1] // 2
    return jnp.concatenate([values[:, mid:], values[:, :mid]], axis=1)


def paired(
    tokens,
    positions,
    cotangent,
    norm1_gain,
    w_query,
    w_key,
    w_value,
    w_out,
    query_gain,
    key_gain,
    norm2_gain,
    w_gate,
    w_up,
    w_down,
):
    x, c, y, za = [lax.axis_index(axis) for axis in ("x", "c", "y", "za")]
    half, width = tokens.shape
    head_dim = query_gain.shape[0] * 2
    bf16, f32 = jnp.bfloat16, jnp.float32
    part, q_part = norm1_gain.shape[0], query_gain.shape[0]
    group = w_query.shape[1] // w_key.shape[1]
    head_groups = w_key.shape[1] // head_dim // 4
    unit_groups = w_gate.shape[1] // 4 // math.gcd(UNIT_BLOCK, w_gate.shape[1] // 4)

    def flip(values):
        return jnp.where(x == 0, values, halves_swapped(values))

    def both(values):
        return ordered(c == 0, values, swap(values, "c"))

    def turn(values):
        return jnp.where(x == c, values, lax.ppermute(values, ("c", "x"), [(1, 2), (2, 1)]))

    place = jnp.stack([x, c, y, za]).astype(jnp.int32)

    small = [norm1_gain, norm2_gain, query_gain, key_gain, positions]
    small = jnp.concatenate([item.astype(f32) for item in small])
    small_got = swap(small, "x")
    head_weights, unit_weights = [w_query, w_key, w_value], [w_gate, w_up]
    first = hold(place, small_got)

    def near(sent):
        return [swap(piece, "x") for piece in sent]

    def relayed(parts):
        return [*parts, swap(parts[0], "y"), swap(parts[1], "za")]

    head_sent = send_columns(first, head_weights, head_groups, "send_heads")
    head_near = near(head_sent)
    own_tokens = turn(hold(tokens, head_sent[0]))
    out_sent = send_rows(hold(place, head_sent[0]), w_out, "send_out")
    out_near = near(out_sent)
    unit_sent = send_columns(hold(place, out_sent[0]), unit_weights, unit_groups, "send_units")
    down_sent = send_rows(hold(place, unit_sent[0]), w_down, "send_down")
    unit_near = near([hold(piece, head_near[0]) for piece in unit_sent])
    down_near = near([hold(piece, head_near[1]) for piece in down_sent])
    own_cot = turn(hold(cotangent, head_near[1]))

    gains, far_gains = small[: 2 * (part + q_part)], small_got[: 2 * (part + q_part)]
    own_places, far_places = small[2 * (part + q_part) :], small_got[2 * (part + q_part) :]
    places = ordered(x == 0, own_places, far_places)
    places = jnp.where(x == c, places, swap(places, "c"))
    gain_one = jnp.concatenate([gains[:part], far_gains[:part]])[None]
    gain_two = jnp.concatenate([gains[part : 2 * part], far_gains[part : 2 * part]])[None]
    q_gain = ordered(
        x == 0, gains[2 * part : 2 * part + q_part], far_gains[2 * part : 2 * part + q_part]
    )[None]
    k_gain = ordered(x == 0, gains[2 * part + q_part :], far_gains[2 * part + q_part :])[None]
    cosine, sine = rotation_tables(places, head_dim)
    cosine = jnp.concatenate([cosine[:, 0], cosine[:, 0]], axis=-1)
    sine = jnp.concatenate([-sine[:, 0], sine[:, 0]], axis=-1)

    h_one = norm_first(place, own_tokens, swap(own_tokens, "c"), gain_one)
    qkv_w = join_columns(place, head_weights, head_groups, relayed(head_near))
    out_parts = relayed(out_near)
    out_w = join_rows(place, w_out, out_parts)
    unit_parts = relayed(unit_near)
    out_low, query_low, key_low, lse, qkv = attend(
        hold(h_one, unit_near[0], out_parts[3]), qkv_w, cosine, sine, q_gain, k_gain, group
    )
    out_low = hold(out_low, unit_near[1], down_near[0], unit_parts[2])
    down_parts = relayed(down_near)
    out_sent, out_kept = out_forward(place, out_low, out_w)
    out_got = hold(swap(out_sent, "c"), down_near[1])
    resid, h_mine = norm_second(place, own_tokens, out_kept, out_got, gain_two)
    h_mine = hold(h_mine, unit_parts[3], down_parts[2])
    h_halves = (h_mine, swap(h_mine, "c"))
    cot_halves = (own_cot, swap(own_cot, "c"))
    gu_w = join_columns(place, unit_weights, unit_groups, unit_parts)
    down_w = join_rows(place, w_down, down_parts)

    def rs(values, axis):
        index, count = lax.axis_index(axis), values.shape[0] // 2
        return rows_at(values, index, count), swap(rows_at(values, 1 - index, count), axis)

    grad_gu_far, grad_down_far, res_part, dh_part = mlp(
        place, h_halves, cot_halves, gu_w, down_w, 1
    )
    down_far_kept, down_far_got = rs(grad_down_far, "y")
    far_got = swap(grad_gu_far[part:], "x")
    grad_gu_near, grad_down_near, res_part, dh_part = mlp(
        place, h_halves, cot_halves, gu_w, down_w, 0, (res_part, dh_part)
    )
    dh_part = hold(dh_part, down_far_got)
    down_got = swap(down_far_kept + down_far_got, "x")
    down_near_kept, down_near_got = rs(grad_down_near, "y")
    near_rows = part // 2
    near_gots = [
        swap(grad_gu_near[part : part + near_rows], "x"),
        swap(grad_gu_near[part + near_rows :], "x"),
    ]

    class Piece:
        def __init__(self, kept, got, path):
            self.kept, self.got, self.path, self.back = kept, got, list(path), []

        def step(self, *others):
            got = hold(self.got, *others)
            if self.back and self.back[0] == "c":
                self.kept, self.got = ordered(c == 0, self.kept, got), None
                return self.kept
            if self.back:
                values = ordered(lax.axis_index(self.back[0]) == 0, self.kept, got)
                self.back = self.back[1:]
            else:
                values = self.kept + got
            if self.path:
                axis = self.path[0]
                self.path = self.path[1:]
                if self.path:
                    self.kept, self.got = rs(values, axis)
                    self.turned = [axis] + getattr(self, "turned", [])
                else:
                    self.kept, self.got = values, swap(values, axis)
                    self.last = True
                return self.kept
            if not self.back and getattr(self, "last", False):
                self.last = False
                self.back = self.turned + ["c"]
            self.kept, self.got = values, swap(values, self.back[0])
            return self.kept

    near_piece = Piece(grad_gu_near[:part], far_got, ("y", "za", "zb"))

    dh_got = swap(other_half(place, dh_part), "c")
    grad_resid, resid_low, gain_two_sum = norm_gradient(
        place, resid, dh_part, dh_got, own_cot, gain_two, True
    )
    resid_low = hold(resid_low, far_got)
    grad_att, grad_out = out_back(place, resid_low, swap(resid_low, "c"), out_low, out_w)
    grad_att, down_near_got, near_got = lax.optimization_barrier(
        (grad_att, down_near_got, near_gots[0])
    )
    near_got = jnp.concatenate([near_got, near_gots[1]], axis=0)
    far_piece = Piece(grad_gu_far[:part], near_got, ("y", "za", "zb"))
    mark = near_piece.step(grad_att)
    out_rows = grad_out.shape[0] // 2
    out_piece = Piece(grad_out[:out_rows], swap(grad_out[out_rows:], "x"), ("y", "za", "zb"))
    down_near_total = down_near_kept + hold(down_near_got, mark)
    down_piece = Piece(down_near_total, down_got, ("za", "zb"))
    down_piece.turned = ["y"]

    def back_of(index, dh, *others):
        grads = hold(grad_att, *others)
        return attend_back(
            query_low,
            key_low,
            qkv,
            grads,
            lse,
            cosine,
            sine,
            q_gain,
            k_gain,
            h_one,
            qkv_w,
            index,
            dh,
        )

    grad_far, head_gains_far, dh_part = back_of(1, None, down_near_total)
    grad_far, near_piece.got, near_gots[1], down_piece.got = lax.optimization_barrier(
        (grad_far, near_piece.got, near_gots[1], down_piece.got)
    )
    far_piece.got = jnp.concatenate([near_gots[0], near_gots[1]], axis=0)
    qkv_far_got = swap(grad_far[part:], "x")
    mark = far_piece.step(grad_far)
    mark = near_piece.step(mark)
    mark = down_piece.step(mark)
    grad_near, head_gains_near, dh_part = back_of(0, dh_part, mark)
    grad_near, near_piece.got, far_piece.got, down_piece.got, out_piece.got = (
        lax.optimization_barrier(
            (grad_near, near_piece.got, far_piece.got, down_piece.got, out_piece.got)
        )
    )
    qkv_near_got = swap(grad_near[part:], "x")
    qkv_near_piece = Piece(grad_near[:part], qkv_far_got, ("y", "za", "zb"))
    qkv_far_piece = Piece(grad_far[:part], qkv_near_got, ("y", "za", "zb"))

    dh_sent = other_half(place, dh_part)
    dh_got = swap(dh_sent, "c")
    mark = near_piece.step(dh_sent)
    mark = down_piece.step(mark)
    mark = far_piece.step(mark)
    mark = out_piece.step(mark)
    input_sum, gain_one_sum = norm_gradient(
        place, own_tokens, dh_part, hold(dh_got, mark), grad_resid, gain_one, False
    )
    head_gains = jnp.sum(head_gains_near, axis=0) + jnp.sum(head_gains_far, axis=0)
    gain_sums = [gain_one_sum[0], gain_two_sum[0]]
    head_sums = jnp.stack([head_gains[0], head_gains[1]])
    head_sums = jnp.where(x == 0, head_sums, jnp.roll(head_sums, q_part, axis=1))

    def gain_rows(at):
        pieces = [values[at * part : (at + 1) * part] for values in gain_sums]
        pieces += [values[at * q_part : (at + 1) * q_part] for values in head_sums]
        flat = jnp.concatenate(pieces)
        pad = -flat.shape[0] % (8 * head_dim)
        return jnp.concatenate([flat, jnp.zeros((pad,), f32)]).reshape(-1, head_dim)

    def rows_result(piece):
        return piece.step(mark).astype(f32)

    def columns_result(near, far, widths, groups):
        others = [hold(piece.got, mark) for piece in (near, far)]
        step = sum(widths)
        results, at = [], 0
        for count in widths:
            pieces = []
            for index in range(2):
                mine = jnp.where(x == index, near.kept, far.kept)
                other = jnp.where(x == index, others[0], others[1])
                for core in range(2):
                    chosen = jnp.where(c == core, mine, other)
                    for step_at in range(groups):
                        first = step_at * step + at
                        pieces.append(chosen[:, first : first + count])
            results.append(jnp.concatenate(pieces, axis=1).astype(f32))
            at += count
        return results

    gain_state = [gain_rows(0), swap(gain_rows(1), "x")]

    def gain_step(axis, *others):
        gain_state[0] = gain_state[0] + hold(gain_state[1], *others)
        if axis:
            gain_state[1] = swap(gain_state[0], axis)
        return gain_state[0]

    def result_start(*others):
        part_sum = hold(res_part, *others)
        sent = swap(other_half(place, part_sum), "c")
        total = resid + rows_at(part_sum, c, half) + sent.astype(f32)
        return total.astype(bf16)

    unit_block = w_gate.shape[1] // 4 // unit_groups
    mark = input_sum
    mark = qkv_near_piece.step(mark)
    mark = near_piece.step(mark)
    mark = out_piece.step(mark)
    mark = gain_step("y", mark)
    mark = down_piece.step(mark)
    mark = far_piece.step(mark)
    mark = qkv_near_piece.step(mark)
    mark = qkv_far_piece.step(mark)
    mark = gain_step("za", mark)
    mark = near_piece.step(mark)
    mark = out_piece.step(mark)
    grad_input = turn(hold(input_sum, mark)).astype(f32)
    mark = down_piece.step(mark)
    mark = qkv_far_piece.step(mark)
    mark = gain_step("zb", mark)
    mark = far_piece.step(mark)
    mark = near_piece.step(mark)
    mark = qkv_near_piece.step(mark)
    mark = gain_step("c", mark)
    mark = out_piece.step(mark)
    mark = down_piece.step(mark)
    mark = grad_down_w = rows_result(down_piece)
    mark = gain_step(None, mark)
    mark = qkv_far_piece.step(mark)
    mark = far_piece.step(mark)
    mark = qkv_near_piece.step(mark)
    mark = out_piece.step(mark)
    mark = far_piece.step(mark)
    result = turn(result_start(mark))
    grad_gate_w, grad_up_w = columns_result(
        near_piece, far_piece, [unit_block, unit_block], unit_groups
    )
    mark = grad_up_w
    mark = qkv_far_piece.step(mark)
    mark = out_piece.step(mark)
    mark = qkv_near_piece.step(mark)
    mark = grad_out_w = rows_result(out_piece)
    mark = qkv_far_piece.step(mark)
    mark = qkv_near_piece.step(mark)
    mark = qkv_far_piece.step(mark)
    grad_query_w, grad_key_w, grad_value_w = columns_result(
        qkv_near_piece, qkv_far_piece, [group * head_dim, head_dim, head_dim], head_groups
    )
    total_gains = gain_state[0].reshape(-1)

    return (
        result,
        grad_input,
        total_gains[:part],
        grad_query_w,
        grad_key_w,
        grad_value_w,
        grad_out_w,
        total_gains[2 * part : 2 * part + q_part],
        total_gains[2 * part + q_part : 2 * (part + q_part)],
        total_gains[part : 2 * part],
        grad_gate_w,
        grad_up_w,
        grad_down_w,
    )


def solution(mesh):
    if mesh.shape["shard"] == 2 and mesh.shape["replica"] == 16:
        names = ("zb", "za", "y", "c", "x")
        grid = Mesh(mesh.devices.reshape((2,) * len(names)), names)
        body, over, owned = paired, names, "x"
    else:
        grid, body, over, owned = mesh, local, ("replica", "shard"), "shard"
    rows, vector, matrix = P(over, None), P(owned), P(owned, None)
    return jax.shard_map(
        body,
        mesh=grid,
        in_specs=(
            rows,
            P(over),
            rows,
            vector,
            matrix,
            matrix,
            matrix,
            matrix,
            vector,
            vector,
            vector,
            matrix,
            matrix,
            matrix,
        ),
        out_specs=(
            rows,
            rows,
            vector,
            matrix,
            matrix,
            matrix,
            matrix,
            vector,
            vector,
            vector,
            matrix,
            matrix,
            matrix,
        ),
        check_vma=False,
    )
```

```python
import functools
from functools import partial
import math

import jax
import jax.numpy as jnp
from jax import lax
from jax.experimental import pallas as pl
from jax.experimental.pallas import tpu as pltpu
from jax.sharding import Mesh, PartitionSpec as P

EPS = 1e-06
THETA = 1000000.0
NEG = -1e30
QUERY_BLOCK = 256
UNIT_BLOCK = 256
VMEM_BYTES = 56 * 1024 * 1024
GAIN_ROWS = 64
ROW_BLOCK = 256


def rms_scale(values):
    return lax.rsqrt(jnp.mean(values * values, axis=-1, keepdims=True) + EPS)


def norm_back(values, gain, incoming):
    scale = rms_scale(values)
    normed = values * scale
    scaled_in = incoming * gain
    return (
        scale * (scaled_in - normed * jnp.mean(scaled_in * normed, axis=-1, keepdims=True)),
        incoming * normed,
    )


def rotation_tables(places, width):
    half_width = width // 2
    freqs = THETA ** (-jnp.arange(half_width, dtype=jnp.float32) * 2.0 / width)
    angles = places.astype(jnp.float32)[:, None, None] * freqs
    return (jnp.cos(angles), jnp.sin(angles))


def rotate(values, cosine, sine_table):
    half_width = values.shape[-1] // 2
    first_half, second_half = (values[..., :half_width], values[..., half_width:])
    return jnp.concatenate(
        [
            first_half * cosine - second_half * sine_table,
            second_half * cosine + first_half * sine_table,
        ],
        axis=-1,
    )


def unrotate(grads, cosine, sine_table):
    half_width = grads.shape[-1] // 2
    first_half, second_half = (grads[..., :half_width], grads[..., half_width:])
    return jnp.concatenate(
        [
            first_half * cosine + second_half * sine_table,
            second_half * cosine - first_half * sine_table,
        ],
        axis=-1,
    )


def inner_rows(left, right):
    return lax.dot_general(
        left, right, (((0,), (0,)), ((), ())), preferred_element_type=jnp.float32
    )


def times_t(left, right):
    return lax.dot_general(
        left, right, (((1,), (1,)), ((), ())), preferred_element_type=jnp.float32
    )


def local(
    tokens,
    positions,
    cotangent,
    norm1_gain,
    w_query,
    w_key,
    w_value,
    w_out,
    query_gain,
    key_gain,
    norm2_gain,
    w_gate,
    w_up,
    w_down,
):
    row_count = tokens.shape[0]
    blocks = lax.axis_size("shard")
    own_index = lax.axis_index("shard")
    head_dim = query_gain.shape[0] * blocks
    attn_set = (
        lax.all_gather(norm1_gain, "shard", axis=0, tiled=True),
        lax.all_gather(w_query, "shard", axis=0, tiled=True),
        lax.all_gather(w_key, "shard", axis=0, tiled=True),
        lax.all_gather(w_value, "shard", axis=0, tiled=True),
        lax.all_gather(w_out, "shard", axis=0, tiled=True),
        lax.all_gather(query_gain, "shard", axis=0, tiled=True),
        lax.all_gather(key_gain, "shard", axis=0, tiled=True),
    )
    gain_one = attn_set[0].astype(jnp.float32)
    q_gain = attn_set[5].astype(jnp.float32)
    k_gain = attn_set[6].astype(jnp.float32)
    q_heads = attn_set[1].shape[1] // head_dim
    kv_heads = attn_set[2].shape[1] // head_dim
    group = q_heads // kv_heads
    inv_scale = 1.0 / math.sqrt(head_dim)
    cosine, sine_table = rotation_tables(positions, head_dim)
    x_float = tokens.astype(jnp.float32)
    h_one = (x_float * rms_scale(x_float) * gain_one).astype(jnp.bfloat16)
    q_proj = jnp.dot(h_one, attn_set[1], preferred_element_type=jnp.float32).reshape(
        row_count, q_heads, head_dim
    )
    k_proj = jnp.dot(h_one, attn_set[2], preferred_element_type=jnp.float32).reshape(
        row_count, kv_heads, head_dim
    )
    v_low = jnp.dot(h_one, attn_set[3], preferred_element_type=jnp.float32).astype(jnp.bfloat16)
    q_low = (rotate(q_proj * rms_scale(q_proj) * q_gain, cosine, sine_table) * inv_scale).astype(
        jnp.bfloat16
    )
    q_low = q_low.reshape(row_count, kv_heads, group, head_dim)
    k_low = rotate(k_proj * rms_scale(k_proj) * k_gain, cosine, sine_table).astype(jnp.bfloat16)
    k_low = k_low.reshape(row_count, kv_heads * head_dim)
    key_full, value_full = (
        lax.all_gather(k_low, "shard", axis=0, tiled=True),
        lax.all_gather(v_low, "shard", axis=0, tiled=True),
    )
    query_place = own_index * row_count + jnp.arange(row_count)

    def block_of(full, kblock):
        return full[kblock * row_count : (kblock + 1) * row_count].reshape(
            row_count, kv_heads, head_dim
        )

    def block_scores(keys_all, kblock):
        raw = jnp.einsum(
            "sngd,tnd->ngst", q_low, block_of(keys_all, kblock), preferred_element_type=jnp.float32
        )
        key_place = kblock * row_count + jnp.arange(row_count)
        return jnp.where(key_place[None, :] <= query_place[:, None], raw, NEG)

    empty_scores = jnp.full((kv_heads, group, row_count, row_count), NEG, jnp.float32)
    zero_scores = jnp.zeros((kv_heads, group, row_count, row_count), jnp.float32)
    zero_out = jnp.zeros((row_count, kv_heads, group, head_dim), jnp.float32)
    zero_keys = jnp.zeros((row_count, kv_heads, head_dim), jnp.float32)
    score_list = [
        lax.cond(kblock <= own_index, partial(block_scores, key_full, kblock), lambda: empty_scores)
        for kblock in range(blocks)
    ]
    score_all = jnp.concatenate(score_list, axis=-1)
    peak = jnp.max(score_all, axis=-1, keepdims=True)
    log_total = peak + jnp.log(jnp.sum(jnp.exp(score_all - peak), axis=-1, keepdims=True))
    probs_low = jnp.exp(score_all - log_total).astype(jnp.bfloat16)

    def block_output(kblock):
        part_probs = probs_low[..., kblock * row_count : (kblock + 1) * row_count]
        return jnp.einsum(
            "ngst,tnd->sngd",
            part_probs,
            block_of(value_full, kblock),
            preferred_element_type=jnp.float32,
        )

    attended = zero_out
    for kblock in range(blocks):
        attended = attended + lax.cond(
            kblock <= own_index, partial(block_output, kblock), lambda: zero_out
        )
    out_low = attended.reshape(row_count, q_heads * head_dim).astype(jnp.bfloat16)
    resid_one = x_float + jnp.dot(out_low, attn_set[4], preferred_element_type=jnp.float32)
    mlp_set = (
        lax.all_gather(norm2_gain, "shard", axis=0, tiled=True),
        lax.all_gather(w_gate, "shard", axis=0, tiled=True),
        lax.all_gather(w_up, "shard", axis=0, tiled=True),
        lax.all_gather(w_down, "shard", axis=0, tiled=True),
    )
    gain_two = mlp_set[0].astype(jnp.float32)
    h_two = (resid_one * rms_scale(resid_one) * gain_two).astype(jnp.bfloat16)
    gate = jnp.dot(h_two, mlp_set[1], preferred_element_type=jnp.float32)
    up_val = jnp.dot(h_two, mlp_set[2], preferred_element_type=jnp.float32)
    sigmoid_gate = jax.nn.sigmoid(gate)
    hidden_low = (gate * sigmoid_gate * up_val).astype(jnp.bfloat16)
    result = (
        resid_one + jnp.dot(hidden_low, mlp_set[3], preferred_element_type=jnp.float32)
    ).astype(jnp.bfloat16)
    mlp_back = (
        lax.all_gather(norm2_gain, "shard", axis=0, tiled=True),
        lax.all_gather(w_gate, "shard", axis=0, tiled=True),
        lax.all_gather(w_up, "shard", axis=0, tiled=True),
        lax.all_gather(w_down, "shard", axis=0, tiled=True),
    )
    grad_hidden = times_t(cotangent, mlp_back[3])
    grad_gate_low = (
        grad_hidden * up_val * sigmoid_gate * (1.0 + gate * (1.0 - sigmoid_gate))
    ).astype(jnp.bfloat16)
    grad_up_low = (grad_hidden * gate * sigmoid_gate).astype(jnp.bfloat16)
    grad_h_two = times_t(grad_gate_low, mlp_back[1]) + times_t(grad_up_low, mlp_back[2])
    resid_part, gain_two_terms = norm_back(resid_one, gain_two, grad_h_two)
    grad_resid = cotangent.astype(jnp.float32) + resid_part
    grad_down = inner_rows(hidden_low, cotangent)
    grad_gate_w = inner_rows(h_two, grad_gate_low)
    grad_up_w = inner_rows(h_two, grad_up_low)
    mlp_shares = (
        lax.psum_scatter(
            jnp.sum(gain_two_terms, axis=0).astype(jnp.bfloat16),
            "shard",
            scatter_dimension=0,
            tiled=True,
        ).astype(jnp.float32),
        lax.psum_scatter(
            grad_gate_w.astype(jnp.bfloat16), "shard", scatter_dimension=0, tiled=True
        ).astype(jnp.float32),
        lax.psum_scatter(
            grad_up_w.astype(jnp.bfloat16), "shard", scatter_dimension=0, tiled=True
        ).astype(jnp.float32),
        lax.psum_scatter(
            grad_down.astype(jnp.bfloat16), "shard", scatter_dimension=0, tiled=True
        ).astype(jnp.float32),
    )
    attn_back = (
        lax.all_gather(norm1_gain, "shard", axis=0, tiled=True),
        lax.all_gather(w_query, "shard", axis=0, tiled=True),
        lax.all_gather(w_key, "shard", axis=0, tiled=True),
        lax.all_gather(w_value, "shard", axis=0, tiled=True),
        lax.all_gather(w_out, "shard", axis=0, tiled=True),
        lax.all_gather(query_gain, "shard", axis=0, tiled=True),
        lax.all_gather(key_gain, "shard", axis=0, tiled=True),
    )
    resid_low = grad_resid.astype(jnp.bfloat16)
    grad_att_low = (
        times_t(resid_low, attn_back[4])
        .astype(jnp.bfloat16)
        .reshape(row_count, kv_heads, group, head_dim)
    )
    key_back, value_back = (key_full, value_full)

    def first_pass(kblock):
        part_probs = jnp.exp(block_scores(key_back, kblock) - log_total)
        part_dprobs = jnp.einsum(
            "sngd,tnd->ngst",
            grad_att_low,
            block_of(value_back, kblock),
            preferred_element_type=jnp.float32,
        )
        return (part_probs, part_dprobs)

    pass_list = [
        lax.cond(
            kblock <= own_index, partial(first_pass, kblock), lambda: (zero_scores, zero_scores)
        )
        for kblock in range(blocks)
    ]
    delta_sum = jnp.zeros((kv_heads, group, row_count, 1), jnp.float32)
    for part_probs, part_dprobs in pass_list:
        delta_sum = delta_sum + jnp.sum(part_probs * part_dprobs, axis=-1, keepdims=True)

    def second_pass(kblock):
        part_probs, part_dprobs = pass_list[kblock]
        dscore_low = (part_probs * (part_dprobs - delta_sum)).astype(jnp.bfloat16)
        query_term = jnp.einsum(
            "ngst,tnd->sngd",
            dscore_low,
            block_of(key_back, kblock),
            preferred_element_type=jnp.float32,
        )
        key_term = jnp.einsum(
            "ngst,sngd->tnd", dscore_low, q_low, preferred_element_type=jnp.float32
        )
        value_term = jnp.einsum(
            "ngst,sngd->tnd",
            part_probs.astype(jnp.bfloat16),
            grad_att_low,
            preferred_element_type=jnp.float32,
        )
        return (query_term, key_term, value_term)

    grad_query = zero_out
    key_terms = []
    value_terms = []
    for kblock in range(blocks):
        query_term, key_term, value_term = lax.cond(
            kblock <= own_index,
            partial(second_pass, kblock),
            lambda: (zero_out, zero_keys, zero_keys),
        )
        grad_query = grad_query + query_term
        key_terms.append(key_term.reshape(row_count, kv_heads * head_dim))
        value_terms.append(value_term.reshape(row_count, kv_heads * head_dim))
    grad_key_local, grad_value_local = (
        lax.psum_scatter(
            jnp.concatenate(key_terms, axis=0).astype(jnp.bfloat16),
            "shard",
            scatter_dimension=0,
            tiled=True,
        ).astype(jnp.float32),
        lax.psum_scatter(
            jnp.concatenate(value_terms, axis=0).astype(jnp.bfloat16),
            "shard",
            scatter_dimension=0,
            tiled=True,
        ).astype(jnp.float32),
    )
    grad_value_low = grad_value_local.astype(jnp.bfloat16)
    key_rot = unrotate(grad_key_local.reshape(row_count, kv_heads, head_dim), cosine, sine_table)
    key_proj_grad, key_gain_terms = norm_back(k_proj, k_gain, key_rot)
    grad_key_low = key_proj_grad.reshape(row_count, kv_heads * head_dim).astype(jnp.bfloat16)
    query_rot = unrotate(
        grad_query.reshape(row_count, q_heads, head_dim) * inv_scale, cosine, sine_table
    )
    query_proj_grad, query_gain_terms = norm_back(q_proj, q_gain, query_rot)
    grad_query_low = query_proj_grad.reshape(row_count, q_heads * head_dim).astype(jnp.bfloat16)
    grad_h_one = (
        times_t(grad_query_low, attn_back[1])
        + times_t(grad_key_low, attn_back[2])
        + times_t(grad_value_low, attn_back[3])
    )
    input_part, gain_one_terms = norm_back(x_float, gain_one, grad_h_one)
    grad_input = grad_resid + input_part
    gain_one_sum = jnp.sum(gain_one_terms, axis=0)
    query_gain_sum = jnp.sum(query_gain_terms, axis=(0, 1))
    key_gain_sum = jnp.sum(key_gain_terms, axis=(0, 1))
    grad_out_w = inner_rows(out_low, resid_low)
    grad_query_w = inner_rows(h_one, grad_query_low)
    grad_key_w = inner_rows(h_one, grad_key_low)
    grad_value_w = inner_rows(h_one, grad_value_low)
    attn_shares = (
        lax.psum_scatter(
            gain_one_sum.astype(jnp.bfloat16), "shard", scatter_dimension=0, tiled=True
        ).astype(jnp.float32),
        lax.psum_scatter(
            grad_query_w.astype(jnp.bfloat16), "shard", scatter_dimension=0, tiled=True
        ).astype(jnp.float32),
        lax.psum_scatter(
            grad_key_w.astype(jnp.bfloat16), "shard", scatter_dimension=0, tiled=True
        ).astype(jnp.float32),
        lax.psum_scatter(
            grad_value_w.astype(jnp.bfloat16), "shard", scatter_dimension=0, tiled=True
        ).astype(jnp.float32),
        lax.psum_scatter(
            grad_out_w.astype(jnp.bfloat16), "shard", scatter_dimension=0, tiled=True
        ).astype(jnp.float32),
        lax.psum_scatter(
            query_gain_sum.astype(jnp.bfloat16), "shard", scatter_dimension=0, tiled=True
        ).astype(jnp.float32),
        lax.psum_scatter(
            key_gain_sum.astype(jnp.bfloat16), "shard", scatter_dimension=0, tiled=True
        ).astype(jnp.float32),
    )
    totals = (
        lax.psum(attn_shares[0].astype(jnp.bfloat16), "replica").astype(jnp.float32),
        lax.psum(attn_shares[1].astype(jnp.bfloat16), "replica").astype(jnp.float32),
        lax.psum(attn_shares[2].astype(jnp.bfloat16), "replica").astype(jnp.float32),
        lax.psum(attn_shares[3].astype(jnp.bfloat16), "replica").astype(jnp.float32),
        lax.psum(attn_shares[4].astype(jnp.bfloat16), "replica").astype(jnp.float32),
        lax.psum(attn_shares[5].astype(jnp.bfloat16), "replica").astype(jnp.float32),
        lax.psum(attn_shares[6].astype(jnp.bfloat16), "replica").astype(jnp.float32),
        lax.psum(mlp_shares[0].astype(jnp.bfloat16), "replica").astype(jnp.float32),
        lax.psum(mlp_shares[1].astype(jnp.bfloat16), "replica").astype(jnp.float32),
        lax.psum(mlp_shares[2].astype(jnp.bfloat16), "replica").astype(jnp.float32),
        lax.psum(mlp_shares[3].astype(jnp.bfloat16), "replica").astype(jnp.float32),
    )
    return (
        result,
        grad_input,
        totals[0],
        totals[1],
        totals[2],
        totals[3],
        totals[4],
        totals[5],
        totals[6],
        totals[7],
        totals[8],
        totals[9],
        totals[10],
    )
NO_COST = pl.CostEstimate(flops=0, bytes_accessed=0, transcendentals=0)


def head_norm(values, gain):
    scale = lax.rsqrt(jnp.mean(values * values, axis=-1, keepdims=True) + EPS)
    return values * scale * gain


def place_rows(place_ref, own, parts, w_ref):
    at = 0
    rows = own[0].shape[0]
    for source in own:
        w_ref[:rows, at : at + source.shape[1]] = source[...]
        at += source.shape[1]
    near_y, near_z, far_y, far_z = parts
    row_y, row_z, count = shared_rows(place_ref, rows, rows)
    other_y = pl.multiple_of(rows + (1 - place_ref[2]) * count, count)
    other_z = pl.multiple_of(rows + 2 * count + (1 - place_ref[3]) * count, count)
    for part, row in ((near_y, row_y), (near_z, row_z), (far_y, other_y), (far_z, other_z)):
        w_ref[pl.ds(row, count), :] = part[...]


def attend_kernel(
    place_ref,
    h_ref,
    wq_ref,
    wk_ref,
    wv_ref,
    near_y,
    near_z,
    far_y,
    far_z,
    cos_ref,
    sin_ref,
    qg_ref,
    kg_ref,
    o_ref,
    q_ref,
    k_ref,
    lse_ref,
    qkv_ref,
    w_ref,
):
    place_rows(place_ref, (wq_ref, wk_ref, wv_ref), (near_y, near_z, far_y, far_z), w_ref)
    qkv_ref[...] = jnp.dot(h_ref[...], w_ref[...], preferred_element_type=jnp.float32)
    span, head_dim = cos_ref.shape
    group = o_ref.shape[1] // head_dim
    block = min(QUERY_BLOCK, span)
    cosine, sine = cos_ref[...], sin_ref[...]
    key_lanes = slice(group * head_dim, (group + 1) * head_dim)
    keyed = head_norm(qkv_ref[:, key_lanes], kg_ref[...])
    key_low = (keyed * cosine + pltpu.roll(keyed, head_dim // 2, 1) * sine).astype(jnp.bfloat16)
    k_ref[...] = key_low
    value_t = qkv_ref[:, (group + 1) * head_dim :].astype(jnp.bfloat16).T
    ahead = lax.broadcasted_iota(jnp.int32, (block, block), 0) > lax.broadcasted_iota(
        jnp.int32, (block, block), 1
    )
    for head in range(group):
        lanes = slice(head * head_dim, (head + 1) * head_dim)
        asked = head_norm(qkv_ref[:, lanes], qg_ref[...])
        asked = asked * cosine + pltpu.roll(asked, head_dim // 2, 1) * sine
        query_low = (asked * (1.0 / math.sqrt(head_dim))).astype(jnp.bfloat16)
        q_ref[:, lanes] = query_low
        for start in range(0, span, block):
            stop = start + block
            scores = times_t(key_low[:stop], query_low[start:stop])
            last = jnp.where(ahead, NEG, scores[start:])
            scores = last if start == 0 else jnp.concatenate([scores[:start], last], axis=0)
            peak = jnp.max(scores, axis=0, keepdims=True)
            powers = jnp.exp(scores - peak)
            total = jnp.sum(powers, axis=0, keepdims=True)
            lse_ref[0, head : head + 1, start:stop] = peak + jnp.log(total)
            probs = (powers * (1.0 / total)).astype(jnp.bfloat16)
            out_t = jnp.dot(value_t[:, :stop], probs, preferred_element_type=jnp.float32)
            o_ref[start:stop, lanes] = out_t.T.astype(jnp.bfloat16)


def attend_back_kernel(
    q_ref,
    k_ref,
    qkv_ref,
    do_ref,
    lse_ref,
    cos_ref,
    sin_ref,
    qg_ref,
    kg_ref,
    h_ref,
    w_ref,
    *rest,
    first,
):
    dh_in = None if first else rest[0]
    kept_ref, sent_ref, gain_ref, dh_ref, own_ref, key_acc, value_acc, ht_ref = rest[
        0 if first else 1 :
    ]
    span, head_dim = cos_ref.shape
    group = q_ref.shape[1] // head_dim

    @pl.when(pl.program_id(0) == 0)
    def _():
        ht_ref[...] = h_ref[...].T
        dh_ref[...] = jnp.zeros_like(dh_ref) if first else dh_in[...]

    block = min(QUERY_BLOCK, span)
    inv_scale = 1.0 / math.sqrt(head_dim)
    key_lanes = slice(group * head_dim, (group + 1) * head_dim)
    value_lanes = slice((group + 1) * head_dim, (group + 2) * head_dim)
    key_low, value_low = k_ref[...], qkv_ref[:, value_lanes].astype(jnp.bfloat16)
    key_t = key_low.T
    ahead = lax.broadcasted_iota(jnp.int32, (block, block), 0) > lax.broadcasted_iota(
        jnp.int32, (block, block), 1
    )

    def proj_back(grads, proj, cosine, sine, gain):
        turned = grads * cosine - pltpu.roll(grads, head_dim // 2, 1) * sine
        scale = lax.rsqrt(jnp.mean(proj * proj, axis=-1, keepdims=True) + EPS)
        normed = proj * scale
        scaled = turned * gain
        back = scale * (scaled - normed * jnp.mean(scaled * normed, axis=-1, keepdims=True))
        return back, jnp.sum(turned * normed, axis=0, keepdims=True)

    key_acc[...] = jnp.zeros_like(key_acc)
    value_acc[...] = jnp.zeros_like(value_acc)
    query_gain = jnp.zeros((1, head_dim), jnp.float32)
    for head in range(group):
        lanes = slice(head * head_dim, (head + 1) * head_dim)
        for start in range(0, span, block):
            stop = start + block
            rows = slice(start, stop)
            query_low, grad_out = q_ref[rows, lanes], do_ref[rows, lanes]
            scores = times_t(key_low[:stop], query_low)
            last = jnp.where(ahead, NEG, scores[start:])
            scores = last if start == 0 else jnp.concatenate([scores[:start], last], axis=0)
            probs = jnp.exp(scores - lse_ref[0, head : head + 1, rows])
            dprobs = times_t(value_low[:stop], grad_out)
            delta = jnp.sum(probs * dprobs, axis=0, keepdims=True)
            dscore = (probs * (dprobs - delta)).astype(jnp.bfloat16)
            value_acc[:stop, :] += jnp.dot(
                probs.astype(jnp.bfloat16), grad_out, preferred_element_type=jnp.float32
            )
            key_acc[:stop, :] += jnp.dot(dscore, query_low, preferred_element_type=jnp.float32)
            grad_query = jnp.dot(key_t[:, :stop], dscore, preferred_element_type=jnp.float32).T
            back, gain_term = proj_back(
                grad_query * inv_scale,
                qkv_ref[rows, lanes],
                cos_ref[rows, :],
                sin_ref[rows, :],
                qg_ref[...],
            )
            own_ref[rows, lanes] = back.astype(jnp.bfloat16)
            query_gain = query_gain + gain_term
    back, key_gain = proj_back(
        key_acc[...], qkv_ref[:, key_lanes], cos_ref[...], sin_ref[...], kg_ref[...]
    )
    own_ref[:, key_lanes] = back.astype(jnp.bfloat16)
    own_ref[:, value_lanes] = value_acc[...].astype(jnp.bfloat16)
    gain_ref[0] = jnp.concatenate(
        [query_gain, key_gain, jnp.zeros((gain_ref.shape[1] - 2, head_dim), jnp.float32)], axis=0
    )
    grads = own_ref[...]
    product = jnp.dot(ht_ref[...], grads, preferred_element_type=jnp.float32)
    product = product.astype(jnp.bfloat16)
    kept_ref[...] = product[: kept_ref.shape[0]]
    sent_ref[...] = product[kept_ref.shape[0] :]
    dh_ref[...] += times_t(grads, w_ref[...])


def attend(place, h_one, weights, parts, cosine, sine, q_gain, k_gain, group, head_groups):
    span, head_dim = cosine.shape
    width = h_one.shape[1]
    step = (group + 2) * head_dim
    heads = parts[0].shape[1] // step
    part_rows = parts[0].shape[0]

    def own(head, place):
        block = jnp.where(head < head_groups, place[0], 1 - place[0])
        return (0, (2 * block + place[1]) * head_groups + head % head_groups)

    def column(head, place):
        return (0, head)

    def fixed(head, place):
        return (0, 0)

    rows = weights[0].shape[0]
    wide = pl.BlockSpec((span, step), column)
    q_spec = pl.BlockSpec((span, group * head_dim), column)
    k_spec = pl.BlockSpec((span, head_dim), column)
    table = pl.BlockSpec((span, head_dim), fixed)
    gain = pl.BlockSpec((1, head_dim), fixed)
    return pl.pallas_call(
        attend_kernel,
        grid_spec=pltpu.PrefetchScalarGridSpec(
            num_scalar_prefetch=1,
            grid=(heads,),
            in_specs=[
                pl.BlockSpec(h_one.shape, fixed),
                pl.BlockSpec((rows, group * head_dim), own),
                pl.BlockSpec((rows, head_dim), own),
                pl.BlockSpec((rows, head_dim), own),
            ]
            + [pl.BlockSpec((part_rows, step), column)] * 4
            + [table, table, gain, gain],
            out_specs=[
                q_spec,
                q_spec,
                k_spec,
                pl.BlockSpec((1, group, span), lambda h, place: (h, 0, 0)),
                wide,
                pl.BlockSpec((width, step), column),
            ],
        ),
        out_shape=[
            jax.ShapeDtypeStruct((span, heads * group * head_dim), jnp.bfloat16),
            jax.ShapeDtypeStruct((span, heads * group * head_dim), jnp.bfloat16),
            jax.ShapeDtypeStruct((span, heads * head_dim), jnp.bfloat16),
            jax.ShapeDtypeStruct((heads, group, span), jnp.float32),
            jax.ShapeDtypeStruct((span, heads * step), jnp.float32),
            jax.ShapeDtypeStruct((width, heads * step), jnp.bfloat16),
        ],
        compiler_params=pltpu.CompilerParams(vmem_limit_bytes=VMEM_BYTES),
        cost_estimate=NO_COST,
        name="attend",
    )(place, h_one, *weights, *parts, cosine, sine, q_gain, k_gain)


def norm_first_kernel(place_ref, mine_ref, other_ref, gain_ref, h_ref):
    x, c = place_ref[0], place_ref[1]
    half = mine_ref.shape[0]
    for source, index in ((mine_ref, c), (other_ref, 1 - c)):
        values = source[...].astype(jnp.float32)
        values = jnp.where(x == 0, values, pltpu.roll(values, values.shape[1] // 2, 1))
        normed = (values * rms_scale(values) * gain_ref[...]).astype(jnp.bfloat16)
        h_ref[pl.ds(pl.multiple_of(index * half, half), half), :] = normed


def norm_first(place, mine, other, gain):
    half, width = mine.shape
    return pl.pallas_call(
        norm_first_kernel,
        in_specs=[pl.BlockSpec(memory_space=pltpu.SMEM)]
        + [pl.BlockSpec(memory_space=pltpu.VMEM)] * 3,
        out_specs=pl.BlockSpec(memory_space=pltpu.VMEM),
        out_shape=jax.ShapeDtypeStruct((2 * half, width), jnp.bfloat16),
        compiler_params=pltpu.CompilerParams(vmem_limit_bytes=VMEM_BYTES),
        cost_estimate=NO_COST,
        name="norm_first",
    )(place, mine, other, gain)


def out_forward_kernel(place_ref, o_ref, w_ref, sent_ref, kept_ref):
    product = jnp.dot(o_ref[...], w_ref[...], preferred_element_type=jnp.float32)

    @pl.when(pl.program_id(0) == 0)
    def _():
        sent_ref[...] = product.astype(jnp.bfloat16)

    @pl.when(pl.program_id(0) == 1)
    def _():
        kept_ref[...] = product


def out_forward(place, out_low, out_w):
    half, count = out_low.shape[0] // 2, out_low.shape[1]
    width = out_w.shape[1]
    whole = pl.BlockSpec((half, width), lambda i, place: (0, 0))
    return pl.pallas_call(
        out_forward_kernel,
        grid_spec=pltpu.PrefetchScalarGridSpec(
            num_scalar_prefetch=1,
            grid=(2,),
            in_specs=[
                pl.BlockSpec(
                    (half, count), lambda i, place: (i * place[1] + (1 - i) * (1 - place[1]), 0)
                ),
                pl.BlockSpec((count, width), lambda i, place: (0, 0)),
            ],
            out_specs=[whole, whole],
        ),
        out_shape=[
            jax.ShapeDtypeStruct((half, width), jnp.bfloat16),
            jax.ShapeDtypeStruct((half, width), jnp.float32),
        ],
        compiler_params=pltpu.CompilerParams(vmem_limit_bytes=VMEM_BYTES),
        cost_estimate=NO_COST,
        name="out_forward",
    )(place, out_low, out_w)


def norm_second_kernel(place_ref, x_ref, kept_ref, got_ref, gain_ref, resid_ref, h_ref):
    resid = x_ref[...].astype(jnp.float32) + kept_ref[...] + got_ref[...].astype(jnp.float32)
    resid_ref[...] = resid
    values = jnp.where(place_ref[0] == 0, resid, pltpu.roll(resid, resid.shape[1] // 2, 1))
    h_ref[...] = (values * rms_scale(values) * gain_ref[...]).astype(jnp.bfloat16)


def norm_second(place, tokens, kept, got, gain):
    half, width = tokens.shape
    rows = min(ROW_BLOCK, half)
    spec = pl.BlockSpec((rows, width), lambda i, place: (i, 0))
    return pl.pallas_call(
        norm_second_kernel,
        grid_spec=pltpu.PrefetchScalarGridSpec(
            num_scalar_prefetch=1,
            grid=(half // rows,),
            in_specs=[spec, spec, spec, pl.BlockSpec((1, width), lambda i, place: (0, 0))],
            out_specs=[spec, spec],
        ),
        out_shape=[
            jax.ShapeDtypeStruct((half, width), jnp.float32),
            jax.ShapeDtypeStruct((half, width), jnp.bfloat16),
        ],
        compiler_params=pltpu.CompilerParams(vmem_limit_bytes=VMEM_BYTES),
        cost_estimate=NO_COST,
        name="norm_second",
    )(place, tokens, kept, got, gain)


def attend_back(
    query_low, key_low, qkv, grad_out, lse, cosine, sine, q_gain, k_gain, h_one, qkv_w, part, dh=None
):
    span, head_dim = cosine.shape
    width = h_one.shape[1]
    group = query_low.shape[1] // key_low.shape[1]
    heads = key_low.shape[1] // head_dim // 2
    base = part * heads
    step = (group + 2) * head_dim
    once = pl.Buffered(1)
    wide = pl.BlockSpec((span, step), lambda head: (0, base + head))
    q_spec = pl.BlockSpec((span, group * head_dim), lambda head: (0, base + head))
    k_spec = pl.BlockSpec((span, head_dim), lambda head: (0, base + head))
    table = pl.BlockSpec((span, head_dim), lambda head: (0, 0))
    gain = pl.BlockSpec((1, head_dim), lambda head: (0, 0))
    whole = pl.BlockSpec((span, width), lambda head: (0, 0), pipeline_mode=once)
    first = dh is None
    return pl.pallas_call(
        functools.partial(attend_back_kernel, first=first),
        grid=(heads,),
        in_specs=[
            q_spec,
            k_spec,
            wide,
            q_spec,
            pl.BlockSpec((1, group, span), lambda h: (base + h, 0, 0)),
            table,
            table,
            gain,
            gain,
            whole,
            pl.BlockSpec((width, step), lambda head: (0, base + head)),
        ]
        + ([] if first else [whole]),
        out_specs=[
            pl.BlockSpec((width // 2, step), lambda head: (0, head)),
            pl.BlockSpec((width // 2, step), lambda head: (0, head)),
            pl.BlockSpec((1, 8, head_dim), lambda h: (h, 0, 0)),
            pl.BlockSpec((span, width), lambda head: (0, 0)),
        ],
        out_shape=[
            jax.ShapeDtypeStruct((width // 2, heads * step), jnp.bfloat16),
            jax.ShapeDtypeStruct((width // 2, heads * step), jnp.bfloat16),
            jax.ShapeDtypeStruct((heads, 8, head_dim), jnp.float32),
            jax.ShapeDtypeStruct((span, width), jnp.float32),
        ],
        scratch_shapes=[
            pltpu.VMEM((span, step), jnp.bfloat16),
            pltpu.VMEM((span, head_dim), jnp.float32),
            pltpu.VMEM((span, head_dim), jnp.float32),
            pltpu.VMEM((width, span), jnp.bfloat16),
        ],
        compiler_params=pltpu.CompilerParams(vmem_limit_bytes=VMEM_BYTES),
        cost_estimate=NO_COST,
        name="attend_back",
    )(
        query_low,
        key_low,
        qkv,
        grad_out,
        lse,
        cosine,
        sine,
        q_gain,
        k_gain,
        h_one,
        qkv_w,
        *([] if first else [dh]),
    )


def norm_back_kernel(place_ref, values_ref, part_ref, got_ref, base_ref, gain_ref, *outs):
    x = place_ref[0]

    def flipped(values):
        return jnp.where(x == 0, values, pltpu.roll(values, values.shape[1] // 2, 1))

    *sums, low_ref, gain_out = outs
    values = flipped(values_ref[...].astype(jnp.float32))
    incoming = part_ref[...] + got_ref[...].astype(jnp.float32)
    back, terms = norm_back(values, gain_ref[...], incoming)
    total = base_ref[...].astype(jnp.float32) + flipped(back)
    if sums:
        sums[0][...] = total
    low_ref[...] = total.astype(jnp.bfloat16)
    summed = jnp.sum(terms, axis=0, keepdims=True)

    @pl.when(pl.program_id(0) == 0)
    def _():
        gain_out[...] = jnp.zeros_like(gain_out)

    gain_out[...] += summed


def norm_gradient(place, values, part, got, base, gain, keep):
    half, width = values.shape
    rows = min(ROW_BLOCK, half)
    steps = half // rows
    spec = pl.BlockSpec((rows, width), lambda i, place: (i, 0))
    line = pl.BlockSpec((1, width), lambda i, place: (0, 0))
    shapes = [jax.ShapeDtypeStruct((half, width), jnp.bfloat16)]
    if keep:
        shapes = [jax.ShapeDtypeStruct((half, width), jnp.float32)] + shapes
    return pl.pallas_call(
        norm_back_kernel,
        grid_spec=pltpu.PrefetchScalarGridSpec(
            num_scalar_prefetch=1,
            grid=(steps,),
            in_specs=[
                spec,
                pl.BlockSpec((rows, width), lambda i, place: (place[1] * steps + i, 0)),
                spec,
                spec,
                line,
            ],
            out_specs=[spec] * len(shapes) + [line],
        ),
        out_shape=shapes + [jax.ShapeDtypeStruct((1, width), jnp.float32)],
        compiler_params=pltpu.CompilerParams(vmem_limit_bytes=VMEM_BYTES),
        cost_estimate=NO_COST,
        name="norm_gradient",
    )(place, values, part, got, base, gain)


def whole_rows(place_ref, mine_ref, other_ref, whole_ref):
    half, c = mine_ref.shape[0], place_ref[1]
    whole_ref[pl.ds(pl.multiple_of(c * half, half), half), :] = mine_ref[...]
    whole_ref[pl.ds(pl.multiple_of((1 - c) * half, half), half), :] = other_ref[...]


def out_back_kernel(
    place_ref, mine_ref, other_ref, o_ref, w_ref, do_ref, far_ref, near_ref, dr_ref
):
    @pl.when(pl.program_id(0) == 0)
    def _():
        whole_rows(place_ref, mine_ref, other_ref, dr_ref)

    do_ref[...] = times_t(dr_ref[...], w_ref[...]).astype(jnp.bfloat16)
    product = inner_rows(o_ref[...], dr_ref[...]).astype(jnp.bfloat16)

    @pl.when(pl.program_id(0) < 2)
    def _():
        far_ref[...] = product

    @pl.when(pl.program_id(0) >= 2)
    def _():
        near_ref[...] = product


def out_back(place, mine, other, out_low, out_w):
    half, width = mine.shape
    count = out_low.shape[1]
    block = count // 4

    def at(i):
        return (i + 2) % 4

    whole = pl.BlockSpec((half, width), lambda i: (0, 0))
    return pl.pallas_call(
        out_back_kernel,
        grid=(4,),
        in_specs=[
            pl.BlockSpec(memory_space=pltpu.SMEM),
            whole,
            whole,
            pl.BlockSpec((2 * half, block), lambda i: (0, at(i))),
            pl.BlockSpec((block, width), lambda i: (at(i), 0)),
        ],
        out_specs=[
            pl.BlockSpec((2 * half, block), lambda i: (0, at(i))),
            pl.BlockSpec((block, width), lambda i: (jnp.minimum(i, 1), 0)),
            pl.BlockSpec((block, width), lambda i: (jnp.maximum(i - 2, 0), 0)),
        ],
        out_shape=[
            jax.ShapeDtypeStruct((2 * half, count), jnp.bfloat16),
            jax.ShapeDtypeStruct((count // 2, width), jnp.bfloat16),
            jax.ShapeDtypeStruct((count // 2, width), jnp.bfloat16),
        ],
        scratch_shapes=[pltpu.VMEM((2 * half, width), jnp.bfloat16)],
        compiler_params=pltpu.CompilerParams(vmem_limit_bytes=VMEM_BYTES),
        cost_estimate=NO_COST,
        name="out_back",
    )(place, mine, other, out_low, out_w)


def half_kernel(place_ref, whole_ref, half_ref):
    half_ref[...] = whole_ref[...].astype(half_ref.dtype)


def other_half(place, values):
    half, width = values.shape[0] // 2, values.shape[1]
    rows = min(ROW_BLOCK, half)
    steps = half // rows
    return pl.pallas_call(
        half_kernel,
        grid_spec=pltpu.PrefetchScalarGridSpec(
            num_scalar_prefetch=1,
            grid=(steps,),
            in_specs=[
                pl.BlockSpec((rows, width), lambda i, place: ((1 - place[1]) * steps + i, 0))
            ],
            out_specs=pl.BlockSpec((rows, width), lambda i, place: (i, 0)),
        ),
        out_shape=jax.ShapeDtypeStruct((half, width), jnp.bfloat16),
        compiler_params=pltpu.CompilerParams(vmem_limit_bytes=VMEM_BYTES),
        cost_estimate=NO_COST,
        name="other_half",
    )(place, values)


def mlp_kernel(place_ref, hm_ref, ho_ref, dm_ref, do_ref, *rest, block, first):
    gate_ref, up_ref = rest[:2]
    unit_parts, rest = rest[2:6], rest[6:]
    down_refs, rest = (rest[:4], rest[4:]) if first else (rest[:1], rest[1:])
    res_in, dh_in = (None, None) if first else rest[:2]
    kept_ref, sent_ref, gdown_ref, res_ref, dh_ref, h_ref, dy_ref, ht_ref, gu_ref, down_all = rest[
        0 if first else 2 :
    ]

    @pl.when(pl.program_id(0) == 0)
    def _():
        whole_rows(place_ref, hm_ref, ho_ref, h_ref)
        whole_rows(place_ref, dm_ref, do_ref, dy_ref)
        ht_ref[...] = h_ref[...].T
        res_ref[...] = jnp.zeros_like(res_ref) if first else res_in[...]
        dh_ref[...] = jnp.zeros_like(dh_ref) if first else dh_in[...]
        if first:
            near_y, near_z, far_y, far_z = down_refs
            row_y, row_z, count = shared_rows(place_ref, 0, down_all.shape[0])
            other_y = pl.multiple_of((1 - place_ref[2]) * count, count)
            other_z = pl.multiple_of(2 * count + (1 - place_ref[3]) * count, count)
            for part, row in (
                (near_y, row_y),
                (near_z, row_z),
                (far_y, other_y),
                (far_z, other_z),
            ):
                down_all[pl.ds(row, count), :] = part[...]

    place_rows(place_ref, (gate_ref, up_ref), unit_parts, gu_ref)
    if first:
        down_ref = down_all.at[pl.ds(pl.multiple_of(pl.program_id(0) * block, block), block), :]
    else:
        down_ref = down_refs[0]
    weights = gu_ref[...]
    both = jnp.dot(h_ref[...], weights, preferred_element_type=jnp.float32)
    gate, up_val = both[:, :block], both[:, block:]
    sigmoid_gate = jax.nn.sigmoid(gate)
    active = gate * sigmoid_gate
    grad_hidden = times_t(dy_ref[...], down_ref[...])
    hidden = (active * up_val).astype(jnp.bfloat16)
    grad_gate = (
        grad_hidden * up_val * sigmoid_gate * (1.0 + gate * (1.0 - sigmoid_gate))
    ).astype(jnp.bfloat16)
    grads = jnp.concatenate([grad_gate, (grad_hidden * active).astype(jnp.bfloat16)], axis=1)
    res_ref[...] += jnp.dot(hidden, down_ref[...], preferred_element_type=jnp.float32)
    dh_ref[...] += times_t(grads, weights)
    product = jnp.dot(ht_ref[...], grads, preferred_element_type=jnp.float32)
    product = product.astype(jnp.bfloat16)
    kept_ref[...] = product[: kept_ref.shape[0]]
    sent_ref[...] = product[kept_ref.shape[0] :]
    gdown_ref[...] = inner_rows(hidden, dy_ref[...]).astype(jnp.bfloat16)


def mlp(place, h_halves, dy_halves, unit_weights, unit_parts, w_down, down_parts, part, sums=None):
    half, width = h_halves[0].shape
    span = 2 * half
    units = w_down.shape[0] // 2
    block = math.gcd(UNIT_BLOCK, units)
    steps = units // block
    rows, part_rows = unit_weights[0].shape[0], unit_parts[0].shape[0]
    first = sums is None
    once = pl.Buffered(1)

    def fixed(j, place):
        return (0, 0)

    def own(j, place):
        index = 1 - place[0] if part else place[0]
        return (0, (2 * index + place[1]) * steps + j)

    piece = pl.BlockSpec((half, width), fixed, pipeline_mode=once)
    whole = pl.BlockSpec((span, width), fixed, pipeline_mode=once)
    total = pl.BlockSpec((span, width), fixed)
    columns = pl.BlockSpec((width // 2, 2 * block), lambda j, place: (0, j))
    if first:
        down_specs = [pl.BlockSpec(down_parts[0].shape, fixed, pipeline_mode=once)] * 4
        downs = down_parts
    else:
        down_specs = [pl.BlockSpec((block, width), lambda j, place: (place[1] * steps + j, 0))]
        downs = [w_down]
    return pl.pallas_call(
        functools.partial(mlp_kernel, block=block, first=first),
        grid_spec=pltpu.PrefetchScalarGridSpec(
            num_scalar_prefetch=1,
            grid=(steps,),
            in_specs=[
                piece,
                piece,
                piece,
                piece,
                pl.BlockSpec((rows, block), own),
                pl.BlockSpec((rows, block), own),
            ]
            + [pl.BlockSpec((part_rows, 2 * block), lambda j, place: (0, part * steps + j))] * 4
            + down_specs
            + ([] if first else [whole, whole]),
            out_specs=[
                columns,
                columns,
                pl.BlockSpec((block, width), lambda j, place: (j, 0)),
                total,
                total,
            ],
            scratch_shapes=[
                pltpu.VMEM((span, width), jnp.bfloat16),
                pltpu.VMEM((span, width), jnp.bfloat16),
                pltpu.VMEM((width, span), jnp.bfloat16),
                pltpu.VMEM((width, 2 * block), jnp.bfloat16),
                pltpu.VMEM((units if first else 16, width), jnp.bfloat16),
            ],
        ),
        out_shape=[
            jax.ShapeDtypeStruct((width // 2, 2 * units), jnp.bfloat16),
            jax.ShapeDtypeStruct((width // 2, 2 * units), jnp.bfloat16),
            jax.ShapeDtypeStruct((units, width), jnp.bfloat16),
            jax.ShapeDtypeStruct((span, width), jnp.float32),
            jax.ShapeDtypeStruct((span, width), jnp.float32),
        ],
        compiler_params=pltpu.CompilerParams(vmem_limit_bytes=VMEM_BYTES),
        cost_estimate=NO_COST,
        name="mlp",
    )(place, *h_halves, *dy_halves, *unit_weights, *unit_parts, *downs, *(sums or ()))


def split_add_kernel(place_ref, kept_ref, got_ref, keep_ref, send_ref):
    total = kept_ref[...] + got_ref[...]

    @pl.when(pl.program_id(0) == 0)
    def _():
        send_ref[...] = total

    @pl.when(pl.program_id(0) == 1)
    def _():
        keep_ref[...] = total


def split_add(place, axis, kept, got):
    rows, width = kept.shape[0] // 2, kept.shape[1]
    spec = pl.BlockSpec(
        (rows, width), lambda i, place: (i * place[axis] + (1 - i) * (1 - place[axis]), 0)
    )
    fixed = pl.BlockSpec((rows, width), lambda i, place: (0, 0))
    return pl.pallas_call(
        split_add_kernel,
        grid_spec=pltpu.PrefetchScalarGridSpec(
            num_scalar_prefetch=1,
            grid=(2,),
            in_specs=[spec, spec],
            out_specs=[fixed, fixed],
        ),
        out_shape=[jax.ShapeDtypeStruct((rows, width), kept.dtype)] * 2,
        compiler_params=pltpu.CompilerParams(vmem_limit_bytes=VMEM_BYTES),
        cost_estimate=NO_COST,
        name="split_add",
    )(place, kept, got)


def add_kernel(left_ref, right_ref, total_ref):
    total_ref[...] = left_ref[...] + right_ref[...]


def plain_add(left, right):
    rows, width = left.shape[0] // 2, left.shape[1]
    spec = pl.BlockSpec((rows, width), lambda i: (i, 0))
    return pl.pallas_call(
        add_kernel,
        grid=(2,),
        in_specs=[spec, spec],
        out_specs=spec,
        out_shape=jax.ShapeDtypeStruct(left.shape, left.dtype),
        compiler_params=pltpu.CompilerParams(vmem_limit_bytes=VMEM_BYTES),
        cost_estimate=NO_COST,
        name="plain_add",
    )(left, right)


def join_kernel(place_ref, mine_ref, other_ref, whole_ref):
    @pl.when(pl.program_id(0) == 0)
    def _():
        whole_ref[...] = mine_ref[...].astype(whole_ref.dtype)

    @pl.when(pl.program_id(0) == 1)
    def _():
        whole_ref[...] = other_ref[...].astype(whole_ref.dtype)


def join(place, axis, mine, other, dtype):
    rows, width = mine.shape
    fixed = pl.BlockSpec((rows, width), lambda i, place: (0, 0))
    return pl.pallas_call(
        join_kernel,
        grid_spec=pltpu.PrefetchScalarGridSpec(
            num_scalar_prefetch=1,
            grid=(2,),
            in_specs=[fixed, fixed],
            out_specs=pl.BlockSpec(
                (rows, width),
                lambda i, place: ((1 - i) * place[axis] + i * (1 - place[axis]), 0),
            ),
        ),
        out_shape=jax.ShapeDtypeStruct((2 * rows, width), dtype),
        compiler_params=pltpu.CompilerParams(vmem_limit_bytes=VMEM_BYTES),
        cost_estimate=NO_COST,
        name="join",
    )(place, mine, other)


def copy_kernel(plan, place_ref, *refs):
    sems = refs[-1]
    copies = [
        pltpu.make_async_copy(source, target, sems.at[index])
        for index, (source, target) in enumerate(plan(place_ref, refs[:-1]))
    ]
    for copy in copies:
        copy.start()
    for copy in copies:
        copy.wait()


def copied(plan, count, place, operands, shapes, name):
    anywhere = pl.BlockSpec(memory_space=pl.ANY)
    return pl.pallas_call(
        functools.partial(copy_kernel, plan),
        in_specs=[pl.BlockSpec(memory_space=pltpu.SMEM)] + [anywhere] * len(operands),
        out_specs=[pl.BlockSpec(memory_space=pltpu.VMEM)] * len(shapes),
        out_shape=[jax.ShapeDtypeStruct(shape, jnp.bfloat16) for shape in shapes],
        scratch_shapes=[pltpu.SemaphoreType.DMA((count,))],
        compiler_params=pltpu.CompilerParams(vmem_limit_bytes=VMEM_BYTES),
        cost_estimate=NO_COST,
        name=name,
    )(place, *operands)


def column_moves(sources, target, groups, first, second, row, rows):
    moves, at = [], 0
    for block in (first, second):
        for group in range(groups):
            for source in sources:
                quarter = source.shape[1] // 4
                count = quarter // groups
                start = pl.multiple_of(block * quarter + group * count, math.gcd(count, quarter))
                moves.append(
                    (
                        source.at[pl.ds(row, rows), pl.ds(start, count)],
                        target.at[pl.ds(0, rows), pl.ds(at, count)],
                    )
                )
                at += count
    return moves


def shared_rows(place_ref, start, rows):
    count = rows // 4
    near_y = start + place_ref[2] * count
    near_z = start + 2 * count + place_ref[3] * count
    return pl.multiple_of(near_y, count), pl.multiple_of(near_z, count), count


def send_columns(place, weights, groups, name):
    def plan(place_ref, refs):
        x, c = place_ref[0], place_ref[1]
        sources, targets = refs[:-2], refs[-2:]
        row_y, row_z, count = shared_rows(place_ref, 0, sources[0].shape[0])
        moves = []
        for row, target in zip((row_y, row_z), targets):
            moves += column_moves(
                sources, target, groups, 2 * (1 - x) + c, 2 * x + c, row, count
            )
        return moves

    shape = (weights[0].shape[0] // 4, sum(w.shape[1] for w in weights) // 2)
    return copied(plan, 4 * groups * len(weights), place, weights, [shape] * 2, name)


def send_rows(place, weight, name):
    def plan(place_ref, refs):
        source, *targets = refs
        half = source.shape[0] // 2
        row_y, row_z, count = shared_rows(place_ref, place_ref[1] * half, half)
        return [
            (source.at[pl.ds(row, count)], target)
            for row, target in zip((row_y, row_z), targets)
        ]

    shape = (weight.shape[0] // 8, weight.shape[1])
    return copied(plan, 2, place, [weight], [shape] * 2, name)


def far_moves(place_ref, parts, target, rows):
    near_y, near_z, far_y, far_z = parts
    row_y, row_z, count = shared_rows(place_ref, rows, rows)
    other_y = pl.multiple_of(rows + (1 - place_ref[2]) * count, count)
    other_z = pl.multiple_of(rows + 2 * count + (1 - place_ref[3]) * count, count)
    return [
        (part, target.at[pl.ds(row, count)])
        for part, row in ((near_y, row_y), (near_z, row_z), (far_y, other_y), (far_z, other_z))
    ]


def join_rows(place, weight, parts):
    def plan(place_ref, refs):
        source, *parts, target = refs
        rows = source.shape[0] // 2
        row = pl.multiple_of(place_ref[1] * rows, rows)
        moves = [(source.at[pl.ds(row, rows)], target.at[pl.ds(0, rows)])]
        return moves + far_moves(place_ref, parts, target, rows)

    return copied(plan, 5, place, [weight, *parts], [weight.shape], "join_rows")[0]


def swap(values, axis):
    return lax.ppermute(values, axis, [(0, 1), (1, 0)])


def rows_at(values, index, count):
    return lax.dynamic_slice_in_dim(values, index * count, count, axis=0)


def cols_at(values, index, count):
    return lax.dynamic_slice_in_dim(values, index * count, count, axis=1)


def ordered(first, mine, other, axis=0):
    return jnp.where(
        first,
        jnp.concatenate([mine, other], axis=axis),
        jnp.concatenate([other, mine], axis=axis),
    )


def hold(value, *others):
    return lax.optimization_barrier((value, *others))[0]


def mixed(parts, groups):
    pieces = []
    for group in range(groups):
        for part in parts:
            count = part.shape[1] // groups
            pieces.append(part[:, group * count : (group + 1) * count])
    return jnp.concatenate(pieces, axis=1)


def halves_swapped(values):
    mid = values.shape[1] // 2
    return jnp.concatenate([values[:, mid:], values[:, :mid]], axis=1)


def paired(
    tokens,
    positions,
    cotangent,
    norm1_gain,
    w_query,
    w_key,
    w_value,
    w_out,
    query_gain,
    key_gain,
    norm2_gain,
    w_gate,
    w_up,
    w_down,
):
    x, c, y, za = [lax.axis_index(axis) for axis in ("x", "c", "y", "za")]
    half, width = tokens.shape
    head_dim = query_gain.shape[0] * 2
    bf16, f32 = jnp.bfloat16, jnp.float32
    part, q_part = norm1_gain.shape[0], query_gain.shape[0]
    group = w_query.shape[1] // w_key.shape[1]
    head_groups = w_key.shape[1] // head_dim // 4
    unit_groups = w_gate.shape[1] // 4 // math.gcd(UNIT_BLOCK, w_gate.shape[1] // 4)

    def flip(values):
        return jnp.where(x == 0, values, halves_swapped(values))

    def turn(values):
        return jnp.where(x == c, values, lax.ppermute(values, ("c", "x"), [(1, 2), (2, 1)]))

    place = jnp.stack([x, c, y, za]).astype(jnp.int32)

    small = [norm1_gain, norm2_gain, query_gain, key_gain, positions]
    small = jnp.concatenate([item.astype(f32) for item in small])
    small_got = swap(small, "x")
    head_weights, unit_weights = [w_query, w_key, w_value], [w_gate, w_up]
    first = hold(place, small_got)

    def near(sent):
        return [swap(piece, "x") for piece in sent]

    def relayed(parts):
        return [*parts, swap(parts[0], "y"), swap(parts[1], "za")]

    head_sent = send_columns(first, head_weights, head_groups, "send_heads")
    head_near = near(head_sent)
    out_sent = send_rows(hold(place, head_sent[0]), w_out, "send_out")
    unit_sent = send_columns(hold(place, out_sent[0]), unit_weights, unit_groups, "send_units")
    down_sent = send_rows(hold(place, unit_sent[0]), w_down, "send_down")
    gains, far_gains = small[: 2 * (part + q_part)], small_got[: 2 * (part + q_part)]
    own_places, far_places = small[2 * (part + q_part) :], small_got[2 * (part + q_part) :]
    places = ordered(x == 0, own_places, far_places)
    places = jnp.where(x == c, places, swap(places, "c"))
    gain_one = jnp.concatenate([gains[:part], far_gains[:part]])[None]
    gain_two = jnp.concatenate([gains[part : 2 * part], far_gains[part : 2 * part]])[None]
    q_gain = ordered(
        x == 0, gains[2 * part : 2 * part + q_part], far_gains[2 * part : 2 * part + q_part]
    )[None]
    k_gain = ordered(x == 0, gains[2 * part + q_part :], far_gains[2 * part + q_part :])[None]
    cosine, sine = rotation_tables(places, head_dim)
    cosine = jnp.concatenate([cosine[:, 0], cosine[:, 0]], axis=-1)
    sine = jnp.concatenate([-sine[:, 0], sine[:, 0]], axis=-1)

    tokens, *head_near = lax.optimization_barrier((tokens, *head_near, down_sent[0], cosine, sine))[:3]
    own_tokens = turn(tokens)
    out_near = near([hold(piece, head_near[0]) for piece in out_sent])
    unit_near = near([hold(piece, head_near[0]) for piece in unit_sent])
    down_near = near([hold(piece, head_near[0]) for piece in down_sent])
    own_cot = turn(hold(cotangent, head_near[0]))

    head_parts = relayed(head_near)
    h_one = norm_first(place, own_tokens, swap(hold(own_tokens, *out_near, *head_parts[2:]), "c"), gain_one)
    out_parts = relayed(out_near)
    out_low, query_low, key_low, lse, qkv, qkv_w = attend(
        place,
        h_one,
        head_weights,
        head_parts,
        cosine,
        sine,
        q_gain,
        k_gain,
        group,
        head_groups,
    )
    out_low = hold(out_low, *unit_near, *down_near, *out_parts[2:])
    out_w = join_rows(place, w_out, out_parts)
    unit_parts = relayed(unit_near)
    out_sent, out_kept = out_forward(place, out_low, out_w)
    out_got = swap(out_sent, "c")
    down_parts = relayed(down_near)
    resid, h_mine = norm_second(place, own_tokens, out_kept, out_got, gain_two)
    h_mine = hold(h_mine, *unit_parts[2:], *down_parts[2:])
    h_halves = (h_mine, swap(h_mine, "c"))
    cot_halves = (own_cot, swap(own_cot, "c"))

    def rs(values, axis):
        index, count = lax.axis_index(axis), values.shape[0] // 2
        return rows_at(values, index, count), swap(rows_at(values, 1 - index, count), axis)

    far_kept, far_sent, grad_down_far, res_part, dh_part = mlp(
        place, h_halves, cot_halves, unit_weights, unit_parts, w_down, down_parts, 1
    )
    down_far_kept, down_far_got = rs(grad_down_far, "y")
    far_got = swap(far_sent, "x")
    near_kept, near_sent, grad_down_near, res_part, dh_part = mlp(
        place,
        h_halves,
        cot_halves,
        unit_weights,
        unit_parts,
        w_down,
        down_parts,
        0,
        (res_part, dh_part),
    )
    near_got = swap(near_sent, "x")
    dh_part = hold(dh_part, down_far_got)
    down_got = swap(down_far_kept + down_far_got, "x")
    down_near_kept, down_near_got = rs(grad_down_near, "y")

    class Piece:
        def __init__(self, kept, got, path):
            self.kept, self.got, self.path, self.back = kept, got, list(path), []

        def step(self, *others):
            got = hold(self.got, *others)
            if self.back and self.back[0] == "c":
                return join(place, 1, self.kept, got, f32)
            if self.back:
                values = ordered(lax.axis_index(self.back[0]) == 0, self.kept, got)
                self.back = self.back[1:]
            else:
                values = self.kept + got
            if self.path:
                axis = self.path[0]
                self.path = self.path[1:]
                if self.path:
                    self.kept, self.got = rs(values, axis)
                    self.turned = [axis] + getattr(self, "turned", [])
                else:
                    self.kept, self.got = values, swap(values, axis)
                    self.last = True
                return self.kept
            if not self.back and getattr(self, "last", False):
                self.last = False
                self.back = self.turned + ["c"]
            self.kept, self.got = values, swap(values, self.back[0])
            return self.kept

    near_piece = Piece(near_kept, far_got, ("y", "za", "zb"))

    dh_got = swap(other_half(place, dh_part), "c")
    grad_resid, resid_low, gain_two_sum = norm_gradient(
        place, resid, dh_part, dh_got, own_cot, gain_two, True
    )
    resid_low = hold(resid_low, far_got)
    grad_att, grad_out_far, grad_out_near = out_back(
        place, resid_low, swap(resid_low, "c"), out_low, out_w
    )
    out_got = swap(grad_out_far, "x")
    mark = near_piece.step(grad_att)
    far_piece = Piece(far_kept, near_got, ("za", "y", "zb"))
    out_piece = Piece(grad_out_near, out_got, ("za", "y", "zb"))

    def back_of(index, dh, *others):
        grads = hold(grad_att, *others)
        return attend_back(
            query_low,
            key_low,
            qkv,
            grads,
            lse,
            cosine,
            sine,
            q_gain,
            k_gain,
            h_one,
            qkv_w,
            index,
            dh,
        )

    far_rows, far_rows_sent, head_gains_far, dh_part = back_of(1, None, mark)
    qkv_far_got = swap(far_rows_sent, "x")
    far_rows, near_piece.got, far_piece.got, down_near_got = lax.optimization_barrier(
        (far_rows, near_piece.got, far_piece.got, down_near_got)
    )
    down_piece = Piece(down_near_kept + down_near_got, down_got, ("za", "zb"))
    down_piece.turned = ["y"]
    mark = far_piece.step(far_rows)
    mark = near_piece.step(mark)
    near_rows, near_rows_sent, head_gains_near, dh_part = back_of(0, dh_part, mark)
    qkv_near_got = swap(near_rows_sent, "x")
    dh_part, near_piece.got, far_piece.got, down_piece.got = lax.optimization_barrier(
        (dh_part, near_piece.got, far_piece.got, down_piece.got)
    )
    qkv_near_piece = Piece(near_rows, qkv_far_got, ("y", "za", "zb"))
    qkv_far_piece = Piece(far_rows, qkv_near_got, ("y", "za", "zb"))

    dh_sent = other_half(place, dh_part)
    dh_got = swap(dh_sent, "c")
    mark = down_piece.step(dh_sent)
    mark = far_piece.step(mark)
    mark = near_piece.step(mark)
    input_sum, gain_one_sum = norm_gradient(
        place, own_tokens, dh_part, hold(dh_got, mark), grad_resid, gain_one, False
    )
    head_gains = jnp.sum(head_gains_near, axis=0) + jnp.sum(head_gains_far, axis=0)
    gain_sums = [gain_one_sum[0], gain_two_sum[0]]
    head_sums = jnp.stack([head_gains[0], head_gains[1]])
    head_sums = jnp.where(x == 0, head_sums, jnp.roll(head_sums, q_part, axis=1))

    def gain_rows(at):
        pieces = [values[at * part : (at + 1) * part] for values in gain_sums]
        pieces += [values[at * q_part : (at + 1) * q_part] for values in head_sums]
        flat = jnp.concatenate(pieces)
        pad = -flat.shape[0] % (8 * head_dim)
        return jnp.concatenate([flat, jnp.zeros((pad,), f32)]).reshape(-1, head_dim)

    def rows_result(piece):
        return piece.step(mark)

    def columns_result(near, far, widths, groups):
        others = [hold(piece.got, mark) for piece in (near, far)]
        step = sum(widths)
        results, at = [], 0
        for count in widths:
            pieces = []
            for index in range(2):
                mine = jnp.where(x == index, near.kept, far.kept)
                other = jnp.where(x == index, others[0], others[1])
                for core in range(2):
                    chosen = jnp.where(c == core, mine, other)
                    for step_at in range(groups):
                        first = step_at * step + at
                        pieces.append(chosen[:, first : first + count])
            results.append(jnp.concatenate(pieces, axis=1).astype(f32))
            at += count
        return results

    gain_state = [gain_rows(0), swap(gain_rows(1), "x")]

    def gain_step(axis, *others):
        gain_state[0] = gain_state[0] + hold(gain_state[1], *others)
        if axis:
            gain_state[1] = swap(gain_state[0], axis)
        return gain_state[0]

    def result_start(*others):
        part_sum = hold(res_part, *others)
        sent = swap(other_half(place, part_sum), "c")
        total = resid + rows_at(part_sum, c, half) + sent.astype(f32)
        return total.astype(bf16)

    unit_block = w_gate.shape[1] // 4 // unit_groups
    mark = input_sum
    mark = down_piece.step(mark)
    mark = out_piece.step(mark)
    mark = far_piece.step(mark)
    mark = qkv_near_piece.step(mark)
    mark = near_piece.step(mark)
    mark = out_piece.step(mark)
    mark = gain_step("y", mark)
    input_turned = turn(hold(input_sum, mark))
    mark = down_piece.step(mark)
    mark = qkv_near_piece.step(mark)
    mark = qkv_far_piece.step(mark)
    mark = far_piece.step(mark)
    mark = out_piece.step(mark)
    mark = near_piece.step(mark)
    mark = gain_step("za", mark)
    mark = qkv_far_piece.step(mark)
    mark = qkv_near_piece.step(mark)
    mark = down_piece.step(mark)
    mark = far_piece.step(mark)
    mark = out_piece.step(mark)
    mark = grad_input = hold(input_turned, mark).astype(f32)
    mark = gain_step("zb", mark)
    mark = qkv_far_piece.step(mark)
    mark = qkv_near_piece.step(mark)
    mark = near_piece.step(mark)
    mark = far_piece.step(mark)
    mark = gain_step("c", mark)
    result_turned = turn(result_start(mark))
    mark = qkv_far_piece.step(mark)
    mark = qkv_near_piece.step(mark)
    mark = down_piece.step(mark)
    grad_gate_w, grad_up_w = columns_result(
        near_piece, far_piece, [unit_block, unit_block], unit_groups
    )
    mark = hold(grad_up_w, grad_gate_w)
    mark = out_piece.step(mark)
    mark = qkv_far_piece.step(mark)
    mark = grad_down_w = rows_result(down_piece)
    mark = result = hold(result_turned, mark)
    mark = gain_step(None, mark)
    mark = qkv_near_piece.step(mark)
    mark = out_piece.step(mark)
    mark = grad_out_w = rows_result(out_piece)
    mark = qkv_far_piece.step(mark)
    grad_query_w, grad_key_w, grad_value_w = columns_result(
        qkv_near_piece, qkv_far_piece, [group * head_dim, head_dim, head_dim], head_groups
    )
    total_gains = gain_state[0].reshape(-1)

    return (
        result,
        grad_input,
        total_gains[:part],
        grad_query_w,
        grad_key_w,
        grad_value_w,
        grad_out_w,
        total_gains[2 * part : 2 * part + q_part],
        total_gains[2 * part + q_part : 2 * (part + q_part)],
        total_gains[part : 2 * part],
        grad_gate_w,
        grad_up_w,
        grad_down_w,
    )


def solution(mesh):
    if mesh.shape["shard"] == 2 and mesh.shape["replica"] == 16:
        names = ("zb", "za", "y", "c", "x")
        grid = Mesh(mesh.devices.reshape((2,) * len(names)), names)
        body, over, owned = paired, names, "x"
    else:
        grid, body, over, owned = mesh, local, ("replica", "shard"), "shard"
    rows, vector, matrix = P(over, None), P(owned), P(owned, None)
    return jax.shard_map(
        body,
        mesh=grid,
        in_specs=(
            rows,
            P(over),
            rows,
            vector,
            matrix,
            matrix,
            matrix,
            matrix,
            vector,
            vector,
            vector,
            matrix,
            matrix,
            matrix,
        ),
        out_specs=(
            rows,
            rows,
            vector,
            matrix,
            matrix,
            matrix,
            matrix,
            vector,
            vector,
            vector,
            matrix,
            matrix,
            matrix,
        ),
        check_vma=False,
    )
```

```python
import functools
from functools import partial
import math

import jax
import jax.numpy as jnp
from jax import lax
from jax.experimental import pallas as pl
from jax.experimental.pallas import tpu as pltpu
from jax.sharding import Mesh, PartitionSpec as P

EPS = 1e-06
THETA = 1000000.0
NEG = -1e30
QUERY_BLOCK = 256
UNIT_BLOCK = 256
VMEM_BYTES = 56 * 1024 * 1024
GAIN_ROWS = 64
ROW_BLOCK = 256


def rms_scale(values):
    return lax.rsqrt(jnp.mean(values * values, axis=-1, keepdims=True) + EPS)


def norm_back(values, gain, incoming):
    scale = rms_scale(values)
    normed = values * scale
    scaled_in = incoming * gain
    return (
        scale * (scaled_in - normed * jnp.mean(scaled_in * normed, axis=-1, keepdims=True)),
        incoming * normed,
    )


def rotation_tables(places, width):
    half_width = width // 2
    freqs = THETA ** (-jnp.arange(half_width, dtype=jnp.float32) * 2.0 / width)
    angles = places.astype(jnp.float32)[:, None, None] * freqs
    return (jnp.cos(angles), jnp.sin(angles))


def rotate(values, cosine, sine_table):
    half_width = values.shape[-1] // 2
    first_half, second_half = (values[..., :half_width], values[..., half_width:])
    return jnp.concatenate(
        [
            first_half * cosine - second_half * sine_table,
            second_half * cosine + first_half * sine_table,
        ],
        axis=-1,
    )


def unrotate(grads, cosine, sine_table):
    half_width = grads.shape[-1] // 2
    first_half, second_half = (grads[..., :half_width], grads[..., half_width:])
    return jnp.concatenate(
        [
            first_half * cosine + second_half * sine_table,
            second_half * cosine - first_half * sine_table,
        ],
        axis=-1,
    )


def inner_rows(left, right):
    return lax.dot_general(
        left, right, (((0,), (0,)), ((), ())), preferred_element_type=jnp.float32
    )


def times_t(left, right):
    return lax.dot_general(
        left, right, (((1,), (1,)), ((), ())), preferred_element_type=jnp.float32
    )


def local(
    tokens,
    positions,
    cotangent,
    norm1_gain,
    w_query,
    w_key,
    w_value,
    w_out,
    query_gain,
    key_gain,
    norm2_gain,
    w_gate,
    w_up,
    w_down,
):
    row_count = tokens.shape[0]
    blocks = lax.axis_size("shard")
    own_index = lax.axis_index("shard")
    head_dim = query_gain.shape[0] * blocks
    attn_set = (
        lax.all_gather(norm1_gain, "shard", axis=0, tiled=True),
        lax.all_gather(w_query, "shard", axis=0, tiled=True),
        lax.all_gather(w_key, "shard", axis=0, tiled=True),
        lax.all_gather(w_value, "shard", axis=0, tiled=True),
        lax.all_gather(w_out, "shard", axis=0, tiled=True),
        lax.all_gather(query_gain, "shard", axis=0, tiled=True),
        lax.all_gather(key_gain, "shard", axis=0, tiled=True),
    )
    gain_one = attn_set[0].astype(jnp.float32)
    q_gain = attn_set[5].astype(jnp.float32)
    k_gain = attn_set[6].astype(jnp.float32)
    q_heads = attn_set[1].shape[1] // head_dim
    kv_heads = attn_set[2].shape[1] // head_dim
    group = q_heads // kv_heads
    inv_scale = 1.0 / math.sqrt(head_dim)
    cosine, sine_table = rotation_tables(positions, head_dim)
    x_float = tokens.astype(jnp.float32)
    h_one = (x_float * rms_scale(x_float) * gain_one).astype(jnp.bfloat16)
    q_proj = jnp.dot(h_one, attn_set[1], preferred_element_type=jnp.float32).reshape(
        row_count, q_heads, head_dim
    )
    k_proj = jnp.dot(h_one, attn_set[2], preferred_element_type=jnp.float32).reshape(
        row_count, kv_heads, head_dim
    )
    v_low = jnp.dot(h_one, attn_set[3], preferred_element_type=jnp.float32).astype(jnp.bfloat16)
    q_low = (rotate(q_proj * rms_scale(q_proj) * q_gain, cosine, sine_table) * inv_scale).astype(
        jnp.bfloat16
    )
    q_low = q_low.reshape(row_count, kv_heads, group, head_dim)
    k_low = rotate(k_proj * rms_scale(k_proj) * k_gain, cosine, sine_table).astype(jnp.bfloat16)
    k_low = k_low.reshape(row_count, kv_heads * head_dim)
    key_full, value_full = (
        lax.all_gather(k_low, "shard", axis=0, tiled=True),
        lax.all_gather(v_low, "shard", axis=0, tiled=True),
    )
    query_place = own_index * row_count + jnp.arange(row_count)

    def block_of(full, kblock):
        return full[kblock * row_count : (kblock + 1) * row_count].reshape(
            row_count, kv_heads, head_dim
        )

    def block_scores(keys_all, kblock):
        raw = jnp.einsum(
            "sngd,tnd->ngst", q_low, block_of(keys_all, kblock), preferred_element_type=jnp.float32
        )
        key_place = kblock * row_count + jnp.arange(row_count)
        return jnp.where(key_place[None, :] <= query_place[:, None], raw, NEG)

    empty_scores = jnp.full((kv_heads, group, row_count, row_count), NEG, jnp.float32)
    zero_scores = jnp.zeros((kv_heads, group, row_count, row_count), jnp.float32)
    zero_out = jnp.zeros((row_count, kv_heads, group, head_dim), jnp.float32)
    zero_keys = jnp.zeros((row_count, kv_heads, head_dim), jnp.float32)
    score_list = [
        lax.cond(kblock <= own_index, partial(block_scores, key_full, kblock), lambda: empty_scores)
        for kblock in range(blocks)
    ]
    score_all = jnp.concatenate(score_list, axis=-1)
    peak = jnp.max(score_all, axis=-1, keepdims=True)
    log_total = peak + jnp.log(jnp.sum(jnp.exp(score_all - peak), axis=-1, keepdims=True))
    probs_low = jnp.exp(score_all - log_total).astype(jnp.bfloat16)

    def block_output(kblock):
        part_probs = probs_low[..., kblock * row_count : (kblock + 1) * row_count]
        return jnp.einsum(
            "ngst,tnd->sngd",
            part_probs,
            block_of(value_full, kblock),
            preferred_element_type=jnp.float32,
        )

    attended = zero_out
    for kblock in range(blocks):
        attended = attended + lax.cond(
            kblock <= own_index, partial(block_output, kblock), lambda: zero_out
        )
    out_low = attended.reshape(row_count, q_heads * head_dim).astype(jnp.bfloat16)
    resid_one = x_float + jnp.dot(out_low, attn_set[4], preferred_element_type=jnp.float32)
    mlp_set = (
        lax.all_gather(norm2_gain, "shard", axis=0, tiled=True),
        lax.all_gather(w_gate, "shard", axis=0, tiled=True),
        lax.all_gather(w_up, "shard", axis=0, tiled=True),
        lax.all_gather(w_down, "shard", axis=0, tiled=True),
    )
    gain_two = mlp_set[0].astype(jnp.float32)
    h_two = (resid_one * rms_scale(resid_one) * gain_two).astype(jnp.bfloat16)
    gate = jnp.dot(h_two, mlp_set[1], preferred_element_type=jnp.float32)
    up_val = jnp.dot(h_two, mlp_set[2], preferred_element_type=jnp.float32)
    sigmoid_gate = jax.nn.sigmoid(gate)
    hidden_low = (gate * sigmoid_gate * up_val).astype(jnp.bfloat16)
    result = (
        resid_one + jnp.dot(hidden_low, mlp_set[3], preferred_element_type=jnp.float32)
    ).astype(jnp.bfloat16)
    mlp_back = (
        lax.all_gather(norm2_gain, "shard", axis=0, tiled=True),
        lax.all_gather(w_gate, "shard", axis=0, tiled=True),
        lax.all_gather(w_up, "shard", axis=0, tiled=True),
        lax.all_gather(w_down, "shard", axis=0, tiled=True),
    )
    grad_hidden = times_t(cotangent, mlp_back[3])
    grad_gate_low = (
        grad_hidden * up_val * sigmoid_gate * (1.0 + gate * (1.0 - sigmoid_gate))
    ).astype(jnp.bfloat16)
    grad_up_low = (grad_hidden * gate * sigmoid_gate).astype(jnp.bfloat16)
    grad_h_two = times_t(grad_gate_low, mlp_back[1]) + times_t(grad_up_low, mlp_back[2])
    resid_part, gain_two_terms = norm_back(resid_one, gain_two, grad_h_two)
    grad_resid = cotangent.astype(jnp.float32) + resid_part
    grad_down = inner_rows(hidden_low, cotangent)
    grad_gate_w = inner_rows(h_two, grad_gate_low)
    grad_up_w = inner_rows(h_two, grad_up_low)
    mlp_shares = (
        lax.psum_scatter(
            jnp.sum(gain_two_terms, axis=0).astype(jnp.bfloat16),
            "shard",
            scatter_dimension=0,
            tiled=True,
        ).astype(jnp.float32),
        lax.psum_scatter(
            grad_gate_w.astype(jnp.bfloat16), "shard", scatter_dimension=0, tiled=True
        ).astype(jnp.float32),
        lax.psum_scatter(
            grad_up_w.astype(jnp.bfloat16), "shard", scatter_dimension=0, tiled=True
        ).astype(jnp.float32),
        lax.psum_scatter(
            grad_down.astype(jnp.bfloat16), "shard", scatter_dimension=0, tiled=True
        ).astype(jnp.float32),
    )
    attn_back = (
        lax.all_gather(norm1_gain, "shard", axis=0, tiled=True),
        lax.all_gather(w_query, "shard", axis=0, tiled=True),
        lax.all_gather(w_key, "shard", axis=0, tiled=True),
        lax.all_gather(w_value, "shard", axis=0, tiled=True),
        lax.all_gather(w_out, "shard", axis=0, tiled=True),
        lax.all_gather(query_gain, "shard", axis=0, tiled=True),
        lax.all_gather(key_gain, "shard", axis=0, tiled=True),
    )
    resid_low = grad_resid.astype(jnp.bfloat16)
    grad_att_low = (
        times_t(resid_low, attn_back[4])
        .astype(jnp.bfloat16)
        .reshape(row_count, kv_heads, group, head_dim)
    )
    key_back, value_back = (key_full, value_full)

    def first_pass(kblock):
        part_probs = jnp.exp(block_scores(key_back, kblock) - log_total)
        part_dprobs = jnp.einsum(
            "sngd,tnd->ngst",
            grad_att_low,
            block_of(value_back, kblock),
            preferred_element_type=jnp.float32,
        )
        return (part_probs, part_dprobs)

    pass_list = [
        lax.cond(
            kblock <= own_index, partial(first_pass, kblock), lambda: (zero_scores, zero_scores)
        )
        for kblock in range(blocks)
    ]
    delta_sum = jnp.zeros((kv_heads, group, row_count, 1), jnp.float32)
    for part_probs, part_dprobs in pass_list:
        delta_sum = delta_sum + jnp.sum(part_probs * part_dprobs, axis=-1, keepdims=True)

    def second_pass(kblock):
        part_probs, part_dprobs = pass_list[kblock]
        dscore_low = (part_probs * (part_dprobs - delta_sum)).astype(jnp.bfloat16)
        query_term = jnp.einsum(
            "ngst,tnd->sngd",
            dscore_low,
            block_of(key_back, kblock),
            preferred_element_type=jnp.float32,
        )
        key_term = jnp.einsum(
            "ngst,sngd->tnd", dscore_low, q_low, preferred_element_type=jnp.float32
        )
        value_term = jnp.einsum(
            "ngst,sngd->tnd",
            part_probs.astype(jnp.bfloat16),
            grad_att_low,
            preferred_element_type=jnp.float32,
        )
        return (query_term, key_term, value_term)

    grad_query = zero_out
    key_terms = []
    value_terms = []
    for kblock in range(blocks):
        query_term, key_term, value_term = lax.cond(
            kblock <= own_index,
            partial(second_pass, kblock),
            lambda: (zero_out, zero_keys, zero_keys),
        )
        grad_query = grad_query + query_term
        key_terms.append(key_term.reshape(row_count, kv_heads * head_dim))
        value_terms.append(value_term.reshape(row_count, kv_heads * head_dim))
    grad_key_local, grad_value_local = (
        lax.psum_scatter(
            jnp.concatenate(key_terms, axis=0).astype(jnp.bfloat16),
            "shard",
            scatter_dimension=0,
            tiled=True,
        ).astype(jnp.float32),
        lax.psum_scatter(
            jnp.concatenate(value_terms, axis=0).astype(jnp.bfloat16),
            "shard",
            scatter_dimension=0,
            tiled=True,
        ).astype(jnp.float32),
    )
    grad_value_low = grad_value_local.astype(jnp.bfloat16)
    key_rot = unrotate(grad_key_local.reshape(row_count, kv_heads, head_dim), cosine, sine_table)
    key_proj_grad, key_gain_terms = norm_back(k_proj, k_gain, key_rot)
    grad_key_low = key_proj_grad.reshape(row_count, kv_heads * head_dim).astype(jnp.bfloat16)
    query_rot = unrotate(
        grad_query.reshape(row_count, q_heads, head_dim) * inv_scale, cosine, sine_table
    )
    query_proj_grad, query_gain_terms = norm_back(q_proj, q_gain, query_rot)
    grad_query_low = query_proj_grad.reshape(row_count, q_heads * head_dim).astype(jnp.bfloat16)
    grad_h_one = (
        times_t(grad_query_low, attn_back[1])
        + times_t(grad_key_low, attn_back[2])
        + times_t(grad_value_low, attn_back[3])
    )
    input_part, gain_one_terms = norm_back(x_float, gain_one, grad_h_one)
    grad_input = grad_resid + input_part
    gain_one_sum = jnp.sum(gain_one_terms, axis=0)
    query_gain_sum = jnp.sum(query_gain_terms, axis=(0, 1))
    key_gain_sum = jnp.sum(key_gain_terms, axis=(0, 1))
    grad_out_w = inner_rows(out_low, resid_low)
    grad_query_w = inner_rows(h_one, grad_query_low)
    grad_key_w = inner_rows(h_one, grad_key_low)
    grad_value_w = inner_rows(h_one, grad_value_low)
    attn_shares = (
        lax.psum_scatter(
            gain_one_sum.astype(jnp.bfloat16), "shard", scatter_dimension=0, tiled=True
        ).astype(jnp.float32),
        lax.psum_scatter(
            grad_query_w.astype(jnp.bfloat16), "shard", scatter_dimension=0, tiled=True
        ).astype(jnp.float32),
        lax.psum_scatter(
            grad_key_w.astype(jnp.bfloat16), "shard", scatter_dimension=0, tiled=True
        ).astype(jnp.float32),
        lax.psum_scatter(
            grad_value_w.astype(jnp.bfloat16), "shard", scatter_dimension=0, tiled=True
        ).astype(jnp.float32),
        lax.psum_scatter(
            grad_out_w.astype(jnp.bfloat16), "shard", scatter_dimension=0, tiled=True
        ).astype(jnp.float32),
        lax.psum_scatter(
            query_gain_sum.astype(jnp.bfloat16), "shard", scatter_dimension=0, tiled=True
        ).astype(jnp.float32),
        lax.psum_scatter(
            key_gain_sum.astype(jnp.bfloat16), "shard", scatter_dimension=0, tiled=True
        ).astype(jnp.float32),
    )
    totals = (
        lax.psum(attn_shares[0].astype(jnp.bfloat16), "replica").astype(jnp.float32),
        lax.psum(attn_shares[1].astype(jnp.bfloat16), "replica").astype(jnp.float32),
        lax.psum(attn_shares[2].astype(jnp.bfloat16), "replica").astype(jnp.float32),
        lax.psum(attn_shares[3].astype(jnp.bfloat16), "replica").astype(jnp.float32),
        lax.psum(attn_shares[4].astype(jnp.bfloat16), "replica").astype(jnp.float32),
        lax.psum(attn_shares[5].astype(jnp.bfloat16), "replica").astype(jnp.float32),
        lax.psum(attn_shares[6].astype(jnp.bfloat16), "replica").astype(jnp.float32),
        lax.psum(mlp_shares[0].astype(jnp.bfloat16), "replica").astype(jnp.float32),
        lax.psum(mlp_shares[1].astype(jnp.bfloat16), "replica").astype(jnp.float32),
        lax.psum(mlp_shares[2].astype(jnp.bfloat16), "replica").astype(jnp.float32),
        lax.psum(mlp_shares[3].astype(jnp.bfloat16), "replica").astype(jnp.float32),
    )
    return (
        result,
        grad_input,
        totals[0],
        totals[1],
        totals[2],
        totals[3],
        totals[4],
        totals[5],
        totals[6],
        totals[7],
        totals[8],
        totals[9],
        totals[10],
    )
NO_COST = pl.CostEstimate(flops=0, bytes_accessed=0, transcendentals=0)


def head_norm(values, gain):
    scale = lax.rsqrt(jnp.mean(values * values, axis=-1, keepdims=True) + EPS)
    return values * scale * gain


def place_rows(place_ref, own, parts, w_ref):
    at = 0
    rows = own[0].shape[0]
    for source in own:
        w_ref[:rows, at : at + source.shape[1]] = source[...]
        at += source.shape[1]
    near_y, near_z, far_y, far_z = parts
    row_y, row_z, count = shared_rows(place_ref, rows, rows)
    other_y = pl.multiple_of(rows + (1 - place_ref[2]) * count, count)
    other_z = pl.multiple_of(rows + 2 * count + (1 - place_ref[3]) * count, count)
    for part, row in ((near_y, row_y), (near_z, row_z), (far_y, other_y), (far_z, other_z)):
        w_ref[pl.ds(row, count), :] = part[...]


def attend_kernel(
    place_ref,
    h_ref,
    wq_ref,
    wk_ref,
    wv_ref,
    near_y,
    near_z,
    far_y,
    far_z,
    cos_ref,
    sin_ref,
    qg_ref,
    kg_ref,
    o_ref,
    q_ref,
    k_ref,
    lse_ref,
    qkv_ref,
    w_ref,
):
    place_rows(place_ref, (wq_ref, wk_ref, wv_ref), (near_y, near_z, far_y, far_z), w_ref)
    qkv_ref[...] = jnp.dot(h_ref[...], w_ref[...], preferred_element_type=jnp.float32)
    span, head_dim = cos_ref.shape
    group = o_ref.shape[1] // head_dim
    block = min(QUERY_BLOCK, span)
    cosine, sine = cos_ref[...], sin_ref[...]
    key_lanes = slice(group * head_dim, (group + 1) * head_dim)
    keyed = head_norm(qkv_ref[:, key_lanes], kg_ref[...])
    key_low = (keyed * cosine + pltpu.roll(keyed, head_dim // 2, 1) * sine).astype(jnp.bfloat16)
    k_ref[...] = key_low
    value_t = qkv_ref[:, (group + 1) * head_dim :].astype(jnp.bfloat16).T
    ahead = lax.broadcasted_iota(jnp.int32, (block, block), 0) > lax.broadcasted_iota(
        jnp.int32, (block, block), 1
    )
    for head in range(group):
        lanes = slice(head * head_dim, (head + 1) * head_dim)
        asked = head_norm(qkv_ref[:, lanes], qg_ref[...])
        asked = asked * cosine + pltpu.roll(asked, head_dim // 2, 1) * sine
        query_low = (asked * (1.0 / math.sqrt(head_dim))).astype(jnp.bfloat16)
        q_ref[:, lanes] = query_low
        for start in range(0, span, block):
            stop = start + block
            scores = times_t(key_low[:stop], query_low[start:stop])
            last = jnp.where(ahead, NEG, scores[start:])
            scores = last if start == 0 else jnp.concatenate([scores[:start], last], axis=0)
            peak = jnp.max(scores, axis=0, keepdims=True)
            powers = jnp.exp(scores - peak)
            total = jnp.sum(powers, axis=0, keepdims=True)
            lse_ref[0, head : head + 1, start:stop] = peak + jnp.log(total)
            probs = (powers * (1.0 / total)).astype(jnp.bfloat16)
            out_t = jnp.dot(value_t[:, :stop], probs, preferred_element_type=jnp.float32)
            o_ref[start:stop, lanes] = out_t.T.astype(jnp.bfloat16)


def attend_back_kernel(
    q_ref,
    k_ref,
    qkv_ref,
    do_ref,
    lse_ref,
    cos_ref,
    sin_ref,
    qg_ref,
    kg_ref,
    h_ref,
    w_ref,
    *rest,
    first,
):
    dh_in = None if first else rest[0]
    kept_ref, sent_ref, gain_ref, dh_ref, own_ref, key_acc, value_acc, ht_ref = rest[
        0 if first else 1 :
    ]
    span, head_dim = cos_ref.shape
    group = q_ref.shape[1] // head_dim

    @pl.when(pl.program_id(0) == 0)
    def _():
        ht_ref[...] = h_ref[...].T
        dh_ref[...] = jnp.zeros_like(dh_ref) if first else dh_in[...]

    block = min(QUERY_BLOCK, span)
    inv_scale = 1.0 / math.sqrt(head_dim)
    key_lanes = slice(group * head_dim, (group + 1) * head_dim)
    value_lanes = slice((group + 1) * head_dim, (group + 2) * head_dim)
    key_low, value_low = k_ref[...], qkv_ref[:, value_lanes].astype(jnp.bfloat16)
    key_t = key_low.T
    ahead = lax.broadcasted_iota(jnp.int32, (block, block), 0) > lax.broadcasted_iota(
        jnp.int32, (block, block), 1
    )

    def proj_back(grads, proj, cosine, sine, gain):
        turned = grads * cosine - pltpu.roll(grads, head_dim // 2, 1) * sine
        scale = lax.rsqrt(jnp.mean(proj * proj, axis=-1, keepdims=True) + EPS)
        normed = proj * scale
        scaled = turned * gain
        back = scale * (scaled - normed * jnp.mean(scaled * normed, axis=-1, keepdims=True))
        return back, jnp.sum(turned * normed, axis=0, keepdims=True)

    key_acc[...] = jnp.zeros_like(key_acc)
    value_acc[...] = jnp.zeros_like(value_acc)
    query_gain = jnp.zeros((1, head_dim), jnp.float32)
    for head in range(group):
        lanes = slice(head * head_dim, (head + 1) * head_dim)
        for start in range(0, span, block):
            stop = start + block
            rows = slice(start, stop)
            query_low, grad_out = q_ref[rows, lanes], do_ref[rows, lanes]
            scores = times_t(key_low[:stop], query_low)
            last = jnp.where(ahead, NEG, scores[start:])
            scores = last if start == 0 else jnp.concatenate([scores[:start], last], axis=0)
            probs = jnp.exp(scores - lse_ref[0, head : head + 1, rows])
            dprobs = times_t(value_low[:stop], grad_out)
            delta = jnp.sum(probs * dprobs, axis=0, keepdims=True)
            dscore = (probs * (dprobs - delta)).astype(jnp.bfloat16)
            value_acc[:stop, :] += jnp.dot(
                probs.astype(jnp.bfloat16), grad_out, preferred_element_type=jnp.float32
            )
            key_acc[:stop, :] += jnp.dot(dscore, query_low, preferred_element_type=jnp.float32)
            grad_query = jnp.dot(key_t[:, :stop], dscore, preferred_element_type=jnp.float32).T
            back, gain_term = proj_back(
                grad_query * inv_scale,
                qkv_ref[rows, lanes],
                cos_ref[rows, :],
                sin_ref[rows, :],
                qg_ref[...],
            )
            own_ref[rows, lanes] = back.astype(jnp.bfloat16)
            query_gain = query_gain + gain_term
    back, key_gain = proj_back(
        key_acc[...], qkv_ref[:, key_lanes], cos_ref[...], sin_ref[...], kg_ref[...]
    )
    own_ref[:, key_lanes] = back.astype(jnp.bfloat16)
    own_ref[:, value_lanes] = value_acc[...].astype(jnp.bfloat16)
    gain_ref[0] = jnp.concatenate(
        [query_gain, key_gain, jnp.zeros((gain_ref.shape[1] - 2, head_dim), jnp.float32)], axis=0
    )
    grads = own_ref[...]
    product = jnp.dot(ht_ref[...], grads, preferred_element_type=jnp.float32)
    product = product.astype(jnp.bfloat16)
    kept_ref[...] = product[: kept_ref.shape[0]]
    sent_ref[...] = product[kept_ref.shape[0] :]
    dh_ref[...] += times_t(grads, w_ref[...])


def attend(place, h_one, weights, parts, cosine, sine, q_gain, k_gain, group, head_groups):
    span, head_dim = cosine.shape
    width = h_one.shape[1]
    step = (group + 2) * head_dim
    heads = parts[0].shape[1] // step
    part_rows = parts[0].shape[0]

    def own(head, place):
        block = jnp.where(head < head_groups, place[0], 1 - place[0])
        return (0, (2 * block + place[1]) * head_groups + head % head_groups)

    def column(head, place):
        return (0, head)

    def fixed(head, place):
        return (0, 0)

    rows = weights[0].shape[0]
    wide = pl.BlockSpec((span, step), column)
    q_spec = pl.BlockSpec((span, group * head_dim), column)
    k_spec = pl.BlockSpec((span, head_dim), column)
    table = pl.BlockSpec((span, head_dim), fixed)
    gain = pl.BlockSpec((1, head_dim), fixed)
    return pl.pallas_call(
        attend_kernel,
        grid_spec=pltpu.PrefetchScalarGridSpec(
            num_scalar_prefetch=1,
            grid=(heads,),
            in_specs=[
                pl.BlockSpec(h_one.shape, fixed),
                pl.BlockSpec((rows, group * head_dim), own),
                pl.BlockSpec((rows, head_dim), own),
                pl.BlockSpec((rows, head_dim), own),
            ]
            + [pl.BlockSpec((part_rows, step), column)] * 4
            + [table, table, gain, gain],
            out_specs=[
                q_spec,
                q_spec,
                k_spec,
                pl.BlockSpec((1, group, span), lambda h, place: (h, 0, 0)),
                wide,
                pl.BlockSpec((width, step), column),
            ],
        ),
        out_shape=[
            jax.ShapeDtypeStruct((span, heads * group * head_dim), jnp.bfloat16),
            jax.ShapeDtypeStruct((span, heads * group * head_dim), jnp.bfloat16),
            jax.ShapeDtypeStruct((span, heads * head_dim), jnp.bfloat16),
            jax.ShapeDtypeStruct((heads, group, span), jnp.float32),
            jax.ShapeDtypeStruct((span, heads * step), jnp.float32),
            jax.ShapeDtypeStruct((width, heads * step), jnp.bfloat16),
        ],
        compiler_params=pltpu.CompilerParams(vmem_limit_bytes=VMEM_BYTES),
        cost_estimate=NO_COST,
        name="attend",
    )(place, h_one, *weights, *parts, cosine, sine, q_gain, k_gain)


def norm_first_kernel(place_ref, mine_ref, other_ref, gain_ref, h_ref):
    x, c = place_ref[0], place_ref[1]
    half = mine_ref.shape[0]
    for source, index in ((mine_ref, c), (other_ref, 1 - c)):
        values = source[...].astype(jnp.float32)
        values = jnp.where(x == 0, values, pltpu.roll(values, values.shape[1] // 2, 1))
        normed = (values * rms_scale(values) * gain_ref[...]).astype(jnp.bfloat16)
        h_ref[pl.ds(pl.multiple_of(index * half, half), half), :] = normed


def norm_first(place, mine, other, gain):
    half, width = mine.shape
    return pl.pallas_call(
        norm_first_kernel,
        in_specs=[pl.BlockSpec(memory_space=pltpu.SMEM)]
        + [pl.BlockSpec(memory_space=pltpu.VMEM)] * 3,
        out_specs=pl.BlockSpec(memory_space=pltpu.VMEM),
        out_shape=jax.ShapeDtypeStruct((2 * half, width), jnp.bfloat16),
        compiler_params=pltpu.CompilerParams(vmem_limit_bytes=VMEM_BYTES),
        cost_estimate=NO_COST,
        name="norm_first",
    )(place, mine, other, gain)


def out_forward_kernel(place_ref, o_ref, w_ref, sent_ref, kept_ref):
    product = jnp.dot(o_ref[...], w_ref[...], preferred_element_type=jnp.float32)

    @pl.when(pl.program_id(0) == 0)
    def _():
        sent_ref[...] = product.astype(jnp.bfloat16)

    @pl.when(pl.program_id(0) == 1)
    def _():
        kept_ref[...] = product


def out_forward(place, out_low, out_w):
    half, count = out_low.shape[0] // 2, out_low.shape[1]
    width = out_w.shape[1]
    whole = pl.BlockSpec((half, width), lambda i, place: (0, 0))
    return pl.pallas_call(
        out_forward_kernel,
        grid_spec=pltpu.PrefetchScalarGridSpec(
            num_scalar_prefetch=1,
            grid=(2,),
            in_specs=[
                pl.BlockSpec(
                    (half, count), lambda i, place: (i * place[1] + (1 - i) * (1 - place[1]), 0)
                ),
                pl.BlockSpec((count, width), lambda i, place: (0, 0)),
            ],
            out_specs=[whole, whole],
        ),
        out_shape=[
            jax.ShapeDtypeStruct((half, width), jnp.bfloat16),
            jax.ShapeDtypeStruct((half, width), jnp.float32),
        ],
        compiler_params=pltpu.CompilerParams(vmem_limit_bytes=VMEM_BYTES),
        cost_estimate=NO_COST,
        name="out_forward",
    )(place, out_low, out_w)


def norm_second_kernel(place_ref, x_ref, kept_ref, got_ref, gain_ref, resid_ref, h_ref):
    resid = x_ref[...].astype(jnp.float32) + kept_ref[...] + got_ref[...].astype(jnp.float32)
    resid_ref[...] = resid
    values = jnp.where(place_ref[0] == 0, resid, pltpu.roll(resid, resid.shape[1] // 2, 1))
    h_ref[...] = (values * rms_scale(values) * gain_ref[...]).astype(jnp.bfloat16)


def norm_second(place, tokens, kept, got, gain):
    half, width = tokens.shape
    rows = min(ROW_BLOCK, half)
    spec = pl.BlockSpec((rows, width), lambda i, place: (i, 0))
    return pl.pallas_call(
        norm_second_kernel,
        grid_spec=pltpu.PrefetchScalarGridSpec(
            num_scalar_prefetch=1,
            grid=(half // rows,),
            in_specs=[spec, spec, spec, pl.BlockSpec((1, width), lambda i, place: (0, 0))],
            out_specs=[spec, spec],
        ),
        out_shape=[
            jax.ShapeDtypeStruct((half, width), jnp.float32),
            jax.ShapeDtypeStruct((half, width), jnp.bfloat16),
        ],
        compiler_params=pltpu.CompilerParams(vmem_limit_bytes=VMEM_BYTES),
        cost_estimate=NO_COST,
        name="norm_second",
    )(place, tokens, kept, got, gain)


def attend_back(
    query_low, key_low, qkv, grad_out, lse, cosine, sine, q_gain, k_gain, h_one, qkv_w, part, dh=None
):
    span, head_dim = cosine.shape
    width = h_one.shape[1]
    group = query_low.shape[1] // key_low.shape[1]
    heads = key_low.shape[1] // head_dim // 2
    base = part * heads
    step = (group + 2) * head_dim
    once = pl.Buffered(1)
    wide = pl.BlockSpec((span, step), lambda head: (0, base + head))
    q_spec = pl.BlockSpec((span, group * head_dim), lambda head: (0, base + head))
    k_spec = pl.BlockSpec((span, head_dim), lambda head: (0, base + head))
    table = pl.BlockSpec((span, head_dim), lambda head: (0, 0))
    gain = pl.BlockSpec((1, head_dim), lambda head: (0, 0))
    whole = pl.BlockSpec((span, width), lambda head: (0, 0), pipeline_mode=once)
    first = dh is None
    return pl.pallas_call(
        functools.partial(attend_back_kernel, first=first),
        grid=(heads,),
        in_specs=[
            q_spec,
            k_spec,
            wide,
            q_spec,
            pl.BlockSpec((1, group, span), lambda h: (base + h, 0, 0)),
            table,
            table,
            gain,
            gain,
            whole,
            pl.BlockSpec((width, step), lambda head: (0, base + head)),
        ]
        + ([] if first else [whole]),
        out_specs=[
            pl.BlockSpec((width // 2, step), lambda head: (0, head)),
            pl.BlockSpec((width // 2, step), lambda head: (0, head)),
            pl.BlockSpec((1, 8, head_dim), lambda h: (h, 0, 0)),
            pl.BlockSpec((span, width), lambda head: (0, 0)),
        ],
        out_shape=[
            jax.ShapeDtypeStruct((width // 2, heads * step), jnp.bfloat16),
            jax.ShapeDtypeStruct((width // 2, heads * step), jnp.bfloat16),
            jax.ShapeDtypeStruct((heads, 8, head_dim), jnp.float32),
            jax.ShapeDtypeStruct((span, width), jnp.float32),
        ],
        scratch_shapes=[
            pltpu.VMEM((span, step), jnp.bfloat16),
            pltpu.VMEM((span, head_dim), jnp.float32),
            pltpu.VMEM((span, head_dim), jnp.float32),
            pltpu.VMEM((width, span), jnp.bfloat16),
        ],
        compiler_params=pltpu.CompilerParams(vmem_limit_bytes=VMEM_BYTES),
        cost_estimate=NO_COST,
        name="attend_back",
    )(
        query_low,
        key_low,
        qkv,
        grad_out,
        lse,
        cosine,
        sine,
        q_gain,
        k_gain,
        h_one,
        qkv_w,
        *([] if first else [dh]),
    )


def norm_back_kernel(place_ref, values_ref, part_ref, got_ref, base_ref, gain_ref, *outs):
    x = place_ref[0]

    def flipped(values):
        return jnp.where(x == 0, values, pltpu.roll(values, values.shape[1] // 2, 1))

    *sums, low_ref, gain_out = outs
    values = flipped(values_ref[...].astype(jnp.float32))
    incoming = part_ref[...] + got_ref[...].astype(jnp.float32)
    back, terms = norm_back(values, gain_ref[...], incoming)
    total = base_ref[...].astype(jnp.float32) + flipped(back)
    if sums:
        sums[0][...] = total
    low_ref[...] = total.astype(jnp.bfloat16)
    summed = jnp.sum(terms, axis=0, keepdims=True)

    @pl.when(pl.program_id(0) == 0)
    def _():
        gain_out[...] = jnp.zeros_like(gain_out)

    gain_out[...] += summed


def norm_gradient(place, values, part, got, base, gain, keep):
    half, width = values.shape
    rows = min(ROW_BLOCK, half)
    steps = half // rows
    spec = pl.BlockSpec((rows, width), lambda i, place: (i, 0))
    line = pl.BlockSpec((1, width), lambda i, place: (0, 0))
    shapes = [jax.ShapeDtypeStruct((half, width), jnp.bfloat16)]
    if keep:
        shapes = [jax.ShapeDtypeStruct((half, width), jnp.float32)] + shapes
    return pl.pallas_call(
        norm_back_kernel,
        grid_spec=pltpu.PrefetchScalarGridSpec(
            num_scalar_prefetch=1,
            grid=(steps,),
            in_specs=[
                spec,
                pl.BlockSpec((rows, width), lambda i, place: (place[1] * steps + i, 0)),
                spec,
                spec,
                line,
            ],
            out_specs=[spec] * len(shapes) + [line],
        ),
        out_shape=shapes + [jax.ShapeDtypeStruct((1, width), jnp.float32)],
        compiler_params=pltpu.CompilerParams(vmem_limit_bytes=VMEM_BYTES),
        cost_estimate=NO_COST,
        name="norm_gradient",
    )(place, values, part, got, base, gain)


def whole_rows(place_ref, mine_ref, other_ref, whole_ref):
    half, c = mine_ref.shape[0], place_ref[1]
    whole_ref[pl.ds(pl.multiple_of(c * half, half), half), :] = mine_ref[...]
    whole_ref[pl.ds(pl.multiple_of((1 - c) * half, half), half), :] = other_ref[...]


def out_back_kernel(
    place_ref, mine_ref, other_ref, o_ref, w_ref, do_ref, far_ref, near_ref, dr_ref
):
    @pl.when(pl.program_id(0) == 0)
    def _():
        whole_rows(place_ref, mine_ref, other_ref, dr_ref)

    do_ref[...] = times_t(dr_ref[...], w_ref[...]).astype(jnp.bfloat16)
    product = inner_rows(o_ref[...], dr_ref[...]).astype(jnp.bfloat16)

    @pl.when(pl.program_id(0) < 2)
    def _():
        far_ref[...] = product

    @pl.when(pl.program_id(0) >= 2)
    def _():
        near_ref[...] = product


def out_back(place, mine, other, out_low, out_w):
    half, width = mine.shape
    count = out_low.shape[1]
    block = count // 4

    def at(i):
        return (i + 2) % 4

    whole = pl.BlockSpec((half, width), lambda i: (0, 0))
    return pl.pallas_call(
        out_back_kernel,
        grid=(4,),
        in_specs=[
            pl.BlockSpec(memory_space=pltpu.SMEM),
            whole,
            whole,
            pl.BlockSpec((2 * half, block), lambda i: (0, at(i))),
            pl.BlockSpec((block, width), lambda i: (at(i), 0)),
        ],
        out_specs=[
            pl.BlockSpec((2 * half, block), lambda i: (0, at(i))),
            pl.BlockSpec((block, width), lambda i: (jnp.minimum(i, 1), 0)),
            pl.BlockSpec((block, width), lambda i: (jnp.maximum(i - 2, 0), 0)),
        ],
        out_shape=[
            jax.ShapeDtypeStruct((2 * half, count), jnp.bfloat16),
            jax.ShapeDtypeStruct((count // 2, width), jnp.bfloat16),
            jax.ShapeDtypeStruct((count // 2, width), jnp.bfloat16),
        ],
        scratch_shapes=[pltpu.VMEM((2 * half, width), jnp.bfloat16)],
        compiler_params=pltpu.CompilerParams(vmem_limit_bytes=VMEM_BYTES),
        cost_estimate=NO_COST,
        name="out_back",
    )(place, mine, other, out_low, out_w)


def half_kernel(place_ref, whole_ref, half_ref):
    half_ref[...] = whole_ref[...].astype(half_ref.dtype)


def other_half(place, values):
    half, width = values.shape[0] // 2, values.shape[1]
    rows = min(ROW_BLOCK, half)
    steps = half // rows
    return pl.pallas_call(
        half_kernel,
        grid_spec=pltpu.PrefetchScalarGridSpec(
            num_scalar_prefetch=1,
            grid=(steps,),
            in_specs=[
                pl.BlockSpec((rows, width), lambda i, place: ((1 - place[1]) * steps + i, 0))
            ],
            out_specs=pl.BlockSpec((rows, width), lambda i, place: (i, 0)),
        ),
        out_shape=jax.ShapeDtypeStruct((half, width), jnp.bfloat16),
        compiler_params=pltpu.CompilerParams(vmem_limit_bytes=VMEM_BYTES),
        cost_estimate=NO_COST,
        name="other_half",
    )(place, values)


def mlp_kernel(place_ref, hm_ref, ho_ref, dm_ref, do_ref, *rest, block, first):
    gate_ref, up_ref = rest[:2]
    unit_parts, rest = rest[2:6], rest[6:]
    down_refs, rest = (rest[:4], rest[4:]) if first else (rest[:1], rest[1:])
    res_in, dh_in = (None, None) if first else rest[:2]
    kept_ref, sent_ref, gdown_ref, res_ref, dh_ref, h_ref, dy_ref, ht_ref, gu_ref, down_all = rest[
        0 if first else 2 :
    ]

    @pl.when(pl.program_id(0) == 0)
    def _():
        whole_rows(place_ref, hm_ref, ho_ref, h_ref)
        whole_rows(place_ref, dm_ref, do_ref, dy_ref)
        ht_ref[...] = h_ref[...].T
        res_ref[...] = jnp.zeros_like(res_ref) if first else res_in[...]
        dh_ref[...] = jnp.zeros_like(dh_ref) if first else dh_in[...]
        if first:
            near_y, near_z, far_y, far_z = down_refs
            row_y, row_z, count = shared_rows(place_ref, 0, down_all.shape[0])
            other_y = pl.multiple_of((1 - place_ref[2]) * count, count)
            other_z = pl.multiple_of(2 * count + (1 - place_ref[3]) * count, count)
            for part, row in (
                (near_y, row_y),
                (near_z, row_z),
                (far_y, other_y),
                (far_z, other_z),
            ):
                down_all[pl.ds(row, count), :] = part[...]

    place_rows(place_ref, (gate_ref, up_ref), unit_parts, gu_ref)
    if first:
        down_ref = down_all.at[pl.ds(pl.multiple_of(pl.program_id(0) * block, block), block), :]
    else:
        down_ref = down_refs[0]
    weights = gu_ref[...]
    both = jnp.dot(h_ref[...], weights, preferred_element_type=jnp.float32)
    gate, up_val = both[:, :block], both[:, block:]
    sigmoid_gate = jax.nn.sigmoid(gate)
    active = gate * sigmoid_gate
    grad_hidden = times_t(dy_ref[...], down_ref[...])
    hidden = (active * up_val).astype(jnp.bfloat16)
    grad_gate = (
        grad_hidden * up_val * sigmoid_gate * (1.0 + gate * (1.0 - sigmoid_gate))
    ).astype(jnp.bfloat16)
    grads = jnp.concatenate([grad_gate, (grad_hidden * active).astype(jnp.bfloat16)], axis=1)
    res_ref[...] += jnp.dot(hidden, down_ref[...], preferred_element_type=jnp.float32)
    dh_ref[...] += times_t(grads, weights)
    product = jnp.dot(ht_ref[...], grads, preferred_element_type=jnp.float32)
    product = product.astype(jnp.bfloat16)
    kept_ref[...] = product[: kept_ref.shape[0]]
    sent_ref[...] = product[kept_ref.shape[0] :]
    gdown_ref[...] = inner_rows(hidden, dy_ref[...]).astype(jnp.bfloat16)


def mlp(place, h_halves, dy_halves, unit_weights, unit_parts, w_down, down_parts, part, sums=None):
    half, width = h_halves[0].shape
    span = 2 * half
    units = w_down.shape[0] // 2
    block = math.gcd(UNIT_BLOCK, units)
    steps = units // block
    rows, part_rows = unit_weights[0].shape[0], unit_parts[0].shape[0]
    first = sums is None
    once = pl.Buffered(1)

    def fixed(j, place):
        return (0, 0)

    def own(j, place):
        index = 1 - place[0] if part else place[0]
        return (0, (2 * index + place[1]) * steps + j)

    piece = pl.BlockSpec((half, width), fixed, pipeline_mode=once)
    whole = pl.BlockSpec((span, width), fixed, pipeline_mode=once)
    total = pl.BlockSpec((span, width), fixed)
    columns = pl.BlockSpec((width // 2, 2 * block), lambda j, place: (0, j))
    if first:
        down_specs = [pl.BlockSpec(down_parts[0].shape, fixed, pipeline_mode=once)] * 4
        downs = down_parts
    else:
        down_specs = [pl.BlockSpec((block, width), lambda j, place: (place[1] * steps + j, 0))]
        downs = [w_down]
    return pl.pallas_call(
        functools.partial(mlp_kernel, block=block, first=first),
        grid_spec=pltpu.PrefetchScalarGridSpec(
            num_scalar_prefetch=1,
            grid=(steps,),
            in_specs=[
                piece,
                piece,
                piece,
                piece,
                pl.BlockSpec((rows, block), own),
                pl.BlockSpec((rows, block), own),
            ]
            + [pl.BlockSpec((part_rows, 2 * block), lambda j, place: (0, part * steps + j))] * 4
            + down_specs
            + ([] if first else [whole, whole]),
            out_specs=[
                columns,
                columns,
                pl.BlockSpec((block, width), lambda j, place: (j, 0)),
                total,
                total,
            ],
            scratch_shapes=[
                pltpu.VMEM((span, width), jnp.bfloat16),
                pltpu.VMEM((span, width), jnp.bfloat16),
                pltpu.VMEM((width, span), jnp.bfloat16),
                pltpu.VMEM((width, 2 * block), jnp.bfloat16),
                pltpu.VMEM((units if first else 16, width), jnp.bfloat16),
            ],
        ),
        out_shape=[
            jax.ShapeDtypeStruct((width // 2, 2 * units), jnp.bfloat16),
            jax.ShapeDtypeStruct((width // 2, 2 * units), jnp.bfloat16),
            jax.ShapeDtypeStruct((units, width), jnp.bfloat16),
            jax.ShapeDtypeStruct((span, width), jnp.float32),
            jax.ShapeDtypeStruct((span, width), jnp.float32),
        ],
        compiler_params=pltpu.CompilerParams(vmem_limit_bytes=VMEM_BYTES),
        cost_estimate=NO_COST,
        name="mlp",
    )(place, *h_halves, *dy_halves, *unit_weights, *unit_parts, *downs, *(sums or ()))


def split_add_kernel(place_ref, kept_ref, got_ref, keep_ref, send_ref):
    total = kept_ref[...] + got_ref[...]

    @pl.when(pl.program_id(0) == 0)
    def _():
        send_ref[...] = total

    @pl.when(pl.program_id(0) == 1)
    def _():
        keep_ref[...] = total


def split_add(place, axis, kept, got):
    rows, width = kept.shape[0] // 2, kept.shape[1]
    spec = pl.BlockSpec(
        (rows, width), lambda i, place: (i * place[axis] + (1 - i) * (1 - place[axis]), 0)
    )
    fixed = pl.BlockSpec((rows, width), lambda i, place: (0, 0))
    return pl.pallas_call(
        split_add_kernel,
        grid_spec=pltpu.PrefetchScalarGridSpec(
            num_scalar_prefetch=1,
            grid=(2,),
            in_specs=[spec, spec],
            out_specs=[fixed, fixed],
        ),
        out_shape=[jax.ShapeDtypeStruct((rows, width), kept.dtype)] * 2,
        compiler_params=pltpu.CompilerParams(vmem_limit_bytes=VMEM_BYTES),
        cost_estimate=NO_COST,
        name="split_add",
    )(place, kept, got)


def add_kernel(left_ref, right_ref, total_ref):
    total_ref[...] = left_ref[...] + right_ref[...]


def plain_add(left, right):
    rows, width = left.shape[0] // 2, left.shape[1]
    spec = pl.BlockSpec((rows, width), lambda i: (i, 0))
    return pl.pallas_call(
        add_kernel,
        grid=(2,),
        in_specs=[spec, spec],
        out_specs=spec,
        out_shape=jax.ShapeDtypeStruct(left.shape, left.dtype),
        compiler_params=pltpu.CompilerParams(vmem_limit_bytes=VMEM_BYTES),
        cost_estimate=NO_COST,
        name="plain_add",
    )(left, right)


def join_kernel(place_ref, mine_ref, other_ref, whole_ref):
    @pl.when(pl.program_id(0) == 0)
    def _():
        whole_ref[...] = mine_ref[...].astype(whole_ref.dtype)

    @pl.when(pl.program_id(0) == 1)
    def _():
        whole_ref[...] = other_ref[...].astype(whole_ref.dtype)


def join(place, axis, mine, other, dtype):
    rows, width = mine.shape
    fixed = pl.BlockSpec((rows, width), lambda i, place: (0, 0))
    return pl.pallas_call(
        join_kernel,
        grid_spec=pltpu.PrefetchScalarGridSpec(
            num_scalar_prefetch=1,
            grid=(2,),
            in_specs=[fixed, fixed],
            out_specs=pl.BlockSpec(
                (rows, width),
                lambda i, place: ((1 - i) * place[axis] + i * (1 - place[axis]), 0),
            ),
        ),
        out_shape=jax.ShapeDtypeStruct((2 * rows, width), dtype),
        compiler_params=pltpu.CompilerParams(vmem_limit_bytes=VMEM_BYTES),
        cost_estimate=NO_COST,
        name="join",
    )(place, mine, other)


def unmix_kernel(widths, groups, place_ref, *refs):
    x, c = place_ref[0], place_ref[1]
    sources, outs = refs[:4], refs[4:]
    at = pl.program_id(0)
    block, core, group = at // (2 * groups), at // groups % 2, at % groups
    chosen = jnp.where(block == x, 0, 1) + jnp.where(core == c, 0, 2)
    step = sum(widths)
    for index, source in enumerate(sources):

        @pl.when(chosen == index)
        def _(source=source):
            first = 0
            for out, count in zip(outs, widths):
                start = pl.multiple_of(group * step + first, math.gcd(step, count))
                out[...] = source[:, pl.ds(start, count)].astype(jnp.float32)
                first += count


def unmix(place, near, far, near_other, far_other, widths, groups):
    rows = near.shape[0]
    whole = pl.BlockSpec(near.shape, lambda i, place: (0, 0), pipeline_mode=pl.Buffered(1))
    return pl.pallas_call(
        functools.partial(unmix_kernel, widths, groups),
        grid_spec=pltpu.PrefetchScalarGridSpec(
            num_scalar_prefetch=1,
            grid=(4 * groups,),
            in_specs=[whole] * 4,
            out_specs=[pl.BlockSpec((rows, count), lambda i, place: (0, i)) for count in widths],
        ),
        out_shape=[
            jax.ShapeDtypeStruct((rows, 4 * groups * count), jnp.float32) for count in widths
        ],
        compiler_params=pltpu.CompilerParams(vmem_limit_bytes=VMEM_BYTES),
        cost_estimate=NO_COST,
        name="unmix",
    )(place, near, far, near_other, far_other)


def copy_kernel(plan, place_ref, *refs):
    sems = refs[-1]
    copies = [
        pltpu.make_async_copy(source, target, sems.at[index])
        for index, (source, target) in enumerate(plan(place_ref, refs[:-1]))
    ]
    for copy in copies:
        copy.start()
    for copy in copies:
        copy.wait()


def copied(plan, count, place, operands, shapes, name):
    anywhere = pl.BlockSpec(memory_space=pl.ANY)
    return pl.pallas_call(
        functools.partial(copy_kernel, plan),
        in_specs=[pl.BlockSpec(memory_space=pltpu.SMEM)] + [anywhere] * len(operands),
        out_specs=[pl.BlockSpec(memory_space=pltpu.VMEM)] * len(shapes),
        out_shape=[jax.ShapeDtypeStruct(shape, jnp.bfloat16) for shape in shapes],
        scratch_shapes=[pltpu.SemaphoreType.DMA((count,))],
        compiler_params=pltpu.CompilerParams(vmem_limit_bytes=VMEM_BYTES),
        cost_estimate=NO_COST,
        name=name,
    )(place, *operands)


def column_moves(sources, target, groups, first, second, row, rows):
    moves, at = [], 0
    for block in (first, second):
        for group in range(groups):
            for source in sources:
                quarter = source.shape[1] // 4
                count = quarter // groups
                start = pl.multiple_of(block * quarter + group * count, math.gcd(count, quarter))
                moves.append(
                    (
                        source.at[pl.ds(row, rows), pl.ds(start, count)],
                        target.at[pl.ds(0, rows), pl.ds(at, count)],
                    )
                )
                at += count
    return moves


def shared_rows(place_ref, start, rows):
    count = rows // 4
    near_y = start + place_ref[2] * count
    near_z = start + 2 * count + place_ref[3] * count
    return pl.multiple_of(near_y, count), pl.multiple_of(near_z, count), count


def send_columns(place, weights, groups, name):
    def plan(place_ref, refs):
        x, c = place_ref[0], place_ref[1]
        sources, targets = refs[:-2], refs[-2:]
        row_y, row_z, count = shared_rows(place_ref, 0, sources[0].shape[0])
        moves = []
        for row, target in zip((row_y, row_z), targets):
            moves += column_moves(
                sources, target, groups, 2 * (1 - x) + c, 2 * x + c, row, count
            )
        return moves

    shape = (weights[0].shape[0] // 4, sum(w.shape[1] for w in weights) // 2)
    return copied(plan, 4 * groups * len(weights), place, weights, [shape] * 2, name)


def send_rows(place, weight, name):
    def plan(place_ref, refs):
        source, *targets = refs
        half = source.shape[0] // 2
        row_y, row_z, count = shared_rows(place_ref, place_ref[1] * half, half)
        return [
            (source.at[pl.ds(row, count)], target)
            for row, target in zip((row_y, row_z), targets)
        ]

    shape = (weight.shape[0] // 8, weight.shape[1])
    return copied(plan, 2, place, [weight], [shape] * 2, name)


def far_moves(place_ref, parts, target, rows):
    near_y, near_z, far_y, far_z = parts
    row_y, row_z, count = shared_rows(place_ref, rows, rows)
    other_y = pl.multiple_of(rows + (1 - place_ref[2]) * count, count)
    other_z = pl.multiple_of(rows + 2 * count + (1 - place_ref[3]) * count, count)
    return [
        (part, target.at[pl.ds(row, count)])
        for part, row in ((near_y, row_y), (near_z, row_z), (far_y, other_y), (far_z, other_z))
    ]


def join_rows(place, weight, parts):
    def plan(place_ref, refs):
        source, *parts, target = refs
        rows = source.shape[0] // 2
        row = pl.multiple_of(place_ref[1] * rows, rows)
        moves = [(source.at[pl.ds(row, rows)], target.at[pl.ds(0, rows)])]
        return moves + far_moves(place_ref, parts, target, rows)

    return copied(plan, 5, place, [weight, *parts], [weight.shape], "join_rows")[0]


def swap(values, axis):
    return lax.ppermute(values, axis, [(0, 1), (1, 0)])


def rows_at(values, index, count):
    return lax.dynamic_slice_in_dim(values, index * count, count, axis=0)


def cols_at(values, index, count):
    return lax.dynamic_slice_in_dim(values, index * count, count, axis=1)


def ordered(first, mine, other, axis=0):
    return jnp.where(
        first,
        jnp.concatenate([mine, other], axis=axis),
        jnp.concatenate([other, mine], axis=axis),
    )


def hold(value, *others):
    return lax.optimization_barrier((value, *others))[0]


def mixed(parts, groups):
    pieces = []
    for group in range(groups):
        for part in parts:
            count = part.shape[1] // groups
            pieces.append(part[:, group * count : (group + 1) * count])
    return jnp.concatenate(pieces, axis=1)


def halves_swapped(values):
    mid = values.shape[1] // 2
    return jnp.concatenate([values[:, mid:], values[:, :mid]], axis=1)


def paired(
    tokens,
    positions,
    cotangent,
    norm1_gain,
    w_query,
    w_key,
    w_value,
    w_out,
    query_gain,
    key_gain,
    norm2_gain,
    w_gate,
    w_up,
    w_down,
):
    x, c, y, za = [lax.axis_index(axis) for axis in ("x", "c", "y", "za")]
    half, width = tokens.shape
    head_dim = query_gain.shape[0] * 2
    bf16, f32 = jnp.bfloat16, jnp.float32
    part, q_part = norm1_gain.shape[0], query_gain.shape[0]
    group = w_query.shape[1] // w_key.shape[1]
    head_groups = w_key.shape[1] // head_dim // 4
    unit_groups = w_gate.shape[1] // 4 // math.gcd(UNIT_BLOCK, w_gate.shape[1] // 4)

    def flip(values):
        return jnp.where(x == 0, values, halves_swapped(values))

    def turn(values):
        return jnp.where(x == c, values, lax.ppermute(values, ("c", "x"), [(1, 2), (2, 1)]))

    place = jnp.stack([x, c, y, za]).astype(jnp.int32)

    small = [norm1_gain, norm2_gain, query_gain, key_gain, positions]
    small = jnp.concatenate([item.astype(f32) for item in small])
    small_got = swap(small, "x")
    head_weights, unit_weights = [w_query, w_key, w_value], [w_gate, w_up]
    first = hold(place, small_got)

    def near(sent):
        return [swap(piece, "x") for piece in sent]

    def relayed(parts):
        return [*parts, swap(parts[0], "y"), swap(parts[1], "za")]

    head_sent = send_columns(first, head_weights, head_groups, "send_heads")
    head_near = near(head_sent)
    out_sent = send_rows(hold(place, head_sent[0]), w_out, "send_out")
    unit_sent = send_columns(hold(place, out_sent[0]), unit_weights, unit_groups, "send_units")
    down_sent = send_rows(hold(place, unit_sent[0]), w_down, "send_down")
    gains, far_gains = small[: 2 * (part + q_part)], small_got[: 2 * (part + q_part)]
    own_places, far_places = small[2 * (part + q_part) :], small_got[2 * (part + q_part) :]
    places = ordered(x == 0, own_places, far_places)
    places = jnp.where(x == c, places, swap(places, "c"))
    gain_one = jnp.concatenate([gains[:part], far_gains[:part]])[None]
    gain_two = jnp.concatenate([gains[part : 2 * part], far_gains[part : 2 * part]])[None]
    q_gain = ordered(
        x == 0, gains[2 * part : 2 * part + q_part], far_gains[2 * part : 2 * part + q_part]
    )[None]
    k_gain = ordered(x == 0, gains[2 * part + q_part :], far_gains[2 * part + q_part :])[None]
    cosine, sine = rotation_tables(places, head_dim)
    cosine = jnp.concatenate([cosine[:, 0], cosine[:, 0]], axis=-1)
    sine = jnp.concatenate([-sine[:, 0], sine[:, 0]], axis=-1)

    tokens, *head_near = lax.optimization_barrier((tokens, *head_near, down_sent[0], cosine, sine))[:3]
    own_tokens = turn(tokens)
    out_near = near([hold(piece, head_near[0]) for piece in out_sent])
    unit_near = near([hold(piece, head_near[0]) for piece in unit_sent])
    down_near = near([hold(piece, head_near[0]) for piece in down_sent])
    own_cot = turn(hold(cotangent, head_near[0]))

    head_parts = relayed(head_near)
    h_one = norm_first(place, own_tokens, swap(hold(own_tokens, *out_near, *head_parts[2:]), "c"), gain_one)
    out_parts = relayed(out_near)
    out_low, query_low, key_low, lse, qkv, qkv_w = attend(
        place,
        h_one,
        head_weights,
        head_parts,
        cosine,
        sine,
        q_gain,
        k_gain,
        group,
        head_groups,
    )
    out_low = hold(out_low, *unit_near, *down_near, *out_parts[2:])
    out_w = join_rows(place, w_out, out_parts)
    unit_parts = relayed(unit_near)
    out_sent, out_kept = out_forward(place, out_low, out_w)
    out_got = swap(out_sent, "c")
    down_parts = relayed(down_near)
    resid, h_mine = norm_second(place, own_tokens, out_kept, out_got, gain_two)
    h_mine = hold(h_mine, *unit_parts[2:], *down_parts[2:])
    h_halves = (h_mine, swap(h_mine, "c"))
    cot_halves = (own_cot, swap(own_cot, "c"))

    def rs(values, axis):
        index, count = lax.axis_index(axis), values.shape[0] // 2
        return rows_at(values, index, count), swap(rows_at(values, 1 - index, count), axis)

    far_kept, far_sent, grad_down_far, res_part, dh_part = mlp(
        place, h_halves, cot_halves, unit_weights, unit_parts, w_down, down_parts, 1
    )
    down_far_kept, down_far_got = rs(grad_down_far, "y")
    far_got = swap(far_sent, "x")
    near_kept, near_sent, grad_down_near, res_part, dh_part = mlp(
        place,
        h_halves,
        cot_halves,
        unit_weights,
        unit_parts,
        w_down,
        down_parts,
        0,
        (res_part, dh_part),
    )
    near_got = swap(near_sent, "x")
    dh_part = hold(dh_part, down_far_got)
    down_got = swap(down_far_kept + down_far_got, "x")
    down_near_kept, down_near_got = rs(grad_down_near, "y")

    class Piece:
        def __init__(self, kept, got, path):
            self.kept, self.got, self.path, self.back = kept, got, list(path), []

        def step(self, *others):
            got = hold(self.got, *others)
            if self.back and self.back[0] == "c":
                return join(place, 1, self.kept, got, f32)
            if self.back:
                values = ordered(lax.axis_index(self.back[0]) == 0, self.kept, got)
                self.back = self.back[1:]
            else:
                values = self.kept + got
            if self.path:
                axis = self.path[0]
                self.path = self.path[1:]
                if self.path:
                    self.kept, self.got = rs(values, axis)
                    self.turned = [axis] + getattr(self, "turned", [])
                else:
                    self.kept, self.got = values, swap(values, axis)
                    self.last = True
                return self.kept
            if not self.back and getattr(self, "last", False):
                self.last = False
                self.back = self.turned + ["c"]
            self.kept, self.got = values, swap(values, self.back[0])
            return self.kept

    near_piece = Piece(near_kept, far_got, ("y", "za", "zb"))

    dh_got = swap(other_half(place, dh_part), "c")
    grad_resid, resid_low, gain_two_sum = norm_gradient(
        place, resid, dh_part, dh_got, own_cot, gain_two, True
    )
    resid_low = hold(resid_low, far_got)
    grad_att, grad_out_far, grad_out_near = out_back(
        place, resid_low, swap(resid_low, "c"), out_low, out_w
    )
    out_got = swap(grad_out_far, "x")
    mark = near_piece.step(grad_att)
    far_piece = Piece(far_kept, near_got, ("za", "y", "zb"))
    out_piece = Piece(grad_out_near, out_got, ("za", "y", "zb"))

    def back_of(index, dh, *others):
        grads = hold(grad_att, *others)
        return attend_back(
            query_low,
            key_low,
            qkv,
            grads,
            lse,
            cosine,
            sine,
            q_gain,
            k_gain,
            h_one,
            qkv_w,
            index,
            dh,
        )

    far_rows, far_rows_sent, head_gains_far, dh_part = back_of(1, None, mark)
    qkv_far_got = swap(far_rows_sent, "x")
    far_rows, near_piece.got, far_piece.got, down_near_got = lax.optimization_barrier(
        (far_rows, near_piece.got, far_piece.got, down_near_got)
    )
    down_piece = Piece(down_near_kept + down_near_got, down_got, ("za", "zb"))
    down_piece.turned = ["y"]
    mark = far_piece.step(far_rows)
    mark = near_piece.step(mark)
    near_rows, near_rows_sent, head_gains_near, dh_part = back_of(0, dh_part, mark)
    qkv_near_got = swap(near_rows_sent, "x")
    dh_part, near_piece.got, far_piece.got, down_piece.got = lax.optimization_barrier(
        (dh_part, near_piece.got, far_piece.got, down_piece.got)
    )
    qkv_near_piece = Piece(near_rows, qkv_far_got, ("y", "za", "zb"))
    qkv_far_piece = Piece(far_rows, qkv_near_got, ("y", "za", "zb"))

    dh_sent = other_half(place, dh_part)
    dh_got = swap(dh_sent, "c")
    mark = near_piece.step(dh_sent)
    mark = down_piece.step(mark)
    mark = far_piece.step(mark)
    input_sum, gain_one_sum = norm_gradient(
        place, own_tokens, dh_part, hold(dh_got, mark), grad_resid, gain_one, False
    )
    head_gains = jnp.sum(head_gains_near, axis=0) + jnp.sum(head_gains_far, axis=0)
    gain_sums = [gain_one_sum[0], gain_two_sum[0]]
    head_sums = jnp.stack([head_gains[0], head_gains[1]])
    head_sums = jnp.where(x == 0, head_sums, jnp.roll(head_sums, q_part, axis=1))

    def gain_rows(at):
        pieces = [values[at * part : (at + 1) * part] for values in gain_sums]
        pieces += [values[at * q_part : (at + 1) * q_part] for values in head_sums]
        flat = jnp.concatenate(pieces)
        pad = -flat.shape[0] % (8 * head_dim)
        return jnp.concatenate([flat, jnp.zeros((pad,), f32)]).reshape(-1, head_dim)

    def rows_result(piece):
        return piece.step(mark)

    def unmixed(near, far, widths, groups):
        others = [hold(piece.got, mark) for piece in (near, far)]
        return unmix(place, near.kept, far.kept, *others, widths, groups)

    def columns_result(near, far, widths, groups):
        others = [hold(piece.got, mark) for piece in (near, far)]
        step = sum(widths)
        results, at = [], 0
        for count in widths:
            pieces = []
            for index in range(2):
                mine = jnp.where(x == index, near.kept, far.kept)
                other = jnp.where(x == index, others[0], others[1])
                for core in range(2):
                    chosen = jnp.where(c == core, mine, other)
                    for step_at in range(groups):
                        first = step_at * step + at
                        pieces.append(chosen[:, first : first + count])
            results.append(jnp.concatenate(pieces, axis=1).astype(f32))
            at += count
        return results

    gain_state = [gain_rows(0), swap(gain_rows(1), "x")]

    def gain_step(axis, *others):
        gain_state[0] = gain_state[0] + hold(gain_state[1], *others)
        if axis:
            gain_state[1] = swap(gain_state[0], axis)
        return gain_state[0]

    def result_start(*others):
        part_sum = hold(res_part, *others)
        sent = swap(other_half(place, part_sum), "c")
        total = resid + rows_at(part_sum, c, half) + sent.astype(f32)
        return total.astype(bf16)

    unit_block = w_gate.shape[1] // 4 // unit_groups
    mark = input_sum
    mark = down_piece.step(mark)
    mark = out_piece.step(mark)
    mark = far_piece.step(mark)
    mark = qkv_near_piece.step(mark)
    mark = near_piece.step(mark)
    mark = gain_step("y", mark)
    mark = qkv_near_piece.step(mark)
    mark = out_piece.step(mark)
    input_turned = turn(hold(input_sum, mark))
    mark = qkv_far_piece.step(mark)
    mark = qkv_near_piece.step(mark)
    mark = down_piece.step(mark)
    mark = out_piece.step(mark)
    mark = near_piece.step(mark)
    mark = qkv_far_piece.step(mark)
    mark = far_piece.step(mark)
    mark = gain_step("za", mark)
    mark = qkv_far_piece.step(mark)
    mark = qkv_near_piece.step(mark)
    mark = down_piece.step(mark)
    mark = grad_input = hold(input_turned, mark).astype(f32)
    mark = out_piece.step(mark)
    mark = far_piece.step(mark)
    mark = gain_step("zb", mark)
    mark = near_piece.step(mark)
    mark = qkv_far_piece.step(mark)
    mark = qkv_near_piece.step(mark)
    result_turned = turn(result_start(mark))
    mark = far_piece.step(mark)
    mark = down_piece.step(mark)
    grad_gate_w, grad_up_w = lax.optimization_barrier(
        unmixed(near_piece, far_piece, [unit_block, unit_block], unit_groups)
    )
    mark = grad_up_w
    mark = out_piece.step(mark)
    mark = grad_down_w = rows_result(down_piece)
    mark = qkv_far_piece.step(mark)
    mark = qkv_near_piece.step(mark)
    mark = gain_step("c", mark)
    mark = out_piece.step(mark)
    mark = result = hold(result_turned, mark)
    mark = qkv_far_piece.step(mark)
    mark = grad_out_w = rows_result(out_piece)
    mark = gain_step(None, mark)
    grad_query_w, grad_key_w, grad_value_w = columns_result(
        qkv_near_piece, qkv_far_piece, [group * head_dim, head_dim, head_dim], head_groups
    )
    total_gains = gain_state[0].reshape(-1)

    return (
        result,
        grad_input,
        total_gains[:part],
        grad_query_w,
        grad_key_w,
        grad_value_w,
        grad_out_w,
        total_gains[2 * part : 2 * part + q_part],
        total_gains[2 * part + q_part : 2 * (part + q_part)],
        total_gains[part : 2 * part],
        grad_gate_w,
        grad_up_w,
        grad_down_w,
    )


def solution(mesh):
    if mesh.shape["shard"] == 2 and mesh.shape["replica"] == 16:
        names = ("zb", "za", "y", "c", "x")
        grid = Mesh(mesh.devices.reshape((2,) * len(names)), names)
        body, over, owned = paired, names, "x"
    else:
        grid, body, over, owned = mesh, local, ("replica", "shard"), "shard"
    rows, vector, matrix = P(over, None), P(owned), P(owned, None)
    return jax.shard_map(
        body,
        mesh=grid,
        in_specs=(
            rows,
            P(over),
            rows,
            vector,
            matrix,
            matrix,
            matrix,
            matrix,
            vector,
            vector,
            vector,
            matrix,
            matrix,
            matrix,
        ),
        out_specs=(
            rows,
            rows,
            vector,
            matrix,
            matrix,
            matrix,
            matrix,
            vector,
            vector,
            vector,
            matrix,
            matrix,
            matrix,
        ),
        check_vma=False,
    )
```
